32 devices in a mesh: lon: 4 (over z), lat: 2 (over y), ch: 4 (over x, core).
Axes of the slice: x: 2, y: 2, z: 4, core: 2. Of those that a mesh axis runs over, the one named last changes fastest.
Arguments:
- ocean_state: bfloat16 [300, 64, 512], P('ch', 'lat', 'lon'), may hold values from -6 to 6
- land_mask: int32 [64, 512], P('lat', 'lon'), may hold values 0 or 1
- out_grad: bfloat16 [300, 64, 512], P('ch', 'lat', 'lon'), may hold values from -6 to 6
- swath_offset: int32 [2, 4, 512], P('lat', 'lon'), may hold values from 0 to 4095
- swath_value: float32 [2, 4, 512], P('lat', 'lon'), may hold values from -8 to 8
- depth_kernel: float32 [3, 3, 300], P(None, None, 'ch'), may hold values from -2.5 to 2.5
- expand_weight: bfloat16 [300, 600], P(None, 'ch'), may hold values from -0.375 to 0.375
- expand_bias: float32 [600], P('ch'), may hold values from -3 to 3
- project_weight: bfloat16 [600, 300], P('ch'), may hold values from -0.25 to 0.25
Outputs:
- state_grad: bfloat16 [300, 64, 512], P('ch', 'lat', 'lon')
- expand_grad: float32 [300, 600], P(None, 'ch')
- project_grad: float32 [600, 300], P('ch')
- bias_grad: float32 [600], P('ch')
- kernel_grad: float32 [3, 3, 300], P(None, None, 'ch')
The draws below stay inside these ranges and needn't reach their ends.
Inputs may be any that keep to these rules, and one draw needn't show every extreme that they name: `swath_offset`: position of a swath point in row-major order over the 32 x 128 cells of its device's block.
All inputs are finite; a program needn't handle non-finite values. No bound on the sum of `land_mask` on one device may be relied on, other than what follows from the above.
Results may differ from the reference program's by a relative error of at most 0.014.
Values may be sent and summed in bfloat16 or wider, within the bound.
No kernel may reach another device: no remote copies, remote signals or barrier semaphores. Data moves between devices by JAX's collectives and lax.ppermute only.
A program may use at most 64 MiB of HBM per device.

```python
import jax
import jax.numpy as jnp
from jax import lax

C = 300
HID = 600
DILATION_STEP = 2
ROWS = 32
COLS = 128
SWATH = 512
GRID_ROWS = 64
GRID_COLUMNS = 512
N_LON = 4
N_LAT = 2
N_CH = 4


def plant(drawn, key, smallest, high):
    longest = drawn.shape.index(max(drawn.shape))
    spots = []
    for shift in (0, 1):
        where = [jax.random.randint(jax.random.fold_in(key, axis), (), 0, length) for axis, length in enumerate(drawn.shape)]
        where[longest] = (where[longest] + shift) % drawn.shape[longest]
        spots.append(tuple(where))
    return drawn.at[spots[0]].set(smallest).at[spots[1]].set(high)


def block_levels(rng, extent, split, least, top_value):
    def one(dim, shards_of):
        draws = jax.random.uniform(jax.random.fold_in(jax.random.fold_in(rng, 6), dim), (shards_of,), jnp.float32, least / len(split), top_value / len(split))
        return jnp.repeat(jnp.exp(draws), extent[dim] // shards_of).reshape((-1,) + (1,) * (len(extent) - dim - 1))

    factor_of = one(*split[0])
    for cut in split[1:]:
        factor_of = factor_of * one(*cut)
    return factor_of


def normal_values(own_key, dims, width, most, shards=(), kind=jnp.bfloat16):
    array = jax.random.normal(own_key, dims, jnp.float32) * width
    if len(shards) > 0:
        array = block_levels(own_key, dims, shards, -0.22, 0.18) * array
    return jnp.clip(array, min=-most, max=most).astype(kind)


def setup_inputs(seed: int = 0) -> dict:
    key_list = jax.random.split(jax.random.key(seed), 10)
    return {
        "ocean_state": normal_values(key_list[0], (C, GRID_ROWS, GRID_COLUMNS), 1.0, 6.0, ((0, 4), (1, 2), (2, 4))),
        "land_mask": plant((jax.random.randint(key_list[1], (GRID_ROWS, GRID_COLUMNS), 0, 4) < 3).astype(jnp.int32), jax.random.fold_in(key_list[1], 1), 0, 1),
        "out_grad": normal_values(key_list[2], (C, GRID_ROWS, GRID_COLUMNS), 1.0, 6.0, ((0, 4), (1, 2), (2, 4))),
        "swath_offset": plant(jax.random.randint(key_list[3], (N_LAT, N_LON, SWATH), 0, ROWS * COLS), jax.random.fold_in(key_list[3], 1), 0, (ROWS * COLS) - 1).astype(jnp.int32),
        "swath_value": normal_values(key_list[4], (N_LAT, N_LON, SWATH), 2.0, 8.0, ((0, 2), (1, 4)), jnp.float32),
        "depth_kernel": normal_values(key_list[5], (3, 3, C), 0.4, 2.5, ((2, 4),), jnp.float32),
        "expand_weight": normal_values(key_list[6], (C, HID), C ** -0.5, 0.375, ((1, 4),)),
        "expand_bias": normal_values(key_list[7], (HID,), 0.5, 3.0, ((0, 4),), jnp.float32),
        "project_weight": normal_values(key_list[8], (HID, C), HID ** -0.5, 0.25, ((0, 4),)),
    }


def pad_grid(ocean_field):
    longitude_wrapped = jnp.concatenate([ocean_field[:, -DILATION_STEP:], ocean_field, ocean_field[:, :DILATION_STEP]], axis=1)
    seam_folded = ocean_field[GRID_ROWS - DILATION_STEP:, :][::-1, ::-1]
    seam_folded = jnp.concatenate([seam_folded[:, -DILATION_STEP:], seam_folded, seam_folded[:, :DILATION_STEP]], axis=1)
    southern_rows = jnp.zeros((DILATION_STEP, GRID_COLUMNS + 2 * DILATION_STEP), ocean_field.dtype)
    return jnp.concatenate([southern_rows, longitude_wrapped, seam_folded], axis=0)

def conv_plane(ocean_field, taps):
    halo_padded = pad_grid(ocean_field)
    total = jnp.zeros((GRID_ROWS, GRID_COLUMNS), ocean_field.dtype)
    for row_offset in range(3):
        for column_offset in range(3):
            kernel_window = halo_padded[DILATION_STEP * row_offset:DILATION_STEP * row_offset + GRID_ROWS, DILATION_STEP * column_offset:DILATION_STEP * column_offset + GRID_COLUMNS]
            total = total + taps[row_offset, column_offset] * kernel_window
    return total

def reference(ocean_state, land_mask, out_grad, swath_offset, swath_value, depth_kernel, expand_weight, expand_bias, project_weight):
    mask_float = land_mask.astype(jnp.float32)
    masked = ocean_state * land_mask.astype(jnp.bfloat16)[None]
    kernels = jnp.moveaxis(depth_kernel, 2, 0)

    def forward_plane(pair):
        return conv_plane(pair[0].astype(jnp.float32), pair[1]).astype(jnp.bfloat16)
    conv_out = lax.map(forward_plane, (masked, kernels))
    lat_ids = lax.broadcasted_iota(jnp.int32, swath_offset.shape, 0)
    lon_ids = lax.broadcasted_iota(jnp.int32, swath_offset.shape, 1)
    row_ids = (lat_ids * ROWS + swath_offset // COLS).reshape(-1)
    col_ids = (lon_ids * COLS + swath_offset % COLS).reshape(-1)
    swath = jnp.zeros((GRID_ROWS, GRID_COLUMNS), jnp.float32).at[row_ids, col_ids].add(swath_value.reshape(-1))
    cotan = out_grad.astype(jnp.float32).at[0].add(swath)
    cotan = (cotan * mask_float[None]).astype(jnp.bfloat16)
    block_count = GRID_ROWS // 2
    block_cells = 2 * GRID_COLUMNS
    conv_blocks = jnp.moveaxis(conv_out.reshape(C, block_count, block_cells), 1, 0)
    cotan_blocks = jnp.moveaxis(cotan.reshape(C, block_count, block_cells), 1, 0)
    group = HID // N_CH

    def step(carry, pair):
        conv_block, cotan_block = pair
        hidden = jnp.dot(expand_weight.T, conv_block, preferred_element_type=jnp.float32) + expand_bias[:, None]
        activ, gelu_back = jax.vjp(jax.nn.gelu, hidden)
        act_grad = jnp.dot(project_weight, cotan_block, preferred_element_type=jnp.float32)
        pre_grad = gelu_back(act_grad)[0].astype(jnp.bfloat16)
        expand_sum = carry[0] + jnp.dot(conv_block, pre_grad.T, preferred_element_type=jnp.float32)
        project_sum = carry[1] + jnp.dot(activ.astype(jnp.bfloat16), cotan_block.T, preferred_element_type=jnp.float32)
        bias_sum = carry[2] + lax.optimization_barrier(jnp.sum(pre_grad.astype(jnp.float32), axis=1))
        conv_grad = jnp.zeros((C, block_cells), jnp.float32)
        for group_index in range(N_CH):
            lower = group_index * group
            part = jnp.dot(expand_weight[:, lower:lower + group], pre_grad[lower:lower + group], preferred_element_type=jnp.float32)
            conv_grad = conv_grad + lax.optimization_barrier(part.astype(jnp.bfloat16)).astype(jnp.float32)
        return ((expand_sum, project_sum, bias_sum), conv_grad.astype(jnp.bfloat16))
    start = (jnp.zeros((C, HID), jnp.float32), jnp.zeros((HID, C), jnp.float32), jnp.zeros((HID,), jnp.float32))
    sums, grad_blocks = lax.scan(step, start, (conv_blocks, cotan_blocks))
    conv_grad = jnp.moveaxis(grad_blocks, 0, 1).reshape(C, GRID_ROWS, GRID_COLUMNS)

    def adjoint(triple):
        ocean_field, taps, grad = triple
        unused, back = jax.vjp(conv_plane, ocean_field, taps)
        return back(grad)
    state_back, kernel_back = lax.map(adjoint, (masked.astype(jnp.float32), kernels, conv_grad.astype(jnp.float32)))
    state_grad = (mask_float[None] * (cotan.astype(jnp.float32) + state_back)).astype(jnp.bfloat16)
    scale = float(GRID_ROWS * GRID_COLUMNS) ** (-0.5)
    return (state_grad, sums[0] * scale, sums[1] * scale, sums[2] * scale, jnp.moveaxis(kernel_back, 0, 2) * scale)
```

```python
import functools
import math

import jax
import jax.numpy as jnp
from jax import lax
from jax.experimental import pallas as pl
from jax.experimental.pallas import tpu as pltpu
from jax.sharding import PartitionSpec as P

DIL = 2
LANES = 128
BF = jnp.bfloat16
F32 = jnp.float32


def shape(dims, kind):
    return jax.ShapeDtypeStruct(dims, kind)


def call(kernel, outs, args, scratch=(), name=None, flops=0, moved=None):
    if moved is None:
        moved = sum(math.prod(a.shape) * a.dtype.itemsize for a in list(args) + list(outs))
    return pl.pallas_call(
        kernel,
        out_shape=tuple(outs),
        in_specs=[pl.BlockSpec(memory_space=pltpu.VMEM) for _ in args],
        out_specs=tuple(pl.BlockSpec(memory_space=pltpu.VMEM) for _ in outs),
        scratch_shapes=list(scratch),
        name=name,
        compiler_params=pltpu.CompilerParams(vmem_limit_bytes=48 * 1024 * 1024),
        cost_estimate=pl.CostEstimate(flops=flops, bytes_accessed=moved, transcendentals=0),
    )(*args)


def iota(dims, dim):
    return lax.broadcasted_iota(jnp.int32, dims, dim)


def aligned(index):
    return pl.multiple_of(index, 16)


def to_rows(block_ref, weight, scr, pad):
    channels, rows, cols = block_ref.shape

    def body(c, carry):
        value = block_ref[c].astype(F32)
        if weight is not None:
            value = value * weight
        scr[pl.ds(c, rows, stride=pad), :] = value
        return carry

    lax.fori_loop(0, channels, body, 0, unroll=5 if channels % 5 == 0 else 1)
    for c in range(channels, pad):
        scr[pl.ds(c, rows, stride=pad), :] = jnp.zeros((rows, cols), F32)


def pack_columns(value, ext_row, left, right):
    lane = iota(value.shape, 1)
    here = (lane == 2 * ext_row) | (lane == 2 * ext_row + 1)
    size = value.shape[1]
    left = jnp.where(here, pltpu.roll(value, (2 * ext_row) % size, 1), left)
    right = jnp.where(here, pltpu.roll(value, (2 * ext_row + 2) % size, 1), right)
    return left, right


def mirrored(value):
    size = value.shape[1]
    flip = (iota((size, size), 0) + iota((size, size), 1) == size - 1).astype(BF)
    return jnp.dot(value, flip, preferred_element_type=F32).astype(BF)


def emit_strips(read, rows, pad, swap, strips):
    if swap:
        strip_ref, fold_ref, left_ref, right_ref = strips
        at_bottom = lax.axis_index("lat") == 0
        for t in range(DIL):
            low, high = read(t), read(rows - DIL + t)
            strip_ref[t] = jnp.where(at_bottom, high.astype(F32), low.astype(F32)).astype(BF)
    else:
        down_ref, up_ref, fold_ref, left_ref, right_ref = strips
        for t in range(DIL):
            down_ref[t] = read(t)
            up_ref[t] = read(rows - DIL + t)
    for t in range(DIL):
        fold_ref[t] = mirrored(read(rows - 1 - t))
    left = jnp.zeros((pad, LANES), F32)
    right = jnp.zeros((pad, LANES), F32)
    for r in range(rows):
        left, right = pack_columns(read(r).astype(F32), r + DIL, left, right)
    left_ref[...] = left.astype(BF)
    right_ref[...] = right.astype(BF)


def strip_shapes(pad, swap):
    one = shape((DIL, pad, LANES), BF)
    packs = [shape((pad, LANES), BF)] * 2
    return ([one] if swap else [one, one]) + [one] + packs


def prepare_state(swap, state_ref, mask_ref, rows_ref, *rest):
    strips, scr = rest[:-1], rest[-1]
    rows, pad = rows_ref.shape[:2]
    to_rows(state_ref, mask_ref[...].astype(F32), scr, pad)
    for r in range(rows):
        rows_ref[r] = scr[r * pad : (r + 1) * pad, :].astype(BF)
    emit_strips(lambda r: rows_ref[r], rows, pad, swap, strips)


def prepare_cotan(grad_ref, mask_ref, offset_ref, value_ref, rows_ref, *rest):
    quarters, scr = rest[:-1], rest[-1]
    rows, pad, cols = rows_ref.shape
    me = lax.axis_index("ch")
    mask = mask_ref[...].astype(F32)
    to_rows(grad_ref, None, scr, pad)
    offset = offset_ref[...]
    points = offset.shape[1]
    value = value_ref[...]
    total = jnp.zeros((rows, cols), F32)
    row_hot = iota((rows, points), 0) == offset // cols
    col_hot = (iota((cols, points), 0) == offset % cols).astype(BF)
    for _ in range(3):
        part = value.astype(BF)
        value = value - part.astype(F32)
        lhs = jnp.where(row_hot, part.astype(F32), 0.0).astype(BF)
        total = total + lax.dot_general(
            lhs, col_hot, (((1,), (1,)), ((), ())), preferred_element_type=F32
        )
    total = jnp.where(me == 0, total, 0.0)
    first = scr[pl.ds(0, rows, stride=pad), :]
    scr[pl.ds(0, rows, stride=pad), :] = first + total
    for r in range(rows):
        rows_ref[r] = (scr[r * pad : (r + 1) * pad, :] * mask[r : r + 1, :]).astype(BF)
    part_rows = quarters[0].shape[0]
    for k, quarter in enumerate(quarters):
        quarter[...] = rows_ref[pl.ds((me ^ k) * part_rows, part_rows)]


def ring(count, step):
    return [(i, (i + step) % count) for i in range(count)]


def exchange_halo(strips, rows, pad, swap, name):
    n_lat, n_lon = lax.axis_size("lat"), lax.axis_size("lon")
    top = n_lat - 1
    fold_pairs = [
        (lon * n_lat + top, (n_lon - 1 - lon) * n_lat + top) for lon in range(n_lon)
    ]
    if swap:
        strip, fold, left, right = strips
        moved = [lax.ppermute(strip, "lat", [(0, 1), (1, 0)])]
    else:
        down, up, fold, left, right = strips
        moved = [
            lax.ppermute(up, "lat", [(i, i + 1) for i in range(n_lat - 1)]),
            lax.ppermute(down, "lat", [(i + 1, i) for i in range(n_lat - 1)]),
        ]
    fold = lax.ppermute(fold, ("lon", "lat"), fold_pairs)
    kernel = functools.partial(finish_columns, rows, swap)
    halo, left, right = call(
        kernel,
        [shape((2 * DIL, pad, LANES), BF)] + [shape((pad, LANES), BF)] * 2,
        [*moved, fold, left, right],
        name=name,
    )
    from_right = lax.ppermute(left, "lon", ring(n_lon, -1))
    from_left = lax.ppermute(right, "lon", ring(n_lon, 1))
    return halo, from_left, from_right


def finish_columns(rows, swap, *refs):
    if swap:
        strip_ref, fold_ref, left_ref, right_ref, halo_ref, left_out, right_out = refs
        low_ref = high_ref = strip_ref
    else:
        low_ref, high_ref, fold_ref, left_ref, right_ref, halo_ref, left_out, right_out = refs
    lat, count = lax.axis_index("lat"), lax.axis_size("lat")
    left, right = left_ref[...].astype(F32), right_ref[...].astype(F32)
    for t in range(DIL):
        south = jnp.where(lat == 0, 0.0, low_ref[t].astype(F32))
        north = jnp.where(lat == count - 1, fold_ref[t].astype(F32), high_ref[t].astype(F32))
        halo_ref[t] = south.astype(BF)
        halo_ref[DIL + t] = north.astype(BF)
        left, right = pack_columns(south, t, left, right)
        left, right = pack_columns(north, rows + DIL + t, left, right)
    left_out[...] = left.astype(BF)
    right_out[...] = right.astype(BF)


def shifted_rows(block_ref, halo_ref, left_ref, right_ref, group):
    rows = block_ref.shape[0]
    at = pl.ds(aligned(group * 16), 16)
    lane = iota((16, LANES), 1)
    left, right = left_ref[at, :].astype(F32), right_ref[at, :].astype(F32)
    for e in range(rows + 2 * DIL):
        if e < DIL:
            row = halo_ref[e, at, :]
        elif e < rows + DIL:
            row = block_ref[e - DIL, at, :]
        else:
            row = halo_ref[e - rows, at, :]
        row = row.astype(F32)
        west = jnp.where(
            lane < DIL, pltpu.roll(left, (-2 * e) % LANES, 1), pltpu.roll(row, DIL, 1)
        )
        east = jnp.where(
            lane >= LANES - DIL,
            pltpu.roll(right, (LANES - DIL - 2 * e) % LANES, 1),
            pltpu.roll(row, LANES - DIL, 1),
        )
        yield e, (west, row, east)


def stencil(block_ref, halo_ref, left_ref, right_ref, group, taps, north, emit):
    rows = block_ref.shape[0]
    sums = {}
    for e, shifts in shifted_rows(block_ref, halo_ref, left_ref, right_ref, group):
        for a in (2, 1, 0):
            r = e - DIL * a
            if not 0 <= r < rows:
                continue
            used = north if e >= rows + DIL else taps[a]
            term = used[0] * shifts[0] + used[1] * shifts[1] + used[2] * shifts[2]
            sums[r] = term if r not in sums else sums[r] + term
            if a == 2:
                emit(r, sums.pop(r))


def spread(tap_ref, group):
    values = tap_ref[pl.ds(aligned(group * 16), 16), :]
    return [
        [jnp.broadcast_to(values[:, 3 * a + b : 3 * a + b + 1], (16, LANES)) for b in range(3)]
        for a in range(3)
    ]


def conv_forward(ones_row, block_ref, halo_ref, left_ref, right_ref, tap_ref, *rest):
    quarters, scr = rest[:-1], rest[-1]
    pad = block_ref.shape[1]
    me = lax.axis_index("ch")

    def body(group, carry):
        taps = spread(tap_ref, group)
        is_one = iota((16, LANES), 0) + group * 16 == ones_row

        def emit(r, value):
            value = jnp.where(is_one, 1.0, value)
            scr[r, pl.ds(aligned(group * 16), 16), :] = value.astype(BF)

        stencil(block_ref, halo_ref, left_ref, right_ref, group, taps, taps[2], emit)
        return carry

    lax.fori_loop(0, pad // 16, body, 0)
    part_rows = quarters[0].shape[0]
    for k, quarter in enumerate(quarters):
        quarter[...] = scr[pl.ds((me ^ k) * part_rows, part_rows)]


def conv_adjoint(
    block_ref, halo_ref, left_ref, right_ref, tap_ref, cotan_ref, mask_ref, out_ref, scr
):
    rows, pad = block_ref.shape[:2]
    at_top = lax.axis_index("lat") == lax.axis_size("lat") - 1
    mask = mask_ref[...].astype(F32)

    def body(group, carry):
        taps = spread(tap_ref, group)
        back = [[taps[2 - a][2 - b] for b in range(3)] for a in range(3)]
        north = [jnp.where(at_top, taps[2][b], back[2][b]) for b in range(3)]

        def emit(r, value):
            cotan = cotan_ref[r, pl.ds(aligned(group * 16), 16), :].astype(F32)
            scr[pl.ds(pl.multiple_of(r * pad + group * 16, 16), 16), :] = (cotan + value) * mask[
                r : r + 1, :
            ]

        stencil(block_ref, halo_ref, left_ref, right_ref, group, back, north, emit)
        return carry

    lax.fori_loop(0, pad // 16, body, 0)

    def write(c, carry):
        out_ref[c] = scr[pl.ds(c, rows, stride=pad), :].astype(BF)
        return carry

    channels = out_ref.shape[0]
    lax.fori_loop(0, channels, write, 0, unroll=5 if channels % 5 == 0 else 1)


def collect_grad(swap, q0, q1, q2, q3, rows_ref, *strips):
    part_rows = q0.shape[0]
    rows, pad = rows_ref.shape[:2]
    me = lax.axis_index("ch")
    for k, quarter in enumerate((q0, q1, q2, q3)):
        rows_ref[pl.ds((me ^ k) * part_rows, part_rows)] = quarter[...]
    emit_strips(lambda r: rows_ref[r], rows, pad, swap, strips)


def kernel_gradient(grad_ref, block_ref, halo_ref, left_ref, right_ref, out_ref):
    rows, pad = grad_ref.shape[:2]

    def body(group, carry):
        at = pl.ds(aligned(group * 16), 16)
        sums = [[jnp.zeros((16, LANES), F32) for _ in range(3)] for _ in range(3)]
        for e, shifts in shifted_rows(block_ref, halo_ref, left_ref, right_ref, group):
            for a in range(3):
                r = e - DIL * a
                if 0 <= r < rows:
                    grad = grad_ref[r, at, :].astype(F32)
                    for b in range(3):
                        sums[a][b] = sums[a][b] + grad * shifts[b]
        lane = iota((16, LANES), 1)
        out = jnp.zeros((16, LANES), F32)
        for a in range(3):
            for b in range(3):
                total = jnp.sum(sums[a][b], axis=1, keepdims=True)
                out = jnp.where(lane == 3 * a + b, total, out)
        out_ref[at, :] = out
        return carry

    lax.fori_loop(0, pad // 16, body, 0)


def channel_of(slot, part, pad):
    block = sum((slot >= pad * b).astype(jnp.int32) for b in range(1, 4))
    inside = slot - block * pad
    return jnp.where((slot >= 0) & (slot < 4 * pad) & (inside < part), block * part + inside, -1)


def expand_slot(lane, pad):
    return jnp.where(lane < 4 * pad, lane, -1)


def project_slot(lane, pad, split):
    tail = 4 * pad - split
    low = LANES - tail
    return jnp.where(lane >= LANES, lane - LANES, jnp.where(lane >= low, lane - low + split, -1))


def pack_weights(part, pad, expand_ref, bias_ref, project_ref, out_ref):
    channels, hidden = expand_ref.shape
    wide = out_ref.shape[1]
    split = 4 * pad // LANES * LANES
    lane = iota((channels, wide), 1)
    row = iota((channels, wide), 0)
    pick_e = (channel_of(expand_slot(lane, pad), part, pad) == row).astype(BF)
    slot = jnp.where(lane >= split, project_slot(lane - split, pad, split), -1)
    pick_p = (channel_of(slot, part, pad) == row).astype(BF)
    bias = bias_ref[...]
    parts = jnp.zeros((16, hidden), F32)
    at = iota((16, hidden), 0)
    for k in range(3):
        piece = bias.astype(BF).astype(F32)
        bias = bias - piece
        parts = jnp.where(at == k, piece, parts)
    lane, row = iota((16, wide), 1), iota((16, wide), 0)
    pick_b = ((lane == row * pad + part) & (row < 3)).astype(BF)
    turned = (((0,), (0,)), ((), ()))
    packed = (
        lax.dot_general(expand_ref[...], pick_e, turned, preferred_element_type=F32)
        + lax.dot_general(parts.astype(BF), pick_b, turned, preferred_element_type=F32)
        + jnp.dot(project_ref[...], pick_p, preferred_element_type=F32)
    )
    rows = out_ref.shape[0]
    out_ref[0:hidden, :] = packed.astype(BF)
    out_ref[hidden:rows, :] = jnp.zeros((rows - hidden, wide), BF)


GELU_C = math.sqrt(2.0 / math.pi)


def mlp(*refs):
    xs, ys, ws = refs[0:4], refs[4:8], refs[8:12]
    grads, keep_ref, send_ref = refs[12:16], refs[16], refs[17]
    x_scr, y_scr, w_scr, t_scr, act_scr, pre_scr, cg_scr = refs[18:]
    part_rows, pad = xs[0].shape[:2]
    hid = ws[0].shape[0]
    split = 4 * pad // LANES * LANES
    depth = x_scr.shape[0]
    cells = x_scr.shape[1]
    me = lax.axis_index("ch")
    x_scr[4 * pad : depth, :] = jnp.zeros((depth - 4 * pad, cells), BF)
    y_scr[0 : depth - 4 * pad, :] = jnp.zeros((depth - 4 * pad, cells), BF)
    for k in range(4):
        block = me ^ k
        w_scr[k * hid : (k + 1) * hid, :] = ws[k][...]
        for r in range(part_rows):
            cols = slice(r * LANES, (r + 1) * LANES)
            x_scr[pl.ds(aligned(block * pad), pad), cols] = xs[k][r]
            for u in range(pad // 16):
                slot = block * pad + 16 * u
                to = jnp.where(slot < split, slot + LANES, slot - split + depth - 4 * pad)
                y_scr[pl.ds(aligned(to), 16), cols] = ys[k][r, 16 * u : 16 * (u + 1), :]
    t_scr[...] = jnp.transpose(w_scr[:, 0:depth])
    step = 256
    for start in range(0, cells, step):
        cols = slice(start, start + step)
        hidden = jnp.dot(w_scr[:, 0:depth], x_scr[:, cols], preferred_element_type=F32)
        act_grad = jnp.dot(w_scr[:, split : split + depth], y_scr[:, cols], preferred_element_type=F32)
        square = hidden * hidden
        tanh = jnp.tanh(GELU_C * hidden * (1.0 + 0.044715 * square))
        half = 0.5 * (1.0 + tanh)
        slope = half + (0.5 * GELU_C) * hidden * (1.0 - tanh * tanh) * (
            1.0 + (3 * 0.044715) * square
        )
        act_scr[:, cols] = (hidden * half).astype(BF)
        pre = (act_grad * slope).astype(BF)
        pre_scr[:, cols] = pre
        cg_scr[:, cols] = jnp.dot(t_scr[...], pre, preferred_element_type=F32).astype(BF)
    for k in range(4):
        for r in range(part_rows):
            grads[k][r] = cg_scr[
                pl.ds(aligned((me ^ k) * pad), pad), r * LANES : (r + 1) * LANES
            ]
    over_cells = (((1,), (1,)), ((), ()))
    expand = lax.dot_general(pre_scr[...], x_scr[...], over_cells, preferred_element_type=F32)
    project = lax.dot_general(act_scr[...], y_scr[...], over_cells, preferred_element_type=F32)
    shared = split // LANES
    tiles = [expand[:, t * LANES : (t + 1) * LANES] for t in range(shared)]
    tiles.append(expand[:, split : split + LANES] + project[:, 0:LANES])
    tiles += [project[:, t * LANES : (t + 1) * LANES] for t in range(1, shared + 1)]
    for k in range(4):
        to = send_ref if k % 2 else keep_ref
        for t, tile in enumerate(tiles):
            to[k // 2, t * hid : (t + 1) * hid, :] = tile[k * hid : (k + 1) * hid].astype(to.dtype)


def add_cores(keep_ref, got_ref, own_ref, y_ref, x_ref, xy_ref):
    half = own_ref.shape[0]
    lat = lax.axis_index("lat")
    here, there = pl.ds(aligned(lat * half), half), pl.ds(aligned((1 - lat) * half), half)

    def total(group, at):
        return keep_ref[group, at, :] + got_ref[group, at, :].astype(F32)

    own_ref[...] = total(0, here)
    y_ref[...] = total(0, there).astype(BF)
    x_ref[...] = total(1, here).astype(BF)
    xy_ref[...] = total(1, there).astype(BF)


def add_planes(own_ref, a_ref, b_ref, c_ref, keep_ref, *rest):
    sends, scr = rest[:-1], rest[-1]
    scr[...] = own_ref[...] + (
        a_ref[...].astype(F32) + b_ref[...].astype(F32) + c_ref[...].astype(F32)
    )
    piece = keep_ref.shape[0]
    step = piece - 16
    lon = lax.axis_index("lon")
    keep_ref[...] = scr[pl.ds(aligned(lon * step), piece), :]
    for k, send in enumerate(sends):
        send[...] = scr[pl.ds(aligned((lon ^ (k + 1)) * step), piece), :].astype(BF)


def add_lines(own_ref, a_ref, b_ref, c_ref, kernel_ref, out_ref):
    piece = own_ref.shape[0]
    out_ref[0:piece, :] = (
        own_ref[...] + (a_ref[...].astype(F32) + b_ref[...].astype(F32) + c_ref[...].astype(F32))
    ).astype(BF)
    out_ref[piece : out_ref.shape[0], :] = kernel_ref[...].astype(BF)


def join_lines(piece, p0, p1, p2, p3, out_ref, scr):
    step = piece - 16
    half = 4 * step + 16
    extra = out_ref.shape[0] - half
    lon = lax.axis_index("lon")
    for k, ref in enumerate((p0, p1, p2, p3)):
        place = lon ^ k
        out_ref[pl.ds(aligned(place * step), step), :] = ref[0:step, :]

        @pl.when(place == 3)
        def _():
            out_ref[4 * step : half, :] = ref[step:piece, :]

        scr[pl.ds(aligned(place * extra), extra), :] = ref[piece : piece + extra, :].astype(F32)
    total = scr[0:extra, :]
    for k in range(1, 4):
        total = total + scr[k * extra : (k + 1) * extra, :]
    out_ref[half : half + extra, :] = total.astype(BF)


def write_parameters(part, pad, scale, hid, own_ref, got_ref, *rest):
    expand_ref, project_ref, bias_ref, taps_ref, all_scr, turn_scr = rest
    half = all_scr.shape[0] // 2
    extra = own_ref.shape[0] - half
    lat = lax.axis_index("lat")
    all_scr[pl.ds(aligned(lat * half), half), :] = own_ref[0:half, :]
    all_scr[pl.ds(aligned((1 - lat) * half), half), :] = got_ref[0:half, :]
    unpack(part, pad, scale, hid, all_scr, expand_ref, project_ref, bias_ref)
    total = own_ref[half : half + extra, :].astype(F32) + got_ref[half : half + extra, :].astype(F32)
    write_taps(total, scale, taps_ref, turn_scr)


def write_taps(total, scale, taps_ref, turn_scr):
    turn_scr[...] = jnp.zeros(turn_scr.shape, F32)
    turn_scr[0 : total.shape[0], :] = total * scale
    taps_ref[...] = jnp.transpose(turn_scr[...])[0 : taps_ref.shape[0], 0 : taps_ref.shape[1]]


def unpack(part, pad, scale, hid, all_ref, expand_ref, project_ref, bias_ref):
    channels, hidden = expand_ref.shape
    split = 4 * pad // LANES * LANES
    shared = split // LANES
    tiles = [all_ref[t * hid : (t + 1) * hid, :] for t in range(2 * shared + 1)]
    depth = (shared + 1) * LANES
    expand = jnp.concatenate(tiles[: shared + 1], axis=1)
    project = jnp.concatenate(tiles[shared:], axis=1)
    lane, row = iota((channels, depth), 1), iota((channels, depth), 0)
    pick_e = (channel_of(expand_slot(lane, pad), part, pad) == row).astype(BF)
    pick_p = (channel_of(project_slot(lane, pad, split), part, pad) == row).astype(BF)
    pick_b = (iota((16, depth), 1) == part).astype(BF)
    last = (((1,), (1,)), ((), ()))
    dot = functools.partial(lax.dot_general, dimension_numbers=last, preferred_element_type=F32)
    expand_ref[...] = dot(pick_e, expand)[:, 0:hidden] * scale
    bias_ref[...] = dot(pick_b, expand)[0:1, 0:hidden] * scale
    project_ref[...] = dot(project, pick_p)[0:hidden, :] * scale


def unpack_whole(part, pad, scale, hid, all_ref, taps_in, expand_ref, project_ref, bias_ref, taps_ref, turn_scr):
    unpack(part, pad, scale, hid, all_ref, expand_ref, project_ref, bias_ref)
    write_taps(taps_in[...], scale, taps_ref, turn_scr)


def on_device(
    ocean_state,
    land_mask,
    out_grad,
    swath_offset,
    swath_value,
    depth_kernel,
    expand_weight,
    expand_bias,
    project_weight,
):
    part, rows, cols = ocean_state.shape
    n_lon, n_lat, n_ch = lax.axis_size("lon"), lax.axis_size("lat"), lax.axis_size("ch")
    channels, hidden = expand_weight.shape
    assert n_ch == 4 and cols == LANES and rows % n_ch == 0
    pad = (part + 16) // 16 * 16
    hid = (hidden + 15) // 16 * 16
    split = n_ch * pad // LANES * LANES
    tail = n_ch * pad - split
    assert tail == LANES // 2
    wide = 2 * n_ch * pad
    depth = split + LANES
    part_rows = rows // n_ch
    cells = part_rows * cols
    swap = n_lat == 2
    scale = 1.0 / math.sqrt(rows * n_lat * cols * n_lon)
    core = [(i, i ^ 1) for i in range(n_ch)]
    across = [(i, i ^ 2) for i in range(n_ch)]
    both = [(i, i ^ 3) for i in range(n_ch)]
    block = shape((rows, pad, cols), BF)
    quarter = shape((part_rows, pad, cols), BF)
    flat = pltpu.VMEM((rows * pad, cols), F32)

    masked, *strips = call(
        functools.partial(prepare_state, swap),
        [block] + strip_shapes(pad, swap),
        [ocean_state, land_mask],
        [flat],
        "state_rows",
    )
    weights = call(
        functools.partial(pack_weights, part, pad),
        [shape((hid, wide), BF)],
        [expand_weight, expand_bias.reshape(1, hidden), project_weight],
        (),
        "weight_rows",
    )[0]
    taps = jnp.pad(depth_kernel.reshape(9, part).T, ((0, pad - part), (0, LANES - 9)))
    cotan, *cotan_parts = call(
        prepare_cotan,
        [block] + [quarter] * 4,
        [out_grad, land_mask, swath_offset.reshape(1, -1), swath_value.reshape(1, -1)],
        [flat],
        "cotan_rows",
    )
    around = exchange_halo(strips, rows, pad, swap, "state_columns")

    def spread_parts(parts):
        return [
            parts[0],
            lax.ppermute(parts[1], "ch", core),
            lax.ppermute(parts[2], "ch", across),
            lax.ppermute(parts[3], "ch", both),
        ]

    weights_across = lax.ppermute(weights, "ch", across)
    all_weights = [
        weights,
        lax.ppermute(weights, "ch", core),
        weights_across,
        lax.ppermute(weights_across, "ch", core),
    ]
    all_cotan = spread_parts(cotan_parts)
    conv_parts = call(
        functools.partial(conv_forward, part),
        [quarter] * 4,
        [masked, *around, taps],
        [pltpu.VMEM((rows, pad, cols), BF)],
        "conv_forward",
    )
    all_conv = spread_parts(conv_parts)
    tile_rows = wide // LANES * hid
    *grad_parts, keep, send = call(
        mlp,
        [quarter] * 4 + [shape((2, tile_rows, LANES), F32), shape((2, tile_rows, LANES), BF)],
        [*all_conv, *all_cotan, *all_weights],
        [
            pltpu.VMEM((depth, cells), BF),
            pltpu.VMEM((depth, cells), BF),
            pltpu.VMEM((n_ch * hid, wide), BF),
            pltpu.VMEM((depth, n_ch * hid), BF),
            pltpu.VMEM((n_ch * hid, cells), BF),
            pltpu.VMEM((n_ch * hid, cells), BF),
            pltpu.VMEM((depth, cells), BF),
        ],
        "mlp",
        flops=10 * cells * depth * n_ch * hid,
    )
    got = lax.ppermute(send, "ch", core)
    grad_got = spread_parts(grad_parts)
    conv_grad, *grad_strips = call(
        functools.partial(collect_grad, swap),
        [block] + strip_shapes(pad, swap),
        grad_got,
        (),
        "grad_rows",
    )
    grad_around = exchange_halo(grad_strips, rows, pad, swap, "grad_columns")
    kernel_part = call(
        kernel_gradient,
        [shape((pad, LANES), F32)],
        [conv_grad, masked, *around],
        (),
        "kernel_gradient",
    )[0]
    state_grad = call(
        conv_adjoint,
        [shape((part, rows, cols), BF)],
        [conv_grad, *grad_around, taps, cotan, land_mask],
        [flat],
        "conv_adjoint",
    )[0]
    outs = [
        shape((channels, hidden), F32),
        shape((hidden, channels), F32),
        shape((1, hidden), F32),
        shape((9, part), F32),
    ]
    turn = pltpu.VMEM((LANES, LANES), F32)
    if n_lat == 2 and n_lon == 4 and tile_rows % 32 == 0 and (tile_rows // 2 - 16) % 64 == 0:
        half = tile_rows // 2
        step = (half - 16) // 4
        piece = step + 16
        mine, to_y, to_x, to_xy = call(
            add_cores,
            [shape((half, LANES), F32)] + [shape((half, LANES), BF)] * 3,
            [keep, got],
            (),
            "add_cores",
        )
        both_axes = [
            (lat * n_ch + i, (1 - lat) * n_ch + (i ^ 2)) for lat in range(n_lat) for i in range(n_ch)
        ]
        planes = [
            lax.ppermute(to_y, "lat", [(0, 1), (1, 0)]),
            lax.ppermute(to_x, "ch", across),
            lax.ppermute(to_xy, ("lat", "ch"), both_axes),
        ]
        own, *line_parts = call(
            add_planes,
            [shape((piece, LANES), F32)] + [shape((piece, LANES), BF)] * 3,
            [mine, *planes],
            [pltpu.VMEM((half, LANES), F32)],
            "add_planes",
        )
        turns = [[(i, i ^ k) for i in range(n_lon)] for k in range(4)]
        lines = [lax.ppermute(line_parts[k - 1], "lon", turns[k]) for k in (1, 2, 3)]
        summed = call(
            add_lines, [shape((piece + pad, LANES), BF)], [own, *lines, kernel_part], (), "add_lines"
        )[0]
        pieces = [summed] + [lax.ppermute(summed, "lon", turns[k]) for k in (1, 2, 3)]
        mine = call(
            functools.partial(join_lines, piece),
            [shape((half + pad, LANES), BF)],
            pieces,
            [pltpu.VMEM((4 * pad, LANES), F32)],
            "join_lines",
        )[0]
        other = lax.ppermute(mine, "lat", [(0, 1), (1, 0)])
        expand_grad, project_grad, bias_grad, kernel_grad = call(
            functools.partial(write_parameters, part, pad, scale, hid),
            outs,
            [mine, other],
            [pltpu.VMEM((tile_rows, LANES), BF), turn],
            "write_parameters",
        )
    else:
        total = keep + got.astype(F32)
        total = total[0] + lax.ppermute(total[1].astype(BF), "ch", across).astype(F32)
        total, kernel_sum = lax.psum((total, kernel_part), ("lon", "lat"))
        expand_grad, project_grad, bias_grad, kernel_grad = call(
            functools.partial(unpack_whole, part, pad, scale, hid),
            outs,
            [total.astype(BF), kernel_sum],
            [turn],
            "write_parameters",
        )
    return (
        state_grad,
        expand_grad,
        project_grad,
        bias_grad.reshape(hidden),
        kernel_grad.reshape(3, 3, part),
    )


def solution(mesh):
    return jax.shard_map(
        on_device,
        mesh=mesh,
        in_specs=(
            P("ch", "lat", "lon"),
            P("lat", "lon"),
            P("ch", "lat", "lon"),
            P("lat", "lon", None),
            P("lat", "lon", None),
            P(None, None, "ch"),
            P(None, "ch"),
            P("ch"),
            P("ch", None),
        ),
        out_specs=(
            P("ch", "lat", "lon"),
            P(None, "ch"),
            P("ch", None),
            P("ch"),
            P(None, None, "ch"),
        ),
        check_vma=False,
    )
```

```python
import functools
import math

import jax
import jax.numpy as jnp
from jax import lax
from jax.experimental import pallas as pl
from jax.experimental.pallas import tpu as pltpu
from jax.sharding import PartitionSpec as P

DIL = 2
LANES = 128
RIDE = 96
BF = jnp.bfloat16
F32 = jnp.float32


def shape(dims, kind):
    return jax.ShapeDtypeStruct(dims, kind)


def call(kernel, outs, args, scratch=(), name=None, flops=0, aliases=None, far=False, after=()):
    count = len(args)
    if after:
        body, args = kernel, [*args, *after]

        def kernel(*refs):
            body(*refs[:count], *refs[len(args) :])

    if far:
        args = [pltpu.with_memory_space_constraint(a, pltpu.HBM) for a in args]
    spaces = [pltpu.HBM if far else pl.ANY if i >= count else pltpu.VMEM for i in range(len(args))]
    moved = sum(math.prod(a.shape) * a.dtype.itemsize for a in list(args) + list(outs))
    return pl.pallas_call(
        kernel,
        out_shape=tuple(outs),
        in_specs=[pl.BlockSpec(memory_space=space) for space in spaces],
        out_specs=tuple(pl.BlockSpec(memory_space=pltpu.VMEM) for _ in outs),
        scratch_shapes=list(scratch),
        input_output_aliases=aliases or {},
        name=name,
        compiler_params=pltpu.CompilerParams(vmem_limit_bytes=24 * 1024 * 1024),
        cost_estimate=pl.CostEstimate(flops=flops, bytes_accessed=moved, transcendentals=0),
    )(*args)


def iota(dims, dim):
    return lax.broadcasted_iota(jnp.int32, dims, dim)


def aligned(index):
    return pl.multiple_of(index, 16)


def to_rows(block_ref, weight, scr, pad):
    channels, rows, cols = block_ref.shape

    def body(c, carry):
        value = block_ref[c].astype(F32)
        if weight is not None:
            value = value * weight
        scr[pl.ds(c, rows, stride=pad), :] = value
        return carry

    lax.fori_loop(0, channels, body, 0, unroll=5 if channels % 5 == 0 else 1)
    for c in range(channels, pad):
        scr[pl.ds(c, rows, stride=pad), :] = jnp.zeros((rows, cols), F32)


def pack_columns(value, ext_row, left, right):
    lane = iota(value.shape, 1)
    here = (lane == 2 * ext_row) | (lane == 2 * ext_row + 1)
    size = value.shape[1]
    left = jnp.where(here, pltpu.roll(value, (2 * ext_row) % size, 1), left)
    right = jnp.where(here, pltpu.roll(value, (2 * ext_row + 2) % size, 1), right)
    return left, right


def mirrored(value):
    size = value.shape[1]
    flip = (iota((size, size), 0) + iota((size, size), 1) == size - 1).astype(BF)
    return jnp.dot(value, flip, preferred_element_type=F32).astype(BF)


def emit_strips(read, rows, pad, swap, strips):
    if swap:
        strip_ref, fold_ref, left_ref, right_ref = strips
        at_bottom = lax.axis_index("lat") == 0
        for t in range(DIL):
            low, high = read(t), read(rows - DIL + t)
            strip_ref[t] = jnp.where(at_bottom, high.astype(F32), low.astype(F32)).astype(BF)
    else:
        down_ref, up_ref, fold_ref, left_ref, right_ref = strips
        for t in range(DIL):
            down_ref[t] = read(t)
            up_ref[t] = read(rows - DIL + t)
    for t in range(DIL):
        fold_ref[t] = mirrored(read(rows - 1 - t))
    left = jnp.zeros((pad, LANES), F32)
    right = jnp.zeros((pad, LANES), F32)
    for r in range(rows):
        left, right = pack_columns(read(r).astype(F32), r + DIL, left, right)
    left_ref[...] = left.astype(BF)
    right_ref[...] = right.astype(BF)


def strip_shapes(pad, swap):
    one = shape((DIL, pad, LANES), BF)
    packs = [shape((pad, LANES), BF)] * 2
    return ([one] if swap else [one, one]) + [one] + packs


def prepare_state(swap, state_ref, mask_ref, rows_ref, *rest):
    strips, scr = rest[:-1], rest[-1]
    rows, pad = rows_ref.shape[:2]
    to_rows(state_ref, mask_ref[...].astype(F32), scr, pad)
    for r in range(rows):
        rows_ref[r] = scr[r * pad : (r + 1) * pad, :].astype(BF)
    emit_strips(lambda r: rows_ref[r], rows, pad, swap, strips)


def prepare_cotan(part, *refs):
    rows_ref, own_ref, core_ref, far_ref, taps_ref, mask_ref, state_ref = refs[9:16]
    scr, weights_scr, turn_scr, sems = refs[16:20]
    grad_ref, offset_ref, value_ref = refs[20:23]
    held = (grad_ref, mask_ref, offset_ref, value_ref, *refs[23:27], state_ref)
    copies = [pltpu.make_async_copy(refs[k], held[k], sems.at[k]) for k in range(9)]
    for k in (4, 5, 6, 7, 0, 1, 2, 3, 8):
        copies[k].start()
    for k in range(4, 8):
        copies[k].wait()
    pack_weights(part, rows_ref.shape[1], *held[4:8], weights_scr, taps_ref, turn_scr)
    for k in range(0, 4):
        copies[k].wait()
    rows, pad, cols = rows_ref.shape
    me = lax.axis_index("ch")
    mask = mask_ref[...].astype(F32)
    to_rows(grad_ref, None, scr, pad)
    offset = offset_ref[...]
    points = offset.shape[1]
    value = value_ref[...]
    total = jnp.zeros((rows, cols), F32)
    row_hot = iota((rows, points), 0) == offset // cols
    col_hot = (iota((cols, points), 0) == offset % cols).astype(BF)
    for _ in range(3):
        part = value.astype(BF)
        value = value - part.astype(F32)
        lhs = jnp.where(row_hot, part.astype(F32), 0.0).astype(BF)
        total = total + lax.dot_general(
            lhs, col_hot, (((1,), (1,)), ((), ())), preferred_element_type=F32
        )
    total = jnp.where(me == 0, total, 0.0)
    first = scr[pl.ds(0, rows, stride=pad), :]
    scr[pl.ds(0, rows, stride=pad), :] = first + total
    for r in range(rows):
        rows_ref[r] = (scr[r * pad : (r + 1) * pad, :] * mask[r : r + 1, :]).astype(BF)
    tiles = weights_scr.shape[1] // LANES
    hid = weights_scr.shape[0]
    for to in (own_ref, core_ref, far_ref):
        for t in range(tiles):
            to[t * hid : (t + 1) * hid, :] = weights_scr[:, t * LANES : (t + 1) * LANES]
    count = (own_ref.shape[0] - tiles * hid) // pad
    for k, (to, slot) in enumerate(((own_ref, 0), (core_ref, 0), (far_ref, 0), (far_ref, 1))):
        for r in range(count):
            at = tiles * hid + (slot * count + r) * pad
            to[at : at + pad, :] = rows_ref[(me ^ k) * count + r]
    copies[8].wait()


def relay(in_ref, out_ref):
    del in_ref, out_ref


def ring(count, step):
    return [(i, (i + step) % count) for i in range(count)]


def exchange_halo(strips, rows, pad, swap, name, riding=()):
    n_lat, n_lon = lax.axis_size("lat"), lax.axis_size("lon")
    top = n_lat - 1
    fold_pairs = [
        (lon * n_lat + top, (n_lon - 1 - lon) * n_lat + top) for lon in range(n_lon)
    ]
    if swap:
        strip, fold, left, right = strips
        moved = [lax.ppermute(strip, "lat", [(0, 1), (1, 0)])]
    else:
        down, up, fold, left, right = strips
        moved = [
            lax.ppermute(up, "lat", [(i, i + 1) for i in range(n_lat - 1)]),
            lax.ppermute(down, "lat", [(i + 1, i) for i in range(n_lat - 1)]),
        ]
    fold = lax.ppermute(fold, ("lon", "lat"), fold_pairs)
    kernel = functools.partial(finish_columns, rows, swap, len(riding) > 0)
    halo, left, right = call(
        kernel,
        [shape((2 * DIL, pad, LANES), BF)] + [shape((pad, LANES), BF)] * 2,
        [*riding, *moved, fold, left, right],
        name=name,
    )
    from_right = lax.ppermute(left, "lon", ring(n_lon, -1))
    from_left = lax.ppermute(right, "lon", ring(n_lon, 1))
    return halo, from_left, from_right


def finish_columns(rows, swap, riding, *refs):
    if riding:
        ride_ref, *refs = refs
    if swap:
        strip_ref, fold_ref, left_ref, right_ref, halo_ref, left_out, right_out = refs
        low_ref = high_ref = strip_ref
    else:
        low_ref, high_ref, fold_ref, left_ref, right_ref, halo_ref, left_out, right_out = refs
    lat, count = lax.axis_index("lat"), lax.axis_size("lat")
    left, right = left_ref[...].astype(F32), right_ref[...].astype(F32)
    for t in range(DIL):
        south = jnp.where(lat == 0, 0.0, low_ref[t].astype(F32))
        north = jnp.where(lat == count - 1, fold_ref[t].astype(F32), high_ref[t].astype(F32))
        halo_ref[t] = south.astype(BF)
        halo_ref[DIL + t] = north.astype(BF)
        left, right = pack_columns(south, t, left, right)
        left, right = pack_columns(north, rows + DIL + t, left, right)
    if riding:
        ride = pltpu.roll(ride_ref[...].astype(F32), RIDE, 1)
        left, right = left + ride, right + ride
    left_out[...] = left.astype(BF)
    right_out[...] = right.astype(BF)


def shifted_rows(block_ref, halo_ref, left_ref, right_ref, group):
    rows = block_ref.shape[0]
    at = pl.ds(aligned(group * 16), 16)
    lane = iota((16, LANES), 1)
    left, right = left_ref[at, :].astype(F32), right_ref[at, :].astype(F32)
    for e in range(rows + 2 * DIL):
        if e < DIL:
            row = halo_ref[e, at, :]
        elif e < rows + DIL:
            row = block_ref[e - DIL, at, :]
        else:
            row = halo_ref[e - rows, at, :]
        row = row.astype(F32)
        west = jnp.where(
            lane < DIL, pltpu.roll(left, (-2 * e) % LANES, 1), pltpu.roll(row, DIL, 1)
        )
        east = jnp.where(
            lane >= LANES - DIL,
            pltpu.roll(right, (LANES - DIL - 2 * e) % LANES, 1),
            pltpu.roll(row, LANES - DIL, 1),
        )
        yield e, (west, row, east)


def stencil(block_ref, halo_ref, left_ref, right_ref, group, taps, north, emit):
    rows = block_ref.shape[0]
    sums = {}
    for e, shifts in shifted_rows(block_ref, halo_ref, left_ref, right_ref, group):
        for a in (2, 1, 0):
            r = e - DIL * a
            if not 0 <= r < rows:
                continue
            used = north if e >= rows + DIL else taps[a]
            term = used[0] * shifts[0] + used[1] * shifts[1] + used[2] * shifts[2]
            sums[r] = term if r not in sums else sums[r] + term
            if a == 2:
                emit(r, sums.pop(r))


def spread(tap_ref, group):
    values = tap_ref[pl.ds(aligned(group * 16), 16), :]
    return [
        [jnp.broadcast_to(values[:, 3 * a + b : 3 * a + b + 1], (16, LANES)) for b in range(3)]
        for a in range(3)
    ]


def conv_forward(ones_row, block_ref, halo_ref, left_ref, right_ref, tap_ref, *rest):
    quarters, scr = rest[:-1], rest[-1]
    pad = block_ref.shape[1]

    def body(group, carry):
        taps = spread(tap_ref, group)
        is_one = iota((16, LANES), 0) + group * 16 == ones_row

        def emit(r, value):
            value = jnp.where(is_one, 1.0, value)
            scr[r, pl.ds(aligned(group * 16), 16), :] = value.astype(BF)

        stencil(block_ref, halo_ref, left_ref, right_ref, group, taps, taps[2], emit)
        return carry

    lax.fori_loop(0, pad // 16, body, 0)
    me = lax.axis_index("ch")
    count = quarters[0].shape[0]
    for k, quarter in enumerate(quarters):
        quarter[...] = scr[pl.ds((me ^ k) * count, count)]


def conv_adjoint(
    block_ref, halo_ref, left_ref, right_ref, tap_ref, cotan_ref, mask_ref, out_ref, scr
):
    rows, pad = block_ref.shape[:2]
    at_top = lax.axis_index("lat") == lax.axis_size("lat") - 1
    mask = mask_ref[...].astype(F32)

    def body(group, carry):
        taps = spread(tap_ref, group)
        back = [[taps[2 - a][2 - b] for b in range(3)] for a in range(3)]
        north = [jnp.where(at_top, taps[2][b], back[2][b]) for b in range(3)]

        def emit(r, value):
            cotan = cotan_ref[r, pl.ds(aligned(group * 16), 16), :].astype(F32)
            scr[pl.ds(pl.multiple_of(r * pad + group * 16, 16), 16), :] = (cotan + value) * mask[
                r : r + 1, :
            ]

        stencil(block_ref, halo_ref, left_ref, right_ref, group, back, north, emit)
        return carry

    lax.fori_loop(0, pad // 16, body, 0)

    def write(c, carry):
        out_ref[c] = scr[pl.ds(c, rows, stride=pad), :].astype(BF)
        return carry

    channels = out_ref.shape[0]
    lax.fori_loop(0, channels, write, 0, unroll=5 if channels % 5 == 0 else 1)


def collect_grad(swap, q0, q1, q2, q3, rows_ref, *strips):
    part_rows = q0.shape[0]
    rows, pad = rows_ref.shape[:2]
    me = lax.axis_index("ch")
    for k, quarter in enumerate((q0, q1, q2, q3)):
        rows_ref[pl.ds((me ^ k) * part_rows, part_rows)] = quarter[...]
    emit_strips(lambda r: rows_ref[r], rows, pad, swap, strips)


def kernel_gradient(grad_ref, block_ref, halo_ref, left_ref, right_ref, out_ref):
    rows, pad = grad_ref.shape[:2]

    def body(group, carry):
        at = pl.ds(aligned(group * 16), 16)
        sums = [[jnp.zeros((16, LANES), F32) for _ in range(3)] for _ in range(3)]
        for e, shifts in shifted_rows(block_ref, halo_ref, left_ref, right_ref, group):
            for a in range(3):
                r = e - DIL * a
                if 0 <= r < rows:
                    grad = grad_ref[r, at, :].astype(F32)
                    for b in range(3):
                        sums[a][b] = sums[a][b] + grad * shifts[b]
        lane = iota((16, LANES), 1)
        out = jnp.zeros((16, LANES), F32)
        for a in range(3):
            for b in range(3):
                total = jnp.sum(sums[a][b], axis=1, keepdims=True)
                out = jnp.where(lane == 3 * a + b, total, out)
        out_ref[at, :] = out.astype(BF)
        return carry

    lax.fori_loop(0, pad // 16, body, 0)


def channel_of(slot, part, pad):
    block = sum((slot >= pad * b).astype(jnp.int32) for b in range(1, 4))
    inside = slot - block * pad
    return jnp.where((slot >= 0) & (slot < 4 * pad) & (inside < part), block * part + inside, -1)


def expand_slot(lane, pad):
    return jnp.where(lane < 4 * pad, lane, -1)


def project_slot(lane, pad, split):
    tail = 4 * pad - split
    low = LANES - tail
    return jnp.where(lane >= LANES, lane - LANES, jnp.where(lane >= low, lane - low + split, -1))


def pack_weights(part, pad, expand_ref, bias_ref, project_ref, kernel_ref, out_ref, taps_ref, turn_scr):
    hidden, channels = expand_ref.shape
    turn_scr[...] = jnp.zeros(turn_scr.shape, F32)
    for a in range(3):
        turn_scr[3 * a : 3 * a + 3, 0:part] = kernel_ref[a]
    taps_ref[...] = jnp.transpose(turn_scr[...])[0:pad, :]
    wide = out_ref.shape[1]
    split = 4 * pad // LANES * LANES
    lane = iota((channels, wide), 1)
    row = iota((channels, wide), 0)
    pick_e = (channel_of(expand_slot(lane, pad), part, pad) == row).astype(BF)
    slot = jnp.where(lane >= split, project_slot(lane - split, pad, split), -1)
    pick_p = (channel_of(slot, part, pad) == row).astype(BF)
    bias = bias_ref[...]
    parts = jnp.zeros((16, hidden), F32)
    at = iota((16, hidden), 0)
    for k in range(3):
        piece = bias.astype(BF).astype(F32)
        bias = bias - piece
        parts = jnp.where(at == k, piece, parts)
    lane, row = iota((16, wide), 1), iota((16, wide), 0)
    pick_b = ((lane == row * pad + part) & (row < 3)).astype(BF)
    turned = (((0,), (0,)), ((), ()))
    packed = (
        jnp.dot(expand_ref[...], pick_e, preferred_element_type=F32)
        + lax.dot_general(parts.astype(BF), pick_b, turned, preferred_element_type=F32)
        + jnp.dot(project_ref[...], pick_p, preferred_element_type=F32)
    )
    rows = out_ref.shape[0]
    out_ref[0:hidden, :] = packed.astype(BF)
    out_ref[hidden:rows, :] = jnp.zeros((rows - hidden, wide), BF)


GELU_C = math.sqrt(2.0 / math.pi)


def activation_gradient(*refs):
    parts = refs[0:4]
    act_ref, y_scr, w_scr, t_scr = refs[4:]
    me = lax.axis_index("ch")
    tiles = w_scr.shape[1] // LANES
    hid = w_scr.shape[0] // 4
    depth, cells = y_scr.shape
    part_rows = cells // LANES
    pad = (parts[0].shape[0] - tiles * hid) // part_rows
    split = 4 * pad // LANES * LANES
    y_scr[0 : depth - 4 * pad, :] = jnp.zeros((depth - 4 * pad, cells), BF)
    for k, ref in enumerate(parts):
        for t in range(tiles):
            w_scr[k * hid : (k + 1) * hid, t * LANES : (t + 1) * LANES] = ref[
                t * hid : (t + 1) * hid, :
            ]
        block = me ^ k
        start = tiles * hid + (part_rows * pad if k == 3 else 0)
        for r in range(part_rows):
            cols = slice(r * LANES, (r + 1) * LANES)
            for u in range(pad // 16):
                slot = block * pad + 16 * u
                to = jnp.where(slot < split, slot + LANES, slot - split + depth - 4 * pad)
                at = start + r * pad + 16 * u
                y_scr[pl.ds(aligned(to), 16), cols] = ref[at : at + 16, :]
    t_scr[...] = jnp.transpose(w_scr[:, 0:depth])
    step = 256
    for start in range(0, cells, step):
        cols = slice(start, start + step)
        act_ref[:, cols] = jnp.dot(
            w_scr[:, split : split + depth], y_scr[:, cols], preferred_element_type=F32
        )


def hidden_gradient(*refs):
    xs, (act_ref, y_ref, w_ref) = refs[0:4], refs[4:7]
    pre_ref, keep_ref, send_ref, x_scr, value_scr = refs[7:]
    part_rows, pad = xs[0].shape[:2]
    hid = w_ref.shape[0] // 4
    split = 4 * pad // LANES * LANES
    depth, cells = x_scr.shape
    me = lax.axis_index("ch")
    x_scr[4 * pad : depth, :] = jnp.zeros((depth - 4 * pad, cells), BF)
    for k in range(4):
        for r in range(part_rows):
            x_scr[pl.ds(aligned((me ^ k) * pad), pad), r * LANES : (r + 1) * LANES] = xs[k][r]
    step = 256
    for start in range(0, cells, step):
        cols = slice(start, start + step)
        hidden = jnp.dot(w_ref[:, 0:depth], x_scr[:, cols], preferred_element_type=F32)
        square = hidden * hidden
        tanh = jnp.tanh(GELU_C * hidden * (1.0 + 0.044715 * square))
        half = 0.5 * (1.0 + tanh)
        slope = half + (0.5 * GELU_C) * hidden * (1.0 - tanh * tanh) * (
            1.0 + (3 * 0.044715) * square
        )
        value_scr[:, cols] = (hidden * half).astype(BF)
        pre_ref[:, cols] = (act_ref[:, cols] * slope).astype(BF)
    over_cells = (((1,), (1,)), ((), ()))
    expand = lax.dot_general(pre_ref[...], x_scr[...], over_cells, preferred_element_type=F32)
    project = lax.dot_general(value_scr[...], y_ref[...], over_cells, preferred_element_type=F32)
    shared = split // LANES
    tiles = [expand[:, t * LANES : (t + 1) * LANES] for t in range(shared)]
    tiles.append(expand[:, split : split + LANES] + project[:, 0:LANES])
    tiles += [project[:, t * LANES : (t + 1) * LANES] for t in range(1, shared + 1)]
    for k in range(4):
        to = send_ref if k % 2 else keep_ref
        for t, tile in enumerate(tiles):
            to[k // 2, t * hid : (t + 1) * hid, :] = tile[k * hid : (k + 1) * hid].astype(to.dtype)


def conv_gradient(pre_ref, t_ref, *rest):
    outs, scr = rest[:-1], rest[-1]
    part_rows, pad = outs[0].shape[:2]
    me = lax.axis_index("ch")
    step = 256
    for start in range(0, pre_ref.shape[1], step):
        cols = slice(start, start + step)
        scr[:, cols] = jnp.dot(t_ref[...], pre_ref[:, cols], preferred_element_type=F32).astype(BF)
    for k, to in enumerate(outs):
        for r in range(part_rows):
            to[r] = scr[pl.ds(aligned((me ^ k) * pad), pad), r * LANES : (r + 1) * LANES]


def add_cores(keep_ref, got_ref, own_ref, *sends):
    piece = own_ref.shape[1]
    step = piece - 32
    place = 2 * lax.axis_index("lat") + lax.axis_index("lon") % 2
    for k in range(4):
        at = pl.ds(pl.multiple_of((place ^ k) * step, 32), piece)
        for group in range(2):
            total = keep_ref[group, at, :] + got_ref[group, at, :].astype(F32)
            to = sends[k - 1] if k else own_ref
            to[group] = total.astype(to.dtype)


def add_pieces(own_ref, a_ref, b_ref, c_ref, mine_ref, other_ref):
    for group, to in enumerate((mine_ref, other_ref)):
        total = own_ref[group] + (
            a_ref[group].astype(F32) + b_ref[group].astype(F32) + c_ref[group].astype(F32)
        )
        to[...] = total.astype(to.dtype)


def add_across(mine_ref, got_ref, out_ref):
    out_ref[...] = (mine_ref[...] + got_ref[...].astype(F32)).astype(BF)


def finish_pieces(mine_ref, line_ref, kernel_ref, left_ref, right_ref, out_ref):
    piece = mine_ref.shape[0]
    out_ref[0:piece, :] = (mine_ref[...].astype(F32) + line_ref[...].astype(F32)).astype(BF)
    even = lax.axis_index("lon") % 2 == 0
    other = jnp.where(even, left_ref[...].astype(F32), right_ref[...].astype(F32))
    other = pltpu.roll(other, LANES - RIDE + 16, 1)
    lane = iota(other.shape, 1)
    here = kernel_ref[...].astype(F32)
    out_ref[piece : out_ref.shape[0], :] = jnp.where(
        lane < 16, here, jnp.where(lane < 32, other, 0.0)
    ).astype(BF)


def write_parameters(part, pad, scale, hid, p0, p1, p2, p3, *rest):
    expand_ref, project_ref, bias_ref, taps_ref, all_scr, taps_scr, turn_scr = rest
    piece = p0.shape[0] - pad
    step = piece - 32
    place = 2 * lax.axis_index("lat") + lax.axis_index("lon") % 2
    for k, ref in enumerate((p0, p1, p2, p3)):
        to = place ^ k
        all_scr[pl.ds(pl.multiple_of(to * step, 32), step), :] = ref[0:step, :]

        @pl.when(to == 3)
        def _():
            all_scr[4 * step : 4 * step + 32, :] = ref[step:piece, :]

        lat, lon = lax.axis_index("lat") ^ (k >> 1), lax.axis_index("lon") ^ (k & 1)
        taps = ref[piece : piece + pad, :].astype(F32)
        taps_scr[pl.ds(aligned((4 * lat + lon) * pad), pad), :] = taps
        taps_scr[pl.ds(aligned((4 * lat + (lon ^ 3)) * pad), pad), :] = pltpu.roll(
            taps, LANES - 16, 1
        )
    unpack(part, pad, scale, hid, all_scr, expand_ref, project_ref, bias_ref)
    total = taps_scr[0:pad, :]
    for k in range(1, 8):
        total = total + taps_scr[k * pad : (k + 1) * pad, :]
    write_taps(total, scale, taps_ref, turn_scr)


def write_taps(total, scale, taps_ref, turn_scr):
    turn_scr[...] = jnp.zeros(turn_scr.shape, F32)
    turn_scr[0 : total.shape[0], :] = total * scale
    turned = jnp.transpose(turn_scr[...])
    for a in range(3):
        taps_ref[a] = turned[3 * a : 3 * a + 3, 0 : taps_ref.shape[2]]


def unpack(part, pad, scale, hid, all_ref, expand_ref, project_ref, bias_ref):
    hidden, channels = expand_ref.shape
    split = 4 * pad // LANES * LANES
    shared = split // LANES
    tiles = [all_ref[t * hid : (t + 1) * hid, :] for t in range(2 * shared + 1)]
    depth = (shared + 1) * LANES
    expand = jnp.concatenate(tiles[: shared + 1], axis=1)
    project = jnp.concatenate(tiles[shared:], axis=1)
    lane, row = iota((channels, depth), 1), iota((channels, depth), 0)
    pick_e = (channel_of(expand_slot(lane, pad), part, pad) == row).astype(BF)
    pick_p = (channel_of(project_slot(lane, pad, split), part, pad) == row).astype(BF)
    pick_b = (iota((16, depth), 1) == part).astype(BF)
    last = (((1,), (1,)), ((), ()))
    dot = functools.partial(lax.dot_general, dimension_numbers=last, preferred_element_type=F32)
    expand_ref[...] = dot(expand, pick_e)[0:hidden, :] * scale
    bias_ref[...] = dot(pick_b, expand)[0:1, 0:hidden] * scale
    project_ref[...] = dot(project, pick_p)[0:hidden, :] * scale


def unpack_whole(part, pad, scale, hid, all_ref, taps_in, expand_ref, project_ref, bias_ref, taps_ref, turn_scr):
    unpack(part, pad, scale, hid, all_ref, expand_ref, project_ref, bias_ref)
    write_taps(taps_in[...], scale, taps_ref, turn_scr)


def on_device(
    ocean_state,
    land_mask,
    out_grad,
    swath_offset,
    swath_value,
    depth_kernel,
    expand_weight,
    expand_bias,
    project_weight,
):
    part, rows, cols = ocean_state.shape
    n_lon, n_lat, n_ch = lax.axis_size("lon"), lax.axis_size("lat"), lax.axis_size("ch")
    channels, hidden = expand_weight.shape
    assert n_ch == 4 and cols == LANES and rows % n_ch == 0
    pad = (part + 16) // 16 * 16
    hid = (hidden + 15) // 16 * 16
    split = n_ch * pad // LANES * LANES
    tail = n_ch * pad - split
    assert tail == LANES // 2
    wide = 2 * n_ch * pad
    depth = split + LANES
    part_rows = rows // n_ch
    cells = part_rows * cols
    swap = n_lat == 2
    scale = 1.0 / math.sqrt(rows * n_lat * cols * n_lon)
    core = [(i, i ^ 1) for i in range(n_ch)]
    across = [(i, i ^ 2) for i in range(n_ch)]
    block = shape((rows, pad, cols), BF)
    quarter = shape((part_rows, pad, cols), BF)
    flat = pltpu.VMEM((rows * pad, cols), F32)

    turn = pltpu.VMEM((LANES, LANES), F32)
    def spread_parts(parts):
        return [parts[0]] + [
            lax.ppermute(parts[k], "ch", [(i, i ^ k) for i in range(n_ch)]) for k in (3, 2, 1)
        ][::-1]

    tile_rows = wide // LANES * hid
    near_rows, far_rows = tile_rows + part_rows * pad, tile_rows + 2 * part_rows * pad
    prepared = [
        out_grad,
        land_mask,
        swath_offset.reshape(1, -1),
        swath_value.reshape(1, -1),
        expand_weight.T,
        expand_bias.reshape(1, hidden),
        project_weight,
        depth_kernel,
        ocean_state,
    ]
    cotan, own, to_core, to_far, taps, land_mask, ocean_state = call(
        functools.partial(prepare_cotan, part),
        [
            block,
            shape((near_rows, LANES), BF),
            shape((near_rows, LANES), BF),
            shape((far_rows, LANES), BF),
            shape((pad, LANES), F32),
            shape(land_mask.shape, land_mask.dtype),
            shape(ocean_state.shape, ocean_state.dtype),
        ],
        prepared,
        [flat, pltpu.VMEM((hid, wide), BF), turn, pltpu.SemaphoreType.DMA((9,))]
        + [pltpu.VMEM(prepared[k].shape, prepared[k].dtype) for k in (0, 2, 3, 4, 5, 6, 7)],
        "cotan_rows",
        far=True,
    )
    masked, *strips = call(
        functools.partial(prepare_state, swap),
        [block] + strip_shapes(pad, swap),
        [ocean_state, land_mask],
        [flat],
        "state_rows",
        after=[taps],
    )
    around = exchange_halo(strips, rows, pad, swap, "state_columns")
    from_far = lax.ppermute(to_far, "ch", across)
    conv_parts = call(
        functools.partial(conv_forward, part),
        [quarter] * 4,
        [masked, *around, taps],
        [pltpu.VMEM((rows, pad, cols), BF)],
        "conv_forward",
    )
    all_conv = spread_parts(conv_parts)
    from_far = call(
        relay, [from_far], [from_far], (), "cotan_relay", aliases={0: 0}, after=around[1:]
    )[0]
    passed = lax.ppermute(from_far, "ch", core)
    act_grad, cotan_all, weights_all, weights_turned = call(
        activation_gradient,
        [
            shape((n_ch * hid, cells), F32),
            shape((depth, cells), BF),
            shape((n_ch * hid, wide), BF),
            shape((depth, n_ch * hid), BF),
        ],
        [own, lax.ppermute(to_core, "ch", core), from_far, passed],
        (),
        "activation_gradient",
    )
    pre_grad, keep, send = call(
        hidden_gradient,
        [
            shape((n_ch * hid, cells), BF),
            shape((2, tile_rows, LANES), F32),
            shape((2, tile_rows, LANES), BF),
        ],
        [*all_conv, act_grad, cotan_all, weights_all],
        [pltpu.VMEM((depth, cells), BF), pltpu.VMEM((n_ch * hid, cells), BF)],
        "hidden_gradient",
    )
    got = lax.ppermute(send, "ch", core)
    grad_parts = call(
        conv_gradient,
        [quarter] * 4,
        [pre_grad, weights_turned],
        [pltpu.VMEM((depth, cells), BF)],
        "conv_gradient",
    )
    grad_got = spread_parts(grad_parts)
    staged = n_lat == 2 and n_lon == 4 and tile_rows % 32 == 0
    if staged:
        step = (tile_rows - 32) // 128 * 32
        piece = step + 32
        assert 3 * step + piece == tile_rows
        mine, *sends = call(
            add_cores,
            [shape((2, piece, LANES), F32)] + [shape((2, piece, LANES), BF)] * 3,
            [keep, got],
            (),
            "add_cores",
            after=grad_got[1:2],
        )

        def turn_plane(k):
            pairs = []
            for lon in range(n_lon):
                for lat in range(n_lat):
                    pairs.append((lon * n_lat + lat, (lon ^ (k & 1)) * n_lat + (lat ^ (k >> 1))))
            return pairs

        def over_plane(values):
            return [lax.ppermute(values[k - 1], ("lon", "lat"), turn_plane(k)) for k in (1, 2, 3)]

        mine, other = call(
            add_pieces,
            [shape((piece, LANES), F32), shape((piece, LANES), BF)],
            [mine, *over_plane(sends)],
            (),
            "add_pieces",
        )
    conv_grad, *grad_strips = call(
        functools.partial(collect_grad, swap),
        [block] + strip_shapes(pad, swap),
        grad_got,
        (),
        "grad_rows",
        after=[other] if staged else [],
    )
    if staged:
        mine = call(
            add_across,
            [shape((piece, LANES), BF)],
            [mine, lax.ppermute(other, "ch", across)],
            (),
            "add_across",
        )[0]
    kernel_part = call(
        kernel_gradient,
        [shape((pad, LANES), BF)],
        [conv_grad, masked, *around],
        (),
        "kernel_gradient",
        after=[mine] if staged else [],
    )[0]
    grad_around = exchange_halo(grad_strips, rows, pad, swap, "grad_columns", [kernel_part])
    state_grad = call(
        conv_adjoint,
        [shape((part, rows, cols), BF)],
        [conv_grad, *grad_around, taps, cotan, land_mask],
        [flat],
        "conv_adjoint",
    )[0]
    outs = [
        shape((hidden, channels), F32),
        shape((hidden, channels), F32),
        shape((1, hidden), F32),
        shape((3, 3, part), F32),
    ]
    if staged:
        far_lon = [(lon, lon ^ 2) for lon in range(n_lon)]
        summed = call(
            finish_pieces,
            [shape((piece + pad, LANES), BF)],
            [
                mine,
                lax.ppermute(mine, "lon", far_lon),
                kernel_part,
                *grad_around[1:],
            ],
            (),
            "finish_pieces",
        )[0]
        expand_grad, project_grad, bias_grad, kernel_grad = call(
            functools.partial(write_parameters, part, pad, scale, hid),
            outs,
            [summed, *over_plane([summed] * 3)],
            [pltpu.VMEM((tile_rows, LANES), BF), pltpu.VMEM((8 * pad, LANES), F32), turn],
            "write_parameters",
        )
    else:
        total = keep + got.astype(F32)
        total = total[0] + lax.ppermute(total[1].astype(BF), "ch", across).astype(F32)
        total, kernel_sum = lax.psum((total, kernel_part.astype(F32)), ("lon", "lat"))
        expand_grad, project_grad, bias_grad, kernel_grad = call(
            functools.partial(unpack_whole, part, pad, scale, hid),
            outs,
            [total.astype(BF), kernel_sum],
            [turn],
            "write_parameters",
        )
    return (
        state_grad,
        expand_grad.T,
        project_grad,
        bias_grad.reshape(hidden),
        kernel_grad,
    )


def solution(mesh):
    return jax.shard_map(
        on_device,
        mesh=mesh,
        in_specs=(
            P("ch", "lat", "lon"),
            P("lat", "lon"),
            P("ch", "lat", "lon"),
            P("lat", "lon", None),
            P("lat", "lon", None),
            P(None, None, "ch"),
            P(None, "ch"),
            P("ch"),
            P("ch", None),
        ),
        out_specs=(
            P("ch", "lat", "lon"),
            P(None, "ch"),
            P("ch", None),
            P("ch"),
            P(None, None, "ch"),
        ),
        check_vma=False,
    )
```

```python
import functools
import math

import jax
import jax.numpy as jnp
from jax import lax
from jax.experimental import pallas as pl
from jax.experimental.pallas import tpu as pltpu
from jax.sharding import PartitionSpec as P

DIL = 2
LANES = 128
TAP_ROWS = 16
RIDE = 96
BF = jnp.bfloat16
F32 = jnp.float32


def shape(dims, kind):
    return jax.ShapeDtypeStruct(dims, kind)


def call(kernel, outs, args, scratch=(), name=None, flops=0, aliases=None, far=False, after=()):
    count = len(args)
    if after:
        body, args = kernel, [*args, *after]

        def kernel(*refs):
            body(*refs[:count], *refs[len(args) :])

    if far:
        args = [pltpu.with_memory_space_constraint(a, pltpu.HBM) for a in args]
    spaces = [pltpu.HBM if far else pl.ANY if i >= count else pltpu.VMEM for i in range(len(args))]
    moved = sum(math.prod(a.shape) * a.dtype.itemsize for a in list(args) + list(outs))
    return pl.pallas_call(
        kernel,
        out_shape=tuple(outs),
        in_specs=[pl.BlockSpec(memory_space=space) for space in spaces],
        out_specs=tuple(pl.BlockSpec(memory_space=pltpu.VMEM) for _ in outs),
        scratch_shapes=list(scratch),
        input_output_aliases=aliases or {},
        name=name,
        compiler_params=pltpu.CompilerParams(vmem_limit_bytes=24 * 1024 * 1024),
        cost_estimate=pl.CostEstimate(flops=flops, bytes_accessed=moved, transcendentals=0),
    )(*args)


def iota(dims, dim):
    return lax.broadcasted_iota(jnp.int32, dims, dim)


def aligned(index):
    return pl.multiple_of(index, 16)


def to_rows(block_ref, weight, scr, pad):
    channels, rows, cols = block_ref.shape

    def body(c, carry):
        value = block_ref[c].astype(F32)
        if weight is not None:
            value = value * weight
        scr[pl.ds(c, rows, stride=pad), :] = value
        return carry

    lax.fori_loop(0, channels, body, 0, unroll=5 if channels % 5 == 0 else 1)
    for c in range(channels, pad):
        scr[pl.ds(c, rows, stride=pad), :] = jnp.zeros((rows, cols), F32)


def pack_columns(value, ext_row, left, right):
    lane = iota(value.shape, 1)
    here = (lane == 2 * ext_row) | (lane == 2 * ext_row + 1)
    size = value.shape[1]
    left = jnp.where(here, pltpu.roll(value, (2 * ext_row) % size, 1), left)
    right = jnp.where(here, pltpu.roll(value, (2 * ext_row + 2) % size, 1), right)
    return left, right


def mirrored(value):
    size = value.shape[1]
    flip = (iota((size, size), 0) + iota((size, size), 1) == size - 1).astype(BF)
    return jnp.dot(value, flip, preferred_element_type=F32).astype(BF)


def emit_strips(read, rows, pad, fold_ref, left_ref, right_ref):
    for t in range(DIL):
        fold_ref[t] = mirrored(read(rows - 1 - t))
    left = jnp.zeros((pad, LANES), F32)
    right = jnp.zeros((pad, LANES), F32)
    for r in range(rows):
        left, right = pack_columns(read(r).astype(F32), r + DIL, left, right)
    left_ref[...] = left.astype(BF)
    right_ref[...] = right.astype(BF)


def strip_shapes(pad):
    return [shape((DIL, pad, LANES), BF)] + [shape((pad, LANES), BF)] * 2


def outer_shapes(pad, swap):
    return [shape((DIL, pad, LANES), BF)] * (1 if swap else 2)


def emit_outer(low, high, t, swap, outer):
    if swap:
        outer[0][t] = jnp.where(lax.axis_index("lat") == 0, high, low).astype(BF)
    else:
        outer[0][t] = low.astype(BF)
        outer[1][t] = high.astype(BF)


def prepare_state(state_ref, mask_ref, rows_ref, fold_ref, left_ref, right_ref, scr):
    rows, pad = rows_ref.shape[:2]
    to_rows(state_ref, mask_ref[...].astype(F32), scr, pad)
    for r in range(rows):
        rows_ref[r] = scr[r * pad : (r + 1) * pad, :].astype(BF)
    emit_strips(lambda r: rows_ref[r], rows, pad, fold_ref, left_ref, right_ref)


def add_swath(scr, stride, rows, start, offset_ref, value_ref, cols):
    offset = offset_ref[...]
    points = offset.shape[1]
    value = value_ref[...]
    total = jnp.zeros((rows, cols), F32)
    row_hot = iota((rows, points), 0) + start == offset // cols
    col_hot = (iota((cols, points), 0) == offset % cols).astype(BF)
    for _ in range(3):
        part = value.astype(BF)
        value = value - part.astype(F32)
        lhs = jnp.where(row_hot, part.astype(F32), 0.0).astype(BF)
        total = total + lax.dot_general(
            lhs, col_hot, (((1,), (1,)), ((), ())), preferred_element_type=F32
        )
    total = jnp.where(lax.axis_index("ch") == 0, total, 0.0)
    first = scr[pl.ds(0, rows, stride=stride), :]
    scr[pl.ds(0, rows, stride=stride), :] = first + total


def prepare_far(part, swap, count, *refs):
    outs, (scr, row_scr, weights_scr, turn_scr, sems) = refs[count:-5], refs[-5:]
    far_ref, tiles_ref, taps_ref, *outer = outs[: -count]
    held = outs[-count:]
    copies = [pltpu.make_async_copy(refs[k], held[k], sems.at[k]) for k in range(count)]
    for k in (4, 5, 6, 7, 0, 1, 2, 3, 8):
        copies[k].start()
    for k in range(4, 8):
        copies[k].wait()
    grad_ref, mask_ref, offset_ref, value_ref = held[0:4]
    channels, rows, cols = grad_ref.shape
    pad = taps_ref.shape[0]
    pack_weights(part, pad, *held[4:8], weights_scr, taps_ref, turn_scr)
    hid = weights_scr.shape[0]
    full = tiles_ref.shape[0]
    for t in range(full // hid):
        tiles_ref[t * hid : (t + 1) * hid, :] = weights_scr[:, t * LANES : (t + 1) * LANES]
    far_ref[0:full, :] = tiles_ref[...]
    for k in range(0, 4):
        copies[k].wait()
    half = rows // 2
    me = lax.axis_index("ch")
    start = aligned((1 - me // 2) * half)

    def body(c, carry):
        scr[pl.ds(c, half, stride=pad), :] = grad_ref[c, pl.ds(start, half), :].astype(F32)
        return carry

    lax.fori_loop(0, channels, body, 0, unroll=5 if channels % 5 == 0 else 1)
    for c in range(channels, pad):
        scr[pl.ds(c, half, stride=pad), :] = jnp.zeros((half, cols), F32)
    add_swath(scr, pad, half, start, offset_ref, value_ref, cols)
    mask = mask_ref[pl.ds(start, half), :].astype(F32)
    count_rows = half // 2
    for r in range(half):
        scr[r * pad : (r + 1) * pad, :] = scr[r * pad : (r + 1) * pad, :] * mask[r : r + 1, :]
    for k in range(2):
        first = aligned((((me ^ (2 + k)) % 2) * count_rows) * pad)
        size = count_rows * pad
        far_ref[full + k * size : full + (k + 1) * size, :] = scr[pl.ds(first, size), :].astype(BF)
    copies[8].wait()
    state_ref = held[8]
    state_mask = mask_ref[...].astype(F32)

    def outer_rows(c, carry):
        value = state_ref[c].astype(F32) * state_mask
        row_scr[pl.ds(c, DIL, stride=pad), :] = value[0:DIL, :]
        row_scr[pl.ds(DIL * pad + c, DIL, stride=pad), :] = value[rows - DIL :, :]
        return carry

    lax.fori_loop(0, channels, outer_rows, 0, unroll=5 if channels % 5 == 0 else 1)
    for c in range(channels, pad):
        row_scr[pl.ds(c, 2 * DIL, stride=pad), :] = jnp.zeros((2 * DIL, cols), F32)
    for t in range(DIL):
        low = row_scr[t * pad : (t + 1) * pad, :]
        high = row_scr[(DIL + t) * pad : (DIL + t + 1) * pad, :]
        emit_outer(low, high, t, swap, outer)


def prepare_near(grad_ref, mask_ref, offset_ref, value_ref, tiles_ref, rows_ref, own_ref, core_ref, scr):
    rows, pad, cols = rows_ref.shape
    mask = mask_ref[...].astype(F32)
    to_rows(grad_ref, None, scr, pad)
    add_swath(scr, pad, rows, 0, offset_ref, value_ref, cols)
    for r in range(rows):
        rows_ref[r] = (scr[r * pad : (r + 1) * pad, :] * mask[r : r + 1, :]).astype(BF)
    full = tiles_ref.shape[0]
    count = (own_ref.shape[0] - full) // pad
    me = lax.axis_index("ch")
    for k, to in enumerate((own_ref, core_ref)):
        to[0:full, :] = tiles_ref[...]
        for r in range(count):
            at = full + r * pad
            to[at : at + pad, :] = rows_ref[(me ^ k) * count + r]


def relay(in_ref, out_ref):
    del in_ref, out_ref


def ring(count, step):
    return [(i, (i + step) % count) for i in range(count)]


def finish_columns(rows, swap, *refs):
    if swap:
        strip_ref, fold_ref, left_ref, right_ref, halo_ref, left_out, right_out = refs
        low_ref = high_ref = strip_ref
    else:
        low_ref, high_ref, fold_ref, left_ref, right_ref, halo_ref, left_out, right_out = refs
    lat, count = lax.axis_index("lat"), lax.axis_size("lat")
    left, right = left_ref[...].astype(F32), right_ref[...].astype(F32)
    for t in range(DIL):
        south = jnp.where(lat == 0, 0.0, low_ref[t].astype(F32))
        north = jnp.where(lat == count - 1, fold_ref[t].astype(F32), high_ref[t].astype(F32))
        halo_ref[t] = south.astype(BF)
        halo_ref[DIL + t] = north.astype(BF)
        left, right = pack_columns(south, t, left, right)
        left, right = pack_columns(north, rows + DIL + t, left, right)
    left_out[...] = left.astype(BF)
    right_out[...] = right.astype(BF)


def odd_lon():
    return lax.axis_index("lon") % 2 == 1


def pack_for_third(rows, riding, *refs):
    if riding:
        ride_ref, *refs = refs
    got_ref, fold_ref, left_ref, right_ref, out_ref = refs
    low = lax.axis_index("lat") == 0
    left, right = left_ref[...].astype(F32), right_ref[...].astype(F32)
    for t in range(DIL):
        got = got_ref[t].astype(F32)
        left, right = pack_columns(jnp.where(low, 0.0, got), t, left, right)
        left, right = pack_columns(jnp.where(low, got, 0.0), rows + DIL + t, left, right)
        out_ref[t] = fold_ref[t]
    pack = jnp.where(odd_lon(), right, left)
    if riding:
        pack = pack + pltpu.roll(ride_ref[...].astype(F32), RIDE, 1)
    out_ref[DIL] = pack.astype(BF)


def pack_for_first(rows, got_ref, fold_ref, left_ref, right_ref, third_ref, halo_ref, out_ref, side_ref):
    low = lax.axis_index("lat") == 0
    odd = odd_lon()
    left, right = left_ref[...].astype(F32), right_ref[...].astype(F32)
    side = third_ref[DIL].astype(F32)
    size = side.shape[1]
    lane = iota(side.shape, 1)
    for t in range(DIL):
        got = got_ref[t].astype(F32)
        south = jnp.where(low, 0.0, got)
        north = jnp.where(low, got, third_ref[t].astype(F32))
        halo_ref[t] = south.astype(BF)
        halo_ref[DIL + t] = north.astype(BF)
        left, right = pack_columns(south, t, left, right)
        left, right = pack_columns(north, rows + DIL + t, left, right)
        at = 2 * (rows + DIL + t)
        own = fold_ref[t].astype(F32)
        own = jnp.where(
            odd, pltpu.roll(own, at, 1), pltpu.roll(own, (at - (size - DIL)) % size, 1)
        )
        here = jnp.logical_and((lane == at) | (lane == at + 1), jnp.logical_not(low))
        side = jnp.where(here, own, side)
    out_ref[0] = jnp.where(odd, left, right).astype(BF)
    for k in range(1, out_ref.shape[0]):
        out_ref[k] = jnp.zeros(side.shape, BF)
    side_ref[...] = side.astype(BF)


def two_by_four():
    return lax.axis_size("lat") == 2 and lax.axis_size("lon") == 4


def exchange_halo(rows, strips, outer, swap, name, planes=1, riding=(), after=()):
    n_lat, n_lon = lax.axis_size("lat"), lax.axis_size("lon")
    fold, left, right = strips
    pad = left.shape[0]
    halo_shape, pack = shape((2 * DIL, pad, LANES), BF), shape((pad, LANES), BF)
    if two_by_four():
        got = lax.ppermute(outer[0], "lat", [(0, 1), (1, 0)])
        third_out = call(
            functools.partial(pack_for_third, rows, len(riding) > 0),
            [shape((DIL + 1, pad, LANES), BF)],
            [*riding, got, fold, left, right],
            (),
            name + "_third",
            after=after,
        )[0]
        third = lax.ppermute(third_out, "lon", [(lon, lon ^ 3) for lon in range(n_lon)])
        halo, first, side = call(
            functools.partial(pack_for_first, rows),
            [halo_shape, shape((planes, pad, LANES), BF), pack],
            [got, fold, left, right, third],
            (),
            name + "_first",
        )
        got = lax.ppermute(first, "lon", [(lon, lon ^ 1) for lon in range(n_lon)])
        return (halo, got, side), (third_out, third, first)
    top = n_lat - 1
    fold_pairs = [(lon * n_lat + top, (n_lon - 1 - lon) * n_lat + top) for lon in range(n_lon)]
    if swap:
        moved = [lax.ppermute(outer[0], "lat", [(0, 1), (1, 0)])]
    else:
        moved = [
            lax.ppermute(outer[1], "lat", [(i, i + 1) for i in range(n_lat - 1)]),
            lax.ppermute(outer[0], "lat", [(i + 1, i) for i in range(n_lat - 1)]),
        ]
    fold = lax.ppermute(fold, ("lon", "lat"), fold_pairs)
    halo, left, right = call(
        functools.partial(finish_columns, rows, swap),
        [halo_shape, pack, pack],
        [*moved, fold, left, right],
        (),
        name + "_columns",
    )
    from_right = lax.ppermute(left, "lon", ring(n_lon, -1))
    from_left = lax.ppermute(right, "lon", ring(n_lon, 1))
    return (halo, from_left, from_right), ()


def shifted_rows(block_ref, halo_ref, left_ref, right_ref, group):
    rows = block_ref.shape[0]
    at = pl.ds(aligned(group * 16), 16)
    lane = iota((16, LANES), 1)
    left = left_ref[(0, at) if two_by_four() else at].astype(F32)
    right = right_ref[at, :].astype(F32)
    if two_by_four():
        odd = odd_lon()
        left, right = jnp.where(odd, left, right), jnp.where(odd, right, left)
    for e in range(rows + 2 * DIL):
        if e < DIL:
            row = halo_ref[e, at, :]
        elif e < rows + DIL:
            row = block_ref[e - DIL, at, :]
        else:
            row = halo_ref[e - rows, at, :]
        row = row.astype(F32)
        west = jnp.where(
            lane < DIL, pltpu.roll(left, (-2 * e) % LANES, 1), pltpu.roll(row, DIL, 1)
        )
        east = jnp.where(
            lane >= LANES - DIL,
            pltpu.roll(right, (LANES - DIL - 2 * e) % LANES, 1),
            pltpu.roll(row, LANES - DIL, 1),
        )
        yield e, (west, row, east)


def stencil(block_ref, halo_ref, left_ref, right_ref, group, taps, north, emit):
    rows = block_ref.shape[0]
    sums = {}
    for e, shifts in shifted_rows(block_ref, halo_ref, left_ref, right_ref, group):
        for a in (2, 1, 0):
            r = e - DIL * a
            if not 0 <= r < rows:
                continue
            used = north if e >= rows + DIL else taps[a]
            term = used[0] * shifts[0] + used[1] * shifts[1] + used[2] * shifts[2]
            sums[r] = term if r not in sums else sums[r] + term
            if a == 2:
                emit(r, sums.pop(r))


def spread(tap_ref, group):
    values = tap_ref[pl.ds(aligned(group * 16), 16), :]
    return [
        [jnp.broadcast_to(values[:, 3 * a + b : 3 * a + b + 1], (16, LANES)) for b in range(3)]
        for a in range(3)
    ]


def conv_forward(ones_row, block_ref, halo_ref, left_ref, right_ref, tap_ref, *rest):
    quarters, scr = rest[:-1], rest[-1]
    pad = block_ref.shape[1]

    def body(group, carry):
        taps = spread(tap_ref, group)
        is_one = iota((16, LANES), 0) + group * 16 == ones_row

        def emit(r, value):
            value = jnp.where(is_one, 1.0, value)
            scr[r, pl.ds(aligned(group * 16), 16), :] = value.astype(BF)

        stencil(block_ref, halo_ref, left_ref, right_ref, group, taps, taps[2], emit)
        return carry

    lax.fori_loop(0, pad // 16, body, 0)
    me = lax.axis_index("ch")
    count = quarters[0].shape[0]
    for k, quarter in enumerate(quarters):
        quarter[...] = scr[pl.ds((me ^ k) * count, count)]


def conv_adjoint(
    block_ref, halo_ref, left_ref, right_ref, tap_ref, cotan_ref, mask_ref, out_ref, mark_ref, scr
):
    rows, pad = block_ref.shape[:2]
    at_top = lax.axis_index("lat") == lax.axis_size("lat") - 1
    mask = mask_ref[...].astype(F32)

    def body(group, carry):
        taps = spread(tap_ref, group)
        back = [[taps[2 - a][2 - b] for b in range(3)] for a in range(3)]
        north = [jnp.where(at_top, taps[2][b], back[2][b]) for b in range(3)]

        def emit(r, value):
            cotan = cotan_ref[r, pl.ds(aligned(group * 16), 16), :].astype(F32)
            scr[pl.ds(pl.multiple_of(r * pad + group * 16, 16), 16), :] = (cotan + value) * mask[
                r : r + 1, :
            ]

        stencil(block_ref, halo_ref, left_ref, right_ref, group, back, north, emit)
        return carry

    lax.fori_loop(0, pad // 16, body, 0)

    def write(c, carry):
        out_ref[c] = scr[pl.ds(c, rows, stride=pad), :].astype(BF)
        return carry

    channels = out_ref.shape[0]
    lax.fori_loop(0, channels, write, 0, unroll=5 if channels % 5 == 0 else 1)
    mark_ref[...] = jnp.zeros(mark_ref.shape, F32)


def collect_grad(swap, own, near, far, passed, rows_ref, *rest):
    part_rows = own.shape[0]
    rows, pad = rows_ref.shape[:2]
    me = lax.axis_index("ch")
    for k, quarter in enumerate((own, near, far.at[0], passed.at[1])):
        rows_ref[pl.ds((me ^ k) * part_rows, part_rows)] = quarter[...]
    strips, outer = rest[:3], rest[3:]
    for t in range(DIL):
        emit_outer(rows_ref[t].astype(F32), rows_ref[rows - DIL + t].astype(F32), t, swap, outer)
    emit_strips(lambda r: rows_ref[r], rows, pad, *strips)


def kernel_gradient(grad_ref, block_ref, halo_ref, left_ref, right_ref, out_ref):
    rows, pad = grad_ref.shape[:2]

    def body(group, carry):
        at = pl.ds(aligned(group * 16), 16)
        sums = [[jnp.zeros((16, LANES), F32) for _ in range(3)] for _ in range(3)]
        for e, shifts in shifted_rows(block_ref, halo_ref, left_ref, right_ref, group):
            for a in range(3):
                r = e - DIL * a
                if 0 <= r < rows:
                    grad = grad_ref[r, at, :].astype(F32)
                    for b in range(3):
                        sums[a][b] = sums[a][b] + grad * shifts[b]
        lane = iota((16, LANES), 1)
        out = jnp.zeros((16, LANES), F32)
        for a in range(3):
            for b in range(3):
                total = jnp.sum(sums[a][b], axis=1, keepdims=True)
                out = jnp.where(lane == 3 * a + b, total, out)
        out_ref[at, :] = out.astype(BF)
        return carry

    lax.fori_loop(0, pad // 16, body, 0)


def channel_of(slot, part, pad):
    block = sum((slot >= pad * b).astype(jnp.int32) for b in range(1, 4))
    inside = slot - block * pad
    return jnp.where((slot >= 0) & (slot < 4 * pad) & (inside < part), block * part + inside, -1)


def expand_slot(lane, pad):
    return jnp.where(lane < 4 * pad, lane, -1)


def project_slot(lane, pad, split):
    tail = 4 * pad - split
    low = LANES - tail
    return jnp.where(lane >= LANES, lane - LANES, jnp.where(lane >= low, lane - low + split, -1))


def pack_weights(part, pad, expand_ref, bias_ref, project_ref, kernel_ref, out_ref, taps_ref, turn_scr):
    hidden, channels = expand_ref.shape
    turn_scr[...] = jnp.zeros(turn_scr.shape, F32)
    for a in range(3):
        turn_scr[3 * a : 3 * a + 3, 0:part] = kernel_ref[a]
    taps_ref[...] = jnp.transpose(turn_scr[...])[0:pad, :]
    wide = out_ref.shape[1]
    split = 4 * pad // LANES * LANES
    lane = iota((channels, wide), 1)
    row = iota((channels, wide), 0)
    pick_e = (channel_of(expand_slot(lane, pad), part, pad) == row).astype(BF)
    slot = jnp.where(lane >= split, project_slot(lane - split, pad, split), -1)
    pick_p = (channel_of(slot, part, pad) == row).astype(BF)
    bias = bias_ref[...]
    parts = jnp.zeros((16, hidden), F32)
    at = iota((16, hidden), 0)
    for k in range(3):
        piece = bias.astype(BF).astype(F32)
        bias = bias - piece
        parts = jnp.where(at == k, piece, parts)
    lane, row = iota((16, wide), 1), iota((16, wide), 0)
    pick_b = ((lane == row * pad + part) & (row < 3)).astype(BF)
    turned = (((0,), (0,)), ((), ()))
    packed = (
        jnp.dot(expand_ref[...], pick_e, preferred_element_type=F32)
        + lax.dot_general(parts.astype(BF), pick_b, turned, preferred_element_type=F32)
        + jnp.dot(project_ref[...], pick_p, preferred_element_type=F32)
    )
    rows = out_ref.shape[0]
    out_ref[0:hidden, :] = packed.astype(BF)
    out_ref[hidden:rows, :] = jnp.zeros((rows - hidden, wide), BF)


GELU_C = math.sqrt(2.0 / math.pi)


def activation_gradient(*refs):
    parts = refs[0:4]
    act_ref, y_scr, w_scr, t_scr = refs[4:]
    me = lax.axis_index("ch")
    tiles = w_scr.shape[1] // LANES
    hid = w_scr.shape[0] // 4
    depth, cells = y_scr.shape
    part_rows = cells // LANES
    pad = (parts[0].shape[0] - tiles * hid) // part_rows
    split = 4 * pad // LANES * LANES
    y_scr[0 : depth - 4 * pad, :] = jnp.zeros((depth - 4 * pad, cells), BF)
    for k, ref in enumerate(parts):
        for t in range(tiles):
            w_scr[k * hid : (k + 1) * hid, t * LANES : (t + 1) * LANES] = ref[
                t * hid : (t + 1) * hid, :
            ]
        block = me ^ k
        start = tiles * hid + (part_rows * pad if k == 3 else 0)
        for r in range(part_rows):
            cols = slice(r * LANES, (r + 1) * LANES)
            for u in range(pad // 16):
                slot = block * pad + 16 * u
                to = jnp.where(slot < split, slot + LANES, slot - split + depth - 4 * pad)
                at = start + r * pad + 16 * u
                y_scr[pl.ds(aligned(to), 16), cols] = ref[at : at + 16, :]
    t_scr[...] = jnp.transpose(w_scr[:, 0:depth])
    step = 256
    for start in range(0, cells, step):
        cols = slice(start, start + step)
        act_ref[:, cols] = jnp.dot(
            w_scr[:, split : split + depth], y_scr[:, cols], preferred_element_type=F32
        )


def hidden_gradient(*refs):
    xs, (act_ref, y_ref, w_ref) = refs[0:4], refs[4:7]
    pre_ref, keep_ref, send_ref, x_scr, value_scr = refs[7:]
    part_rows, pad = xs[0].shape[:2]
    hid = w_ref.shape[0] // 4
    split = 4 * pad // LANES * LANES
    depth, cells = x_scr.shape
    me = lax.axis_index("ch")
    x_scr[4 * pad : depth, :] = jnp.zeros((depth - 4 * pad, cells), BF)
    for k in range(4):
        for r in range(part_rows):
            x_scr[pl.ds(aligned((me ^ k) * pad), pad), r * LANES : (r + 1) * LANES] = xs[k][r]
    step = 256
    for start in range(0, cells, step):
        cols = slice(start, start + step)
        hidden = jnp.dot(w_ref[:, 0:depth], x_scr[:, cols], preferred_element_type=F32)
        square = hidden * hidden
        tanh = jnp.tanh(GELU_C * hidden * (1.0 + 0.044715 * square))
        half = 0.5 * (1.0 + tanh)
        slope = half + (0.5 * GELU_C) * hidden * (1.0 - tanh * tanh) * (
            1.0 + (3 * 0.044715) * square
        )
        value_scr[:, cols] = (hidden * half).astype(BF)
        pre_ref[:, cols] = (act_ref[:, cols] * slope).astype(BF)
    over_cells = (((1,), (1,)), ((), ()))
    expand = lax.dot_general(pre_ref[...], x_scr[...], over_cells, preferred_element_type=F32)
    project = lax.dot_general(value_scr[...], y_ref[...], over_cells, preferred_element_type=F32)
    shared = split // LANES
    tiles = [expand[:, t * LANES : (t + 1) * LANES] for t in range(shared)]
    tiles.append(expand[:, split : split + LANES] + project[:, 0:LANES])
    tiles += [project[:, t * LANES : (t + 1) * LANES] for t in range(1, shared + 1)]
    for k in range(4):
        to = send_ref if k % 2 else keep_ref
        for t, tile in enumerate(tiles):
            to[k // 2, t * hid : (t + 1) * hid, :] = tile[k * hid : (k + 1) * hid].astype(to.dtype)


def conv_gradient(pre_ref, t_ref, *rest):
    (own_ref, core_ref, far_ref), scr = rest[:-1], rest[-1]
    outs = (own_ref, core_ref, far_ref.at[0], far_ref.at[1])
    part_rows, pad = own_ref.shape[:2]
    me = lax.axis_index("ch")
    step = 256
    for start in range(0, pre_ref.shape[1], step):
        cols = slice(start, start + step)
        scr[:, cols] = jnp.dot(t_ref[...], pre_ref[:, cols], preferred_element_type=F32).astype(BF)
    for k, to in enumerate(outs):
        for r in range(part_rows):
            to[r] = scr[pl.ds(aligned((me ^ k) * pad), pad), r * LANES : (r + 1) * LANES]


def add_cores(keep_ref, got_ref, own_ref, *sends):
    piece = own_ref.shape[1]
    step = piece - 32
    place = 2 * lax.axis_index("lat") + lax.axis_index("lon") % 2
    for k in range(4):
        at = pl.ds(pl.multiple_of((place ^ k) * step, 32), piece)
        for group in range(2):
            total = keep_ref[group, at, :] + got_ref[group, at, :].astype(F32)
            to = sends[k - 1] if k else own_ref
            to[group] = total.astype(to.dtype)


def add_pieces(own_ref, a_ref, b_ref, c_ref, mine_ref, other_ref):
    for group, to in enumerate((mine_ref, other_ref)):
        total = own_ref[group] + (
            a_ref[group].astype(F32) + b_ref[group].astype(F32) + c_ref[group].astype(F32)
        )
        to[...] = total.astype(to.dtype)


def add_across(mine_ref, got_ref, out_ref):
    out_ref[...] = (mine_ref[...] + got_ref[...].astype(F32)).astype(BF)


def finish_pieces(mine_ref, line_ref, kernel_ref, third_ref, out_ref, turn_scr):
    piece, pad = mine_ref.shape[0], kernel_ref.shape[0]
    out_ref[0:piece, :] = (mine_ref[...].astype(F32) + line_ref[...].astype(F32)).astype(BF)
    other = pltpu.roll(third_ref[DIL].astype(F32), LANES - RIDE, 1)
    turn_scr[...] = jnp.zeros(turn_scr.shape, F32)
    turn_scr[0:pad, :] = kernel_ref[...].astype(F32) + other
    out_ref[piece:, :] = jnp.transpose(turn_scr[...])[0:TAP_ROWS, :].astype(BF)


def write_parameters(part, pad, scale, hid, p0, p1, p2, p3, *rest):
    expand_ref, project_ref, bias_ref, taps_ref, all_scr, taps_scr = rest
    piece = p0.shape[0] - TAP_ROWS
    step = piece - 32
    place = 2 * lax.axis_index("lat") + lax.axis_index("lon") % 2
    for k, ref in enumerate((p0, p1, p2, p3)):
        to = place ^ k
        all_scr[pl.ds(pl.multiple_of(to * step, 32), step), :] = ref[0:step, :]

        @pl.when(to == 3)
        def _():
            all_scr[4 * step : 4 * step + 32, :] = ref[step:piece, :]

        taps_scr[pl.ds(aligned(to * TAP_ROWS), TAP_ROWS), :] = ref[piece:, :].astype(F32)
    unpack(part, pad, scale, hid, all_scr, expand_ref, project_ref, bias_ref)
    total = taps_scr[0:TAP_ROWS, :]
    for k in range(1, 4):
        total = total + taps_scr[k * TAP_ROWS : (k + 1) * TAP_ROWS, :]
    write_taps(total, scale, taps_ref)


def write_taps(total, scale, taps_ref):
    for a in range(3):
        taps_ref[a] = total[3 * a : 3 * a + 3, 0 : taps_ref.shape[2]] * scale


def unpack(part, pad, scale, hid, all_ref, expand_ref, project_ref, bias_ref):
    hidden, channels = expand_ref.shape
    split = 4 * pad // LANES * LANES
    shared = split // LANES
    tiles = [all_ref[t * hid : (t + 1) * hid, :] for t in range(2 * shared + 1)]
    depth = (shared + 1) * LANES
    expand = jnp.concatenate(tiles[: shared + 1], axis=1)
    project = jnp.concatenate(tiles[shared:], axis=1)
    lane, row = iota((channels, depth), 1), iota((channels, depth), 0)
    pick_e = (channel_of(expand_slot(lane, pad), part, pad) == row).astype(BF)
    pick_p = (channel_of(project_slot(lane, pad, split), part, pad) == row).astype(BF)
    pick_b = (iota((16, depth), 1) == part).astype(BF)
    last = (((1,), (1,)), ((), ()))
    dot = functools.partial(lax.dot_general, dimension_numbers=last, preferred_element_type=F32)
    expand_ref[...] = dot(expand, pick_e)[0:hidden, :] * scale
    bias_ref[...] = dot(pick_b, expand)[0:1, 0:hidden] * scale
    project_ref[...] = dot(project, pick_p)[0:hidden, :] * scale


def unpack_whole(part, pad, scale, hid, all_ref, taps_in, expand_ref, project_ref, bias_ref, taps_ref, turn_scr):
    unpack(part, pad, scale, hid, all_ref, expand_ref, project_ref, bias_ref)
    turn_scr[...] = jnp.zeros(turn_scr.shape, F32)
    turn_scr[0:pad, :] = taps_in[...]
    write_taps(jnp.transpose(turn_scr[...])[0:TAP_ROWS, :], scale, taps_ref)


def on_device(
    ocean_state,
    land_mask,
    out_grad,
    swath_offset,
    swath_value,
    depth_kernel,
    expand_weight,
    expand_bias,
    project_weight,
):
    part, rows, cols = ocean_state.shape
    n_lon, n_lat, n_ch = lax.axis_size("lon"), lax.axis_size("lat"), lax.axis_size("ch")
    channels, hidden = expand_weight.shape
    assert n_ch == 4 and cols == LANES and rows % n_ch == 0
    pad = (part + 16) // 16 * 16
    hid = (hidden + 15) // 16 * 16
    split = n_ch * pad // LANES * LANES
    tail = n_ch * pad - split
    assert tail == LANES // 2
    wide = 2 * n_ch * pad
    depth = split + LANES
    part_rows = rows // n_ch
    cells = part_rows * cols
    swap = n_lat == 2
    scale = 1.0 / math.sqrt(rows * n_lat * cols * n_lon)
    core = [(i, i ^ 1) for i in range(n_ch)]
    across = [(i, i ^ 2) for i in range(n_ch)]
    block = shape((rows, pad, cols), BF)
    quarter = shape((part_rows, pad, cols), BF)
    flat = pltpu.VMEM((rows * pad, cols), F32)

    turn = pltpu.VMEM((LANES, LANES), F32)

    def spread_parts(parts):
        return [parts[0]] + [
            lax.ppermute(parts[k], "ch", [(i, i ^ k) for i in range(n_ch)]) for k in (3, 2, 1)
        ][::-1]

    tile_rows = wide // LANES * hid
    near_rows, far_rows = tile_rows + part_rows * pad, tile_rows + 2 * part_rows * pad
    prepared = [
        out_grad,
        land_mask,
        swath_offset.reshape(1, -1),
        swath_value.reshape(1, -1),
        expand_weight.T,
        expand_bias.reshape(1, hidden),
        project_weight,
        depth_kernel,
        ocean_state,
    ]
    count = len(prepared)
    to_far, tiles, taps, *rest = call(
        functools.partial(prepare_far, part, swap, count),
        [shape((far_rows, LANES), BF), shape((tile_rows, LANES), BF), shape((pad, LANES), F32)]
        + outer_shapes(pad, swap)
        + [shape(a.shape, a.dtype) for a in prepared],
        prepared,
        [
            pltpu.VMEM((rows // 2 * pad, cols), F32),
            pltpu.VMEM((2 * DIL * pad, cols), F32),
            pltpu.VMEM((hid, wide), BF),
            turn,
            pltpu.SemaphoreType.DMA((count,)),
        ],
        "far_rows",
        far=True,
    )
    outer, held = rest[:-count], rest[-count:]
    land_mask, ocean_state = held[1], held[8]
    masked, *strips = call(
        prepare_state,
        [block] + strip_shapes(pad),
        [ocean_state, land_mask],
        [flat],
        "state_rows",
    )
    cotan, own, to_core = call(
        prepare_near,
        [block, shape((near_rows, LANES), BF), shape((near_rows, LANES), BF)],
        [*held[0:4], tiles],
        [flat],
        "cotan_rows",
        after=[masked],
    )
    around, _ = exchange_halo(rows, strips, outer, swap, "state", after=[to_core])
    from_far = lax.ppermute(to_far, "ch", across)
    conv_parts = call(
        functools.partial(conv_forward, part),
        [quarter] * 4,
        [masked, *around, taps],
        [pltpu.VMEM((rows, pad, cols), BF)],
        "conv_forward",
    )
    all_conv = spread_parts(conv_parts)
    from_far = call(
        relay, [from_far], [from_far], (), "cotan_relay", aliases={0: 0}, after=conv_parts[:1]
    )[0]
    passed = lax.ppermute(from_far, "ch", core)
    act_grad, cotan_all, weights_all, weights_turned = call(
        activation_gradient,
        [
            shape((n_ch * hid, cells), F32),
            shape((depth, cells), BF),
            shape((n_ch * hid, wide), BF),
            shape((depth, n_ch * hid), BF),
        ],
        [own, lax.ppermute(to_core, "ch", core), from_far, passed],
        (),
        "activation_gradient",
    )
    pre_grad, keep, send = call(
        hidden_gradient,
        [
            shape((n_ch * hid, cells), BF),
            shape((2, tile_rows, LANES), F32),
            shape((2, tile_rows, LANES), BF),
        ],
        [*all_conv, act_grad, cotan_all, weights_all],
        [pltpu.VMEM((depth, cells), BF), pltpu.VMEM((n_ch * hid, cells), BF)],
        "hidden_gradient",
    )
    got = lax.ppermute(send, "ch", core)
    grad_own, grad_core, grad_far = call(
        conv_gradient,
        [quarter, quarter, shape((2, part_rows, pad, cols), BF)],
        [pre_grad, weights_turned],
        [pltpu.VMEM((depth, cells), BF)],
        "conv_gradient",
    )
    grad_near = lax.ppermute(grad_core, "ch", core)
    grad_far = lax.ppermute(grad_far, "ch", across)
    staged = two_by_four() and tile_rows % 32 == 0
    if staged:
        step = (tile_rows - 32) // 128 * 32
        piece = step + 32
        assert 3 * step + piece == tile_rows
        mine, *sends = call(
            add_cores,
            [shape((2, piece, LANES), F32)] + [shape((2, piece, LANES), BF)] * 3,
            [keep, got],
            (),
            "add_cores",
        )

        def turn_plane(k):
            pairs = []
            for lon in range(n_lon):
                for lat in range(n_lat):
                    pairs.append((lon * n_lat + lat, (lon ^ (k & 1)) * n_lat + (lat ^ (k >> 1))))
            return pairs

        def over_plane(values):
            return [lax.ppermute(values[k - 1], ("lon", "lat"), turn_plane(k)) for k in (1, 2, 3)]

        mine, other = call(
            add_pieces,
            [shape((piece, LANES), F32), shape((piece, LANES), BF)],
            [mine, *over_plane(sends)],
            (),
            "add_pieces",
        )
        grad_far = call(
            relay, [grad_far], [grad_far], (), "grad_relay", aliases={0: 0}, after=[other]
        )[0]
    conv_grad, *grad_strips = call(
        functools.partial(collect_grad, swap),
        [block] + strip_shapes(pad) + outer_shapes(pad, swap),
        [grad_own, grad_near, grad_far, lax.ppermute(grad_far, "ch", core)],
        (),
        "grad_rows",
    )
    kernel_part = call(
        kernel_gradient,
        [shape((pad, LANES), BF)],
        [conv_grad, masked, *around],
        (),
        "kernel_gradient",
    )[0]
    grad_around, marks = exchange_halo(rows, grad_strips[:3], grad_strips[3:], swap, "grad", planes=4, riding=[kernel_part])
    if staged:
        mine = call(
            add_across,
            [shape((piece, LANES), BF)],
            [mine, lax.ppermute(other, "ch", across)],
            (),
            "add_across",
        )[0]
    state_grad, mark = call(
        conv_adjoint,
        [shape((part, rows, cols), BF), shape((8, LANES), F32)],
        [conv_grad, *grad_around, taps, cotan, land_mask],
        [flat],
        "conv_adjoint",
    )
    outs = [
        shape((hidden, channels), F32),
        shape((hidden, channels), F32),
        shape((1, hidden), F32),
        shape((3, 3, part), F32),
    ]
    if staged:
        far_lon = [(lon, lon ^ 2) for lon in range(n_lon)]
        summed = call(
            finish_pieces,
            [shape((piece + TAP_ROWS, LANES), BF)],
            [
                mine,
                lax.ppermute(mine, "lon", far_lon),
                kernel_part,
                marks[1],
            ],
            [turn],
            "finish_pieces",
            after=marks[2:],
        )[0]
        expand_grad, project_grad, bias_grad, kernel_grad = call(
            functools.partial(write_parameters, part, pad, scale, hid),
            outs,
            [summed, *over_plane([summed] * 3)],
            [pltpu.VMEM((tile_rows, LANES), BF), pltpu.VMEM((4 * TAP_ROWS, LANES), F32)],
            "write_parameters",
            after=[mark],
        )
    else:
        total = keep + got.astype(F32)
        total = total[0] + lax.ppermute(total[1].astype(BF), "ch", across).astype(F32)
        total, kernel_sum = lax.psum((total, kernel_part.astype(F32)), ("lon", "lat"))
        expand_grad, project_grad, bias_grad, kernel_grad = call(
            functools.partial(unpack_whole, part, pad, scale, hid),
            outs,
            [total.astype(BF), kernel_sum],
            [turn],
            "write_parameters",
        )
    return (
        state_grad,
        expand_grad.T,
        project_grad,
        bias_grad.reshape(hidden),
        kernel_grad,
    )


def solution(mesh):
    return jax.shard_map(
        on_device,
        mesh=mesh,
        in_specs=(
            P("ch", "lat", "lon"),
            P("lat", "lon"),
            P("ch", "lat", "lon"),
            P("lat", "lon", None),
            P("lat", "lon", None),
            P(None, None, "ch"),
            P(None, "ch"),
            P("ch"),
            P("ch", None),
        ),
        out_specs=(
            P("ch", "lat", "lon"),
            P(None, "ch"),
            P("ch", None),
            P("ch"),
            P(None, None, "ch"),
        ),
        check_vma=False,
    )
```

```python
import functools
import math

import jax
import jax.numpy as jnp
from jax import lax
from jax.experimental import pallas as pl
from jax.experimental.pallas import tpu as pltpu
from jax.sharding import PartitionSpec as P

DIL = 2
LANES = 128
TAP_ROWS = 16
RIDE = 96
BF = jnp.bfloat16
F32 = jnp.float32


def shape(dims, kind):
    return jax.ShapeDtypeStruct(dims, kind)


def call(kernel, outs, args, scratch=(), name=None, flops=0, aliases=None, far=False, after=(), writes=0):
    count = len(args)
    if after:
        body, args = kernel, [*args, *after]

        def kernel(*refs):
            body(*refs[:count], *refs[len(args) :])

    if far:
        args = [pltpu.with_memory_space_constraint(a, pltpu.HBM) for a in args]
    spaces = [pltpu.HBM if far else pl.ANY if i >= count else pltpu.VMEM for i in range(len(args))]
    moved = sum(math.prod(a.shape) * a.dtype.itemsize for a in list(args) + list(outs))
    return pl.pallas_call(
        kernel,
        out_shape=tuple(outs),
        in_specs=[pl.BlockSpec(memory_space=space) for space in spaces],
        out_specs=tuple(
            pl.BlockSpec(memory_space=pl.ANY if i < writes else pltpu.VMEM) for i in range(len(outs))
        ),
        scratch_shapes=list(scratch),
        input_output_aliases=aliases or {},
        name=name,
        compiler_params=pltpu.CompilerParams(vmem_limit_bytes=24 * 1024 * 1024),
        cost_estimate=pl.CostEstimate(flops=flops, bytes_accessed=moved, transcendentals=0),
    )(*args)


def iota(dims, dim):
    return lax.broadcasted_iota(jnp.int32, dims, dim)


def aligned(index):
    return pl.multiple_of(index, 16)


def to_rows(block_ref, weight, scr, pad):
    channels, rows, cols = block_ref.shape

    def body(c, carry):
        value = block_ref[c].astype(F32)
        if weight is not None:
            value = value * weight
        scr[pl.ds(c, rows, stride=pad), :] = value
        return carry

    lax.fori_loop(0, channels, body, 0, unroll=5 if channels % 5 == 0 else 1)
    for c in range(channels, pad):
        scr[pl.ds(c, rows, stride=pad), :] = jnp.zeros((rows, cols), F32)


def pack_columns(value, ext_row, left, right):
    lane = iota(value.shape, 1)
    here = (lane == 2 * ext_row) | (lane == 2 * ext_row + 1)
    size = value.shape[1]
    left = jnp.where(here, pltpu.roll(value, (2 * ext_row) % size, 1), left)
    right = jnp.where(here, pltpu.roll(value, (2 * ext_row + 2) % size, 1), right)
    return left, right


def mirrored(value):
    size = value.shape[1]
    flip = (iota((size, size), 0) + iota((size, size), 1) == size - 1).astype(BF)
    return jnp.dot(value, flip, preferred_element_type=F32).astype(BF)


def emit_strips(read, rows, pad, fold_ref, left_ref, right_ref):
    for t in range(DIL):
        fold_ref[t] = mirrored(read(rows - 1 - t))
    left = jnp.zeros((pad, LANES), F32)
    right = jnp.zeros((pad, LANES), F32)
    for r in range(rows):
        left, right = pack_columns(read(r).astype(F32), r + DIL, left, right)
    left_ref[...] = left.astype(BF)
    right_ref[...] = right.astype(BF)


def strip_shapes(pad):
    return [shape((DIL, pad, LANES), BF)] + [shape((pad, LANES), BF)] * 2


def outer_shapes(pad, swap):
    return [shape((DIL, pad, LANES), BF)] * (1 if swap else 2)


def emit_outer(low, high, t, swap, outer):
    if swap:
        outer[0][t] = jnp.where(lax.axis_index("lat") == 0, high, low).astype(BF)
    else:
        outer[0][t] = low.astype(BF)
        outer[1][t] = high.astype(BF)


def prepare_state(state_ref, mask_ref, rows_ref, fold_ref, left_ref, right_ref, scr):
    rows, pad = rows_ref.shape[:2]
    to_rows(state_ref, mask_ref[...].astype(F32), scr, pad)
    for r in range(rows):
        rows_ref[r] = scr[r * pad : (r + 1) * pad, :].astype(BF)
    emit_strips(lambda r: rows_ref[r], rows, pad, fold_ref, left_ref, right_ref)


def add_swath(scr, stride, rows, start, offset_ref, value_ref, cols):
    offset = offset_ref[...]
    points = offset.shape[1]
    value = value_ref[...]
    total = jnp.zeros((rows, cols), F32)
    row_hot = iota((rows, points), 0) + start == lax.shift_right_logical(offset, LANES.bit_length() - 1)
    col_hot = (iota((cols, points), 0) == (offset & (LANES - 1))).astype(BF)
    for _ in range(3):
        part = value.astype(BF)
        value = value - part.astype(F32)
        lhs = jnp.where(row_hot, part.astype(F32), 0.0).astype(BF)
        total = total + lax.dot_general(
            lhs, col_hot, (((1,), (1,)), ((), ())), preferred_element_type=F32
        )
    total = jnp.where(lax.axis_index("ch") == 0, total, 0.0)
    first = scr[pl.ds(0, rows, stride=stride), :]
    scr[pl.ds(0, rows, stride=stride), :] = first + total


def prepare_outer(swap, count, *refs):
    outs, (row_scr, sems) = refs[count:-2], refs[-2:]
    outer, held = outs[:-count], outs[-count:]
    state_ref, mask_ref = held[0:2]
    copies = [pltpu.make_async_copy(refs[k], held[k], sems.at[k]) for k in range(count)]
    for copy in copies:
        copy.start()
    pad = outer[0].shape[1]
    channels, rows, cols = state_ref.shape
    half = rows // 2
    lat = lax.axis_index("lat")
    for c in range(channels, pad):
        row_scr[pl.ds(c, 2 * DIL, stride=pad), :] = jnp.zeros((2 * DIL, cols), F32)
    copies[1].wait()
    copies[0].wait()
    if swap:
        start = aligned((1 - lat) * half)
        mask = mask_ref[pl.ds(start, half), :].astype(F32)

        def body(c, carry):
            value = state_ref[c, pl.ds(start, half), :].astype(F32) * mask
            row_scr[pl.ds(c, DIL, stride=pad), :] = jnp.where(
                lat == 0, value[half - DIL :, :], value[0:DIL, :]
            )
            return carry

    else:
        mask = mask_ref[...].astype(F32)

        def body(c, carry):
            value = state_ref[c].astype(F32) * mask
            row_scr[pl.ds(c, DIL, stride=pad), :] = value[0:DIL, :]
            row_scr[pl.ds(DIL * pad + c, DIL, stride=pad), :] = value[rows - DIL :, :]
            return carry

    lax.fori_loop(0, channels, body, 0, unroll=5 if channels % 5 == 0 else 1)
    for k, to in enumerate(outer):
        for t in range(DIL):
            at = (k * DIL + t) * pad
            to[t] = row_scr[at : at + pad, :].astype(BF)
    for copy in copies[2:]:
        copy.wait()


def prepare_far(part, *refs):
    (mask_ref, grad_ref, offset_ref, value_ref), weights = refs[0:4], refs[4:8]
    far_ref, tiles_ref, taps_ref = refs[8:11]
    scr, weights_scr, turn_scr, pick_e, pick_p = refs[11:]
    channels, rows, cols = grad_ref.shape
    pad = taps_ref.shape[0]
    weight_picks(part, pad, weights_scr.shape[1], pick_e.shape[0], pick_e, pick_p)
    pack_weights(part, pad, *weights, pick_e, pick_p, weights_scr, taps_ref, turn_scr)
    hid = weights_scr.shape[0]
    full = tiles_ref.shape[0]
    for t in range(full // hid):
        tiles_ref[t * hid : (t + 1) * hid, :] = weights_scr[:, t * LANES : (t + 1) * LANES]
    far_ref[0:full, :] = tiles_ref[...]
    half = rows // 2
    me = lax.axis_index("ch")
    start = aligned((1 - me // 2) * half)

    def body(c, carry):
        scr[pl.ds(c, half, stride=pad), :] = grad_ref[c, pl.ds(start, half), :].astype(F32)
        return carry

    lax.fori_loop(0, channels, body, 0, unroll=5 if channels % 5 == 0 else 1)
    for c in range(channels, pad):
        scr[pl.ds(c, half, stride=pad), :] = jnp.zeros((half, cols), F32)
    add_swath(scr, pad, half, start, offset_ref, value_ref, cols)
    mask = mask_ref[pl.ds(start, half), :].astype(F32)
    count_rows = half // 2
    for r in range(half):
        scr[r * pad : (r + 1) * pad, :] = scr[r * pad : (r + 1) * pad, :] * mask[r : r + 1, :]
    for k in range(2):
        first = aligned((((me ^ (2 + k)) % 2) * count_rows) * pad)
        size = count_rows * pad
        far_ref[full + k * size : full + (k + 1) * size, :] = scr[pl.ds(first, size), :].astype(BF)


def prepare_near(mask_ref, grad_ref, offset_ref, value_ref, tiles_ref, rows_ref, own_ref, core_ref, scr):
    rows, pad, cols = rows_ref.shape
    mask = mask_ref[...].astype(F32)
    to_rows(grad_ref, None, scr, pad)
    add_swath(scr, pad, rows, 0, offset_ref, value_ref, cols)
    for r in range(rows):
        rows_ref[r] = (scr[r * pad : (r + 1) * pad, :] * mask[r : r + 1, :]).astype(BF)
    full = tiles_ref.shape[0]
    count = (own_ref.shape[0] - full) // pad
    me = lax.axis_index("ch")
    for k, to in enumerate((own_ref, core_ref)):
        to[0:full, :] = tiles_ref[...]
        for r in range(count):
            at = full + r * pad
            to[at : at + pad, :] = rows_ref[(me ^ k) * count + r]


def second_half(in_ref, out_ref):
    out_ref[...] = in_ref[1]


def relay(in_ref, out_ref):
    del in_ref, out_ref


def ring(count, step):
    return [(i, (i + step) % count) for i in range(count)]


def finish_columns(rows, swap, *refs):
    if swap:
        strip_ref, fold_ref, left_ref, right_ref, halo_ref, left_out, right_out = refs
        low_ref = high_ref = strip_ref
    else:
        low_ref, high_ref, fold_ref, left_ref, right_ref, halo_ref, left_out, right_out = refs
    lat, count = lax.axis_index("lat"), lax.axis_size("lat")
    left, right = left_ref[...].astype(F32), right_ref[...].astype(F32)
    for t in range(DIL):
        south = jnp.where(lat == 0, 0.0, low_ref[t].astype(F32))
        north = jnp.where(lat == count - 1, fold_ref[t].astype(F32), high_ref[t].astype(F32))
        halo_ref[t] = south.astype(BF)
        halo_ref[DIL + t] = north.astype(BF)
        left, right = pack_columns(south, t, left, right)
        left, right = pack_columns(north, rows + DIL + t, left, right)
    left_out[...] = left.astype(BF)
    right_out[...] = right.astype(BF)


def odd_lon():
    return lax.axis_index("lon") % 2 == 1


def pack_for_third(rows, riding, *refs):
    if riding:
        ride_ref, *refs = refs
    got_ref, fold_ref, left_ref, right_ref, out_ref = refs
    low = lax.axis_index("lat") == 0
    left, right = left_ref[...].astype(F32), right_ref[...].astype(F32)
    for t in range(DIL):
        got = got_ref[t].astype(F32)
        left, right = pack_columns(jnp.where(low, 0.0, got), t, left, right)
        left, right = pack_columns(jnp.where(low, got, 0.0), rows + DIL + t, left, right)
        out_ref[t] = fold_ref[t]
    pack = jnp.where(odd_lon(), right, left)
    if riding:
        pack = pack + pltpu.roll(ride_ref[...].astype(F32), RIDE, 1)
    out_ref[DIL] = pack.astype(BF)


def pack_for_first(rows, got_ref, fold_ref, left_ref, right_ref, third_ref, halo_ref, out_ref, side_ref):
    low = lax.axis_index("lat") == 0
    odd = odd_lon()
    left, right = left_ref[...].astype(F32), right_ref[...].astype(F32)
    side = third_ref[DIL].astype(F32)
    size = side.shape[1]
    lane = iota(side.shape, 1)
    for t in range(DIL):
        got = got_ref[t].astype(F32)
        south = jnp.where(low, 0.0, got)
        north = jnp.where(low, got, third_ref[t].astype(F32))
        halo_ref[t] = south.astype(BF)
        halo_ref[DIL + t] = north.astype(BF)
        left, right = pack_columns(south, t, left, right)
        left, right = pack_columns(north, rows + DIL + t, left, right)
        at = 2 * (rows + DIL + t)
        own = fold_ref[t].astype(F32)
        own = jnp.where(
            odd, pltpu.roll(own, at, 1), pltpu.roll(own, (at - (size - DIL)) % size, 1)
        )
        here = jnp.logical_and((lane == at) | (lane == at + 1), jnp.logical_not(low))
        side = jnp.where(here, own, side)
    out_ref[0] = jnp.where(odd, left, right).astype(BF)
    for k in range(1, out_ref.shape[0]):
        out_ref[k] = jnp.zeros(side.shape, BF)
    side_ref[...] = side.astype(BF)


def two_by_four():
    return lax.axis_size("lat") == 2 and lax.axis_size("lon") == 4


def exchange_halo(rows, strips, outer, swap, name, planes=1, riding=(), after=()):
    n_lat, n_lon = lax.axis_size("lat"), lax.axis_size("lon")
    fold, left, right = strips
    pad = left.shape[0]
    halo_shape, pack = shape((2 * DIL, pad, LANES), BF), shape((pad, LANES), BF)
    if two_by_four():
        got = lax.ppermute(outer[0], "lat", [(0, 1), (1, 0)])
        third_out = call(
            functools.partial(pack_for_third, rows, len(riding) > 0),
            [shape((DIL + 1, pad, LANES), BF)],
            [*riding, got, fold, left, right],
            (),
            name + "_third",
            after=after,
        )[0]
        third = lax.ppermute(third_out, "lon", [(lon, lon ^ 3) for lon in range(n_lon)])
        halo, first, side = call(
            functools.partial(pack_for_first, rows),
            [halo_shape, shape((planes, pad, LANES), BF), pack],
            [got, fold, left, right, third],
            (),
            name + "_first",
        )
        got = lax.ppermute(first, "lon", [(lon, lon ^ 1) for lon in range(n_lon)])
        return (halo, got, side), (third_out, third, first)
    top = n_lat - 1
    fold_pairs = [(lon * n_lat + top, (n_lon - 1 - lon) * n_lat + top) for lon in range(n_lon)]
    if swap:
        moved = [lax.ppermute(outer[0], "lat", [(0, 1), (1, 0)])]
    else:
        moved = [
            lax.ppermute(outer[1], "lat", [(i, i + 1) for i in range(n_lat - 1)]),
            lax.ppermute(outer[0], "lat", [(i + 1, i) for i in range(n_lat - 1)]),
        ]
    fold = lax.ppermute(fold, ("lon", "lat"), fold_pairs)
    halo, left, right = call(
        functools.partial(finish_columns, rows, swap),
        [halo_shape, pack, pack],
        [*moved, fold, left, right],
        (),
        name + "_columns",
    )
    from_right = lax.ppermute(left, "lon", ring(n_lon, -1))
    from_left = lax.ppermute(right, "lon", ring(n_lon, 1))
    return (halo, from_left, from_right), ()


def padded_row(block_ref, halo_ref, at, e):
    rows = block_ref.shape[0]
    if e < DIL:
        return halo_ref[e, at, :]
    if e < rows + DIL:
        return block_ref[e - DIL, at, :]
    return halo_ref[e - rows, at, :]


def sides(left_ref, right_ref, at):
    left = (left_ref[0, at, :] if two_by_four() else left_ref[at, :]).astype(F32)
    right = right_ref[at, :].astype(F32)
    if two_by_four():
        odd = odd_lon()
        left, right = jnp.where(odd, left, right), jnp.where(odd, right, left)
    return left, right


def shifted_rows(rows, read, left, right):
    lane = iota((16, LANES), 1)
    for e in range(rows + 2 * DIL):
        row = read(e).astype(F32)
        west = jnp.where(
            lane < DIL, pltpu.roll(left, (-2 * e) % LANES, 1), pltpu.roll(row, DIL, 1)
        )
        east = jnp.where(
            lane >= LANES - DIL,
            pltpu.roll(right, (LANES - DIL - 2 * e) % LANES, 1),
            pltpu.roll(row, LANES - DIL, 1),
        )
        yield e, (west, row, east)


def stencil_rows(rows, read, left, right, taps, north, emit):
    sums = {}
    for e, shifts in shifted_rows(rows, read, left, right):
        for a in (2, 1, 0):
            r = e - DIL * a
            if not 0 <= r < rows:
                continue
            used = north if e >= rows + DIL else taps[a]
            term = used[0] * shifts[0] + used[1] * shifts[1] + used[2] * shifts[2]
            sums[r] = term if r not in sums else sums[r] + term
            if a == 2:
                emit(r, sums.pop(r))


def stencil(block_ref, halo_ref, left_ref, right_ref, group, taps, north, emit):
    at = pl.ds(aligned(group * 16), 16)
    left, right = sides(left_ref, right_ref, at)
    read = functools.partial(padded_row, block_ref, halo_ref, at)
    stencil_rows(block_ref.shape[0], read, left, right, taps, north, emit)


def spread(tap_ref, group):
    values = tap_ref[pl.ds(aligned(group * 16), 16), :]
    return [
        [jnp.broadcast_to(values[:, 3 * a + b : 3 * a + b + 1], (16, LANES)) for b in range(3)]
        for a in range(3)
    ]


def conv_forward(ones_row, away, block_ref, halo_ref, left_ref, right_ref, tap_ref, *rest):
    same_ref, others, (row_scr, left_scr, right_scr, scr) = rest[0], rest[1:-4], rest[-4:]
    rows, pad = block_ref.shape[:2]
    half = rows // 2
    me = lax.axis_index("ch")
    upper = (me // 2 + away) % 2
    west, east = sides(left_ref, right_ref, slice(None))
    left_scr[...] = pltpu.roll(west, (LANES - 2 * half * upper) % LANES, 1)
    right_scr[...] = pltpu.roll(east, (LANES - 2 * half * upper) % LANES, 1)
    for t in range(DIL):
        low, high = halo_ref[t].astype(F32), halo_ref[DIL + t].astype(F32)
        before = block_ref[half - DIL + t].astype(F32)
        behind = block_ref[half + t].astype(F32)
        row_scr[t] = jnp.where(upper == 0, low, before).astype(BF)
        row_scr[half + DIL + t] = jnp.where(upper == 0, behind, high).astype(BF)
    for r in range(half):
        row_scr[DIL + r] = block_ref[upper * half + r]

    def body(group, carry):
        taps = spread(tap_ref, group)
        is_one = iota((16, LANES), 0) + group * 16 == ones_row
        at = pl.ds(aligned(group * 16), 16)

        def emit(r, value):
            value = jnp.where(is_one, 1.0, value)
            scr[r, at, :] = value.astype(BF)

        left, right = left_scr[at, :], right_scr[at, :]
        stencil_rows(half, lambda e: row_scr[e, at, :], left, right, taps, taps[2], emit)
        return carry

    lax.fori_loop(0, pad // 16, body, 0)
    count = half // 2
    same_ref[...] = scr[pl.ds((me % 2) * count, count)]
    other = (1 - me % 2) * count
    size = count // len(others)
    for k, to in enumerate(others):
        to[...] = scr[pl.ds(other + k * size, size)]


def conv_adjoint(
    block_ref, halo_ref, left_ref, right_ref, tap_ref, cotan_ref, mask_ref, out_ref, mark_ref, scr, done_scr, sems
):
    rows, pad = block_ref.shape[:2]
    channels = out_ref.shape[0]
    at_top = lax.axis_index("lat") == lax.axis_size("lat") - 1
    mask = mask_ref[...].astype(F32)

    def copy(group, count):
        at = pl.ds(group * 16, count)
        return pltpu.make_async_copy(done_scr.at[at], out_ref.at[at], sems.at[group])

    def body(group, count):
        taps = spread(tap_ref, group)
        back = [[taps[2 - a][2 - b] for b in range(3)] for a in range(3)]
        north = [jnp.where(at_top, taps[2][b], back[2][b]) for b in range(3)]

        def emit(r, value):
            cotan = cotan_ref[r, pl.ds(aligned(group * 16), 16), :].astype(F32)
            scr[pl.ds(r, 16, stride=rows + 8), :] = (cotan + value) * mask[r : r + 1, :]

        stencil(block_ref, halo_ref, left_ref, right_ref, group, back, north, emit)
        for c in range(count):
            at = c * (rows + 8)
            done_scr[group * 16 + c] = scr[at : at + rows, :].astype(BF)
        copy(group, count).start()

    whole = channels // 16

    def each(group, carry):
        body(group, 16)
        return carry

    lax.fori_loop(0, whole, each, 0)
    if channels % 16:
        body(whole, channels % 16)
    mark_ref[...] = jnp.zeros(mark_ref.shape, F32)
    for group in range(whole):
        copy(group, 16).wait()
    if channels % 16:
        copy(whole, channels % 16).wait()


def collect_grad(swap, own, near, far, passed, rows_ref, *rest):
    part_rows = own.shape[0]
    rows, pad = rows_ref.shape[:2]
    me = lax.axis_index("ch")
    for k, quarter in enumerate((own, near, far.at[0], passed)):
        rows_ref[pl.ds((me ^ k) * part_rows, part_rows)] = quarter[...]
    strips, outer = rest[:3], rest[3:]
    for t in range(DIL):
        emit_outer(rows_ref[t].astype(F32), rows_ref[rows - DIL + t].astype(F32), t, swap, outer)
    emit_strips(lambda r: rows_ref[r], rows, pad, *strips)


def shift_columns(block_ref, halo_ref, left_ref, right_ref, west_ref, east_ref):
    def body(group, carry):
        at = pl.ds(aligned(group * 16), 16)
        left, right = sides(left_ref, right_ref, at)
        read = functools.partial(padded_row, block_ref, halo_ref, at)
        for e, shifts in shifted_rows(block_ref.shape[0], read, left, right):
            west_ref[e, at, :] = shifts[0].astype(BF)
            east_ref[e, at, :] = shifts[2].astype(BF)
        return carry

    lax.fori_loop(0, block_ref.shape[1] // 16, body, 0)


def kernel_gradient(grad_ref, block_ref, halo_ref, west_ref, east_ref, out_ref):
    rows, pad = grad_ref.shape[:2]

    def body(group, carry):
        at = pl.ds(aligned(group * 16), 16)
        sums = [[jnp.zeros((16, LANES), F32) for _ in range(3)] for _ in range(3)]
        for e in range(rows + 2 * DIL):
            middle = padded_row(block_ref, halo_ref, at, e)
            shifts = [part.astype(F32) for part in (west_ref[e, at, :], middle, east_ref[e, at, :])]
            for a in range(3):
                r = e - DIL * a
                if 0 <= r < rows:
                    grad = grad_ref[r, at, :].astype(F32)
                    for b in range(3):
                        sums[a][b] = sums[a][b] + grad * shifts[b]
        lane = iota((16, LANES), 1)
        out = jnp.zeros((16, LANES), F32)
        for a in range(3):
            for b in range(3):
                total = jnp.sum(sums[a][b], axis=1, keepdims=True)
                out = jnp.where(lane == 3 * a + b, total, out)
        out_ref[at, :] = out.astype(BF)
        return carry

    lax.fori_loop(0, pad // 16, body, 0)


def channel_of(slot, part, pad):
    block = sum((slot >= pad * b).astype(jnp.int32) for b in range(1, 4))
    inside = slot - block * pad
    return jnp.where((slot >= 0) & (slot < 4 * pad) & (inside < part), block * part + inside, -1)


def expand_slot(lane, pad):
    return jnp.where(lane < 4 * pad, lane, -1)


def project_slot(lane, pad, split):
    tail = 4 * pad - split
    low = LANES - tail
    return jnp.where(lane >= LANES, lane - LANES, jnp.where(lane >= low, lane - low + split, -1))


def weight_picks(part, pad, wide, channels, pick_e_ref, pick_p_ref):
    split = 4 * pad // LANES * LANES
    lane = iota((channels, wide), 1)
    row = iota((channels, wide), 0)
    pick_e_ref[...] = (channel_of(expand_slot(lane, pad), part, pad) == row).astype(BF)
    slot = jnp.where(lane >= split, project_slot(lane - split, pad, split), -1)
    pick_p_ref[...] = (channel_of(slot, part, pad) == row).astype(BF)


def output_picks(part, pad, pick_e_ref, pick_p_ref):
    channels, depth = pick_e_ref.shape
    split = 4 * pad // LANES * LANES
    lane, row = iota((channels, depth), 1), iota((channels, depth), 0)
    pick_e_ref[...] = (channel_of(expand_slot(lane, pad), part, pad) == row).astype(BF)
    pick_p_ref[...] = (channel_of(project_slot(lane, pad, split), part, pad) == row).astype(BF)


def pack_weights(
    part, pad, expand_ref, bias_ref, project_ref, kernel_ref, pick_e_ref, pick_p_ref, out_ref, taps_ref, turn_scr
):
    hidden, channels = expand_ref.shape
    turn_scr[...] = jnp.zeros(turn_scr.shape, F32)
    for a in range(3):
        turn_scr[3 * a : 3 * a + 3, 0:part] = kernel_ref[a]
    taps_ref[...] = jnp.transpose(turn_scr[...])[0:pad, :]
    wide = out_ref.shape[1]
    bias = bias_ref[...]
    parts = jnp.zeros((16, hidden), F32)
    at = iota((16, hidden), 0)
    for k in range(3):
        piece = bias.astype(BF).astype(F32)
        bias = bias - piece
        parts = jnp.where(at == k, piece, parts)
    lane, row = iota((16, wide), 1), iota((16, wide), 0)
    pick_b = ((lane == row * pad + part) & (row < 3)).astype(BF)
    turned = (((0,), (0,)), ((), ()))
    packed = (
        jnp.dot(expand_ref[...], pick_e_ref[...], preferred_element_type=F32)
        + lax.dot_general(parts.astype(BF), pick_b, turned, preferred_element_type=F32)
        + jnp.dot(project_ref[...], pick_p_ref[...], preferred_element_type=F32)
    )
    rows = out_ref.shape[0]
    out_ref[0:hidden, :] = packed.astype(BF)
    out_ref[hidden:rows, :] = jnp.zeros((rows - hidden, wide), BF)


GELU_C = math.sqrt(2.0 / math.pi)


def activation_gradient(part, *refs):
    parts = refs[0:4]
    act_ref, y_scr, w_scr, t_scr, pick_e_ref, pick_p_ref = refs[4:]
    me = lax.axis_index("ch")
    tiles = w_scr.shape[1] // LANES
    hid = w_scr.shape[0] // 4
    depth, cells = y_scr.shape
    part_rows = cells // LANES
    pad = (parts[0].shape[0] - tiles * hid) // part_rows
    split = 4 * pad // LANES * LANES
    output_picks(part, pad, pick_e_ref, pick_p_ref)
    y_scr[0 : depth - 4 * pad, :] = jnp.zeros((depth - 4 * pad, cells), BF)
    for k, ref in enumerate(parts):
        for t in range(tiles):
            w_scr[k * hid : (k + 1) * hid, t * LANES : (t + 1) * LANES] = ref[
                t * hid : (t + 1) * hid, :
            ]
        block = me ^ k
        start = tiles * hid + (part_rows * pad if k == 3 else 0)
        for r in range(part_rows):
            cols = slice(r * LANES, (r + 1) * LANES)
            for u in range(pad // 16):
                slot = block * pad + 16 * u
                to = jnp.where(slot < split, slot + LANES, slot - split + depth - 4 * pad)
                at = start + r * pad + 16 * u
                y_scr[pl.ds(aligned(to), 16), cols] = ref[at : at + 16, :]
    t_scr[...] = jnp.transpose(w_scr[:, 0:depth])
    step = 256
    for start in range(0, cells, step):
        cols = slice(start, start + step)
        act_ref[:, cols] = jnp.dot(
            w_scr[:, split : split + depth], y_scr[:, cols], preferred_element_type=F32
        )


def hidden_gradient(*refs):
    xs, (act_ref, y_ref, w_ref) = refs[0:5], refs[5:8]
    pre_ref, keep_ref, send_ref, x_scr, value_scr = refs[8:]
    part_rows, pad = xs[0].shape[:2]
    hid = w_ref.shape[0] // 4
    split = 4 * pad // LANES * LANES
    depth, cells = x_scr.shape
    me = lax.axis_index("ch")
    x_scr[4 * pad : depth, :] = jnp.zeros((depth - 4 * pad, cells), BF)
    for k, ref, first in ((0, 0, 0), (1, 1, 0), (1, 2, part_rows // 2), (2, 3, 0), (3, 4, 0)):
        for r in range(xs[ref].shape[0]):
            cols = slice((first + r) * LANES, (first + r + 1) * LANES)
            x_scr[pl.ds(aligned((me ^ k) * pad), pad), cols] = xs[ref][r]
    step = 256
    for start in range(0, cells, step):
        cols = slice(start, start + step)
        hidden = jnp.dot(w_ref[:, 0:depth], x_scr[:, cols], preferred_element_type=F32)
        square = hidden * hidden
        tanh = jnp.tanh(hidden * (GELU_C + (0.044715 * GELU_C) * square))
        half = 0.5 + 0.5 * tanh
        slope = half + hidden * (0.5 * GELU_C + (1.5 * 0.044715 * GELU_C) * square) * (
            1.0 - tanh * tanh
        )
        value_scr[:, cols] = (hidden * half).astype(BF)
        pre_ref[:, cols] = (act_ref[:, cols] * slope).astype(BF)
    over_cells = (((1,), (1,)), ((), ()))
    expand = lax.dot_general(pre_ref[...], x_scr[...], over_cells, preferred_element_type=F32)
    project = lax.dot_general(value_scr[...], y_ref[...], over_cells, preferred_element_type=F32)
    shared = split // LANES
    tiles = [expand[:, t * LANES : (t + 1) * LANES] for t in range(shared)]
    tiles.append(expand[:, split : split + LANES] + project[:, 0:LANES])
    tiles += [project[:, t * LANES : (t + 1) * LANES] for t in range(1, shared + 1)]
    used = len(tiles) * hid
    for ref in (keep_ref, send_ref):
        for k in range(2):
            ref[k, used:, :] = jnp.zeros((ref.shape[1] - used, LANES), ref.dtype)
    for k in range(4):
        to = send_ref if k % 2 else keep_ref
        for t, tile in enumerate(tiles):
            to[k // 2, t * hid : (t + 1) * hid, :] = tile[k * hid : (k + 1) * hid].astype(to.dtype)


def conv_gradient(away, pre_ref, t_ref, *rest):
    outs, scr = rest[:-1], rest[-1]
    if away:
        outs = (rest[0].at[0], rest[0].at[1])
    part_rows, pad = outs[0].shape[:2]
    me = lax.axis_index("ch")
    first = ((me // 2 + away) % 2) * 2 * pad
    weights = t_ref[pl.ds(aligned(first), 2 * pad), :]
    step = 256
    for start in range(0, pre_ref.shape[1], step):
        cols = slice(start, start + step)
        scr[:, cols] = jnp.dot(weights, pre_ref[:, cols], preferred_element_type=F32).astype(BF)
    for k, to in enumerate(outs):
        at = pl.ds(aligned(((me + k) % 2) * pad), pad)
        for r in range(part_rows):
            to[r] = scr[at, r * LANES : (r + 1) * LANES]


def add_cores(keep_ref, got_ref, own_ref, *sends):
    piece = own_ref.shape[1]
    place = 2 * lax.axis_index("lat") + lax.axis_index("lon") % 2
    for k in range(4):
        at = pl.ds(aligned((place ^ k) * piece), piece)
        for group in range(2):
            total = keep_ref[group, at, :] + got_ref[group, at, :].astype(F32)
            to = sends[k - 1] if k else own_ref
            to[group] = total.astype(to.dtype)


def add_pieces(own_ref, a_ref, b_ref, c_ref, mine_ref, other_ref):
    for group, to in enumerate((mine_ref, other_ref)):
        total = own_ref[group] + (
            a_ref[group].astype(F32) + b_ref[group].astype(F32) + c_ref[group].astype(F32)
        )
        to[...] = total.astype(to.dtype)


def add_across(mine_ref, got_ref, out_ref):
    out_ref[...] = (mine_ref[...] + got_ref[...].astype(F32)).astype(BF)


def finish_pieces(mine_ref, line_ref, kernel_ref, third_ref, out_ref, turn_scr):
    piece, pad = mine_ref.shape[0], kernel_ref.shape[0]
    out_ref[0:piece, :] = (mine_ref[...].astype(F32) + line_ref[...].astype(F32)).astype(BF)
    other = pltpu.roll(third_ref[DIL].astype(F32), LANES - RIDE, 1)
    turn_scr[...] = jnp.zeros(turn_scr.shape, F32)
    turn_scr[0:pad, :] = kernel_ref[...].astype(F32) + other
    out_ref[piece:, :] = jnp.transpose(turn_scr[...])[0:TAP_ROWS, :].astype(BF)


def write_parameters(part, pad, scale, hid, p0, p1, p2, p3, pick_e, pick_p, *rest):
    expand_ref, project_ref, bias_ref, taps_ref, all_scr, taps_scr = rest
    piece = p0.shape[0] - TAP_ROWS
    place = 2 * lax.axis_index("lat") + lax.axis_index("lon") % 2
    for k, ref in enumerate((p0, p1, p2, p3)):
        to = place ^ k
        all_scr[pl.ds(aligned(to * piece), piece), :] = ref[0:piece, :]
        taps_scr[pl.ds(aligned(to * TAP_ROWS), TAP_ROWS), :] = ref[piece:, :].astype(F32)
    unpack(part, pad, scale, hid, all_scr, pick_e, pick_p, expand_ref, project_ref, bias_ref)
    total = taps_scr[0:TAP_ROWS, :]
    for k in range(1, 4):
        total = total + taps_scr[k * TAP_ROWS : (k + 1) * TAP_ROWS, :]
    write_taps(total, scale, taps_ref)


def write_taps(total, scale, taps_ref):
    for a in range(3):
        taps_ref[a] = total[3 * a : 3 * a + 3, 0 : taps_ref.shape[2]] * scale


def unpack(part, pad, scale, hid, all_ref, pick_e, pick_p, expand_ref, project_ref, bias_ref):
    hidden = expand_ref.shape[0]
    split = 4 * pad // LANES * LANES
    shared = split // LANES
    tiles = [all_ref[t * hid : (t + 1) * hid, :] for t in range(2 * shared + 1)]
    depth = (shared + 1) * LANES
    expand = jnp.concatenate(tiles[: shared + 1], axis=1)
    project = jnp.concatenate(tiles[shared:], axis=1)
    pick_b = (iota((16, depth), 1) == part).astype(BF)
    last = (((1,), (1,)), ((), ()))
    dot = functools.partial(lax.dot_general, dimension_numbers=last, preferred_element_type=F32)
    expand_ref[...] = dot(expand, pick_e[...])[0:hidden, :] * scale
    bias_ref[...] = dot(pick_b, expand)[0:1, 0:hidden] * scale
    project_ref[...] = dot(project, pick_p[...])[0:hidden, :] * scale


def unpack_whole(part, pad, scale, hid, all_ref, taps_in, pick_e, pick_p, *rest):
    expand_ref, project_ref, bias_ref, taps_ref, turn_scr = rest
    unpack(part, pad, scale, hid, all_ref, pick_e, pick_p, expand_ref, project_ref, bias_ref)
    turn_scr[...] = jnp.zeros(turn_scr.shape, F32)
    turn_scr[0:pad, :] = taps_in[...]
    write_taps(jnp.transpose(turn_scr[...])[0:TAP_ROWS, :], scale, taps_ref)


def on_device(
    ocean_state,
    land_mask,
    out_grad,
    swath_offset,
    swath_value,
    depth_kernel,
    expand_weight,
    expand_bias,
    project_weight,
):
    part, rows, cols = ocean_state.shape
    n_lon, n_lat, n_ch = lax.axis_size("lon"), lax.axis_size("lat"), lax.axis_size("ch")
    channels, hidden = expand_weight.shape
    assert n_ch == 4 and cols == LANES and rows % n_ch == 0
    pad = (part + 16) // 16 * 16
    hid = (hidden + 15) // 16 * 16
    split = n_ch * pad // LANES * LANES
    tail = n_ch * pad - split
    assert tail == LANES // 2
    wide = 2 * n_ch * pad
    depth = split + LANES
    part_rows = rows // n_ch
    cells = part_rows * cols
    swap = n_lat == 2
    scale = 1.0 / math.sqrt(rows * n_lat * cols * n_lon)
    core = [(i, i ^ 1) for i in range(n_ch)]
    across = [(i, i ^ 2) for i in range(n_ch)]
    block = shape((rows, pad, cols), BF)
    quarter = shape((part_rows, pad, cols), BF)
    flat = pltpu.VMEM((rows * pad, cols), F32)

    turn = pltpu.VMEM((LANES, LANES), F32)

    tile_rows = wide // LANES * hid
    sum_rows = (tile_rows + 63) // 64 * 64
    near_rows, far_rows = tile_rows + part_rows * pad, tile_rows + 2 * part_rows * pad
    fetched = [
        ocean_state,
        land_mask,
        out_grad,
        swath_offset.reshape(1, -1),
        swath_value.reshape(1, -1),
        expand_weight.T,
        expand_bias.reshape(1, hidden),
        project_weight,
        depth_kernel,
    ]
    count = len(fetched)
    outs = call(
        functools.partial(prepare_outer, swap, count),
        outer_shapes(pad, swap) + [shape(a.shape, a.dtype) for a in fetched],
        fetched,
        [pltpu.VMEM((2 * DIL * pad, cols), F32), pltpu.SemaphoreType.DMA((count,))],
        "outer_rows",
        far=True,
    )
    outer, (ocean_state, land_mask, *held) = outs[:-count], outs[-count:]
    to_far, tiles, taps = call(
        functools.partial(prepare_far, part),
        [shape((far_rows, LANES), BF), shape((tile_rows, LANES), BF), shape((pad, LANES), F32)],
        [land_mask, *held],
        [
            pltpu.VMEM((rows // 2 * pad, cols), F32),
            pltpu.VMEM((hid, wide), BF),
            turn,
            pltpu.VMEM((channels, wide), BF),
            pltpu.VMEM((channels, wide), BF),
        ],
        "far_rows",
    )
    masked, *strips = call(
        prepare_state,
        [block] + strip_shapes(pad),
        [ocean_state, land_mask],
        [flat],
        "state_rows",
        after=[taps],
    )
    cotan, own, to_core = call(
        prepare_near,
        [block, shape((near_rows, LANES), BF), shape((near_rows, LANES), BF)],
        [land_mask, *held[0:3], tiles],
        [flat],
        "cotan_rows",
    )
    around, _ = exchange_halo(rows, strips, outer, swap, "state", after=[to_core])
    from_far = lax.ppermute(to_far, "ch", across)
    ones = functools.partial(conv_forward, part)
    conv_operands = [masked, *around, taps]
    conv_scratch = [
        pltpu.VMEM((rows // 2 + 2 * DIL, pad, cols), BF),
        pltpu.VMEM((pad, LANES), F32),
        pltpu.VMEM((pad, LANES), F32),
        pltpu.VMEM((rows // 2, pad, cols), BF),
    ]
    conv_far = call(
        functools.partial(ones, 1), [quarter] * 2, conv_operands, conv_scratch, "conv_away"
    )
    eighth = shape((part_rows // 2, pad, cols), BF)
    conv_own, *conv_core = call(
        functools.partial(ones, 0),
        [quarter, eighth, eighth],
        conv_operands,
        conv_scratch,
        "conv_here",
        after=conv_far[:1],
    )
    both = [(i, i ^ 3) for i in range(n_ch)]
    all_conv = [
        conv_own,
        *[lax.ppermute(piece, "ch", core) for piece in conv_core],
        lax.ppermute(conv_far[0], "ch", across),
        lax.ppermute(conv_far[1], "ch", both),
    ]
    from_far = call(
        relay, [from_far], [from_far], (), "cotan_relay", aliases={0: 0}, after=around[1:2]
    )[0]
    passed = lax.ppermute(from_far, "ch", core)
    padded = shape((rows + 2 * DIL, pad, cols), BF)
    shifted = call(shift_columns, [padded, padded], [masked, *around], (), "shift_columns")
    act_grad, cotan_all, weights_all, weights_turned, *picks = call(
        functools.partial(activation_gradient, part),
        [
            shape((n_ch * hid, cells), F32),
            shape((depth, cells), BF),
            shape((n_ch * hid, wide), BF),
            shape((depth, n_ch * hid), BF),
            shape((channels, depth), BF),
            shape((channels, depth), BF),
        ],
        [own, lax.ppermute(to_core, "ch", core), from_far, passed],
        (),
        "activation_gradient",
        after=shifted[:1],
    )
    pre_grad, keep, send = call(
        hidden_gradient,
        [
            shape((n_ch * hid, cells), BF),
            shape((2, sum_rows, LANES), F32),
            shape((2, sum_rows, LANES), BF),
        ],
        [*all_conv, act_grad, cotan_all, weights_all],
        [pltpu.VMEM((depth, cells), BF), pltpu.VMEM((n_ch * hid, cells), BF)],
        "hidden_gradient",
    )
    got = lax.ppermute(send, "ch", core)
    grad_scratch = [pltpu.VMEM((2 * pad, cells), BF)]
    grad_far = call(
        functools.partial(conv_gradient, 1),
        [shape((2, part_rows, pad, cols), BF)],
        [pre_grad, weights_turned],
        grad_scratch,
        "gradient_away",
    )[0]
    grad_own, grad_core = call(
        functools.partial(conv_gradient, 0),
        [quarter] * 2,
        [pre_grad, weights_turned],
        grad_scratch,
        "gradient_here",
        after=[grad_far],
    )
    grad_near = lax.ppermute(grad_core, "ch", core)
    grad_far = lax.ppermute(grad_far, "ch", across)
    staged = two_by_four()
    if staged:
        piece = sum_rows // 4
        mine, *sends = call(
            add_cores,
            [shape((2, piece, LANES), F32)] + [shape((2, piece, LANES), BF)] * 3,
            [keep, got],
            (),
            "add_cores",
        )

        def turn_plane(k):
            pairs = []
            for lon in range(n_lon):
                for lat in range(n_lat):
                    pairs.append((lon * n_lat + lat, (lon ^ (k & 1)) * n_lat + (lat ^ (k >> 1))))
            return pairs

        def over_plane(values):
            return [lax.ppermute(values[k - 1], ("lon", "lat"), turn_plane(k)) for k in (1, 2, 3)]

        mine, other = call(
            add_pieces,
            [shape((piece, LANES), F32), shape((piece, LANES), BF)],
            [mine, *over_plane(sends)],
            (),
            "add_pieces",
            after=[grad_near],
        )
    passed = call(
        second_half, [quarter], [grad_far], (), "grad_half", after=[other] if staged else []
    )[0]
    conv_grad, *grad_strips = call(
        functools.partial(collect_grad, swap),
        [block] + strip_shapes(pad) + outer_shapes(pad, swap),
        [grad_own, grad_near, grad_far, lax.ppermute(passed, "ch", core)],
        (),
        "grad_rows",
    )
    kernel_part = call(
        kernel_gradient,
        [shape((pad, LANES), BF)],
        [conv_grad, masked, around[0], *shifted],
        (),
        "kernel_gradient",
    )[0]
    grad_around, marks = exchange_halo(rows, grad_strips[:3], grad_strips[3:], swap, "grad", planes=4, riding=[kernel_part])
    if staged:
        mine = call(
            add_across,
            [shape((piece, LANES), BF)],
            [mine, lax.ppermute(other, "ch", across)],
            (),
            "add_across",
        )[0]
    state_grad, mark = call(
        conv_adjoint,
        [shape((part, rows, cols), BF), shape((8, LANES), F32)],
        [conv_grad, *grad_around, taps, cotan, land_mask],
        [
            pltpu.VMEM((16 * (rows + 8), cols), F32),
            pltpu.VMEM((part, rows, cols), BF),
            pltpu.SemaphoreType.DMA((-(-part // 16),)),
        ],
        "conv_adjoint",
        writes=1,
    )
    outs = [
        shape((hidden, channels), F32),
        shape((hidden, channels), F32),
        shape((1, hidden), F32),
        shape((3, 3, part), F32),
    ]
    if staged:
        far_lon = [(lon, lon ^ 2) for lon in range(n_lon)]
        summed = call(
            finish_pieces,
            [shape((piece + TAP_ROWS, LANES), BF)],
            [
                mine,
                lax.ppermute(mine, "lon", far_lon),
                kernel_part,
                marks[1],
            ],
            [turn],
            "finish_pieces",
            after=marks[2:],
        )[0]
        expand_grad, project_grad, bias_grad, kernel_grad = call(
            functools.partial(write_parameters, part, pad, scale, hid),
            outs,
            [summed, *over_plane([summed] * 3), *picks],
            [pltpu.VMEM((sum_rows, LANES), BF), pltpu.VMEM((4 * TAP_ROWS, LANES), F32)],
            "write_parameters",
            after=[mark],
        )
    else:
        total = keep + got.astype(F32)
        total = total[0] + lax.ppermute(total[1].astype(BF), "ch", across).astype(F32)
        total, kernel_sum = lax.psum((total, kernel_part.astype(F32)), ("lon", "lat"))
        expand_grad, project_grad, bias_grad, kernel_grad = call(
            functools.partial(unpack_whole, part, pad, scale, hid),
            outs,
            [total.astype(BF), kernel_sum, *picks],
            [turn],
            "write_parameters",
        )
    return (
        state_grad,
        expand_grad.T,
        project_grad,
        bias_grad.reshape(hidden),
        kernel_grad,
    )


def solution(mesh):
    return jax.shard_map(
        on_device,
        mesh=mesh,
        in_specs=(
            P("ch", "lat", "lon"),
            P("lat", "lon"),
            P("ch", "lat", "lon"),
            P("lat", "lon", None),
            P("lat", "lon", None),
            P(None, None, "ch"),
            P(None, "ch"),
            P("ch"),
            P("ch", None),
        ),
        out_specs=(
            P("ch", "lat", "lon"),
            P(None, "ch"),
            P("ch", None),
            P("ch"),
            P(None, None, "ch"),
        ),
        check_vma=False,
    )
```

```python
import functools
import math

import jax
import jax.numpy as jnp
from jax import lax
from jax.experimental import pallas as pl
from jax.experimental.pallas import tpu as pltpu
from jax.sharding import PartitionSpec as P

DIL = 2
LANES = 128
TAP_ROWS = 16
RIDE = 96
BF = jnp.bfloat16
F32 = jnp.float32


def shape(dims, kind):
    return jax.ShapeDtypeStruct(dims, kind)


def call(kernel, outs, args, scratch=(), name=None, flops=0, aliases=None, far=False, after=(), writes=0):
    count = len(args)
    if after:
        body, args = kernel, [*args, *after]

        def kernel(*refs):
            body(*refs[:count], *refs[len(args) :])

    if far:
        args = [pltpu.with_memory_space_constraint(a, pltpu.HBM) for a in args]
    spaces = [pltpu.HBM if far else pl.ANY if i >= count else pltpu.VMEM for i in range(len(args))]
    moved = sum(math.prod(a.shape) * a.dtype.itemsize for a in list(args) + list(outs))
    return pl.pallas_call(
        kernel,
        out_shape=tuple(outs),
        in_specs=[pl.BlockSpec(memory_space=space) for space in spaces],
        out_specs=tuple(
            pl.BlockSpec(memory_space=pl.ANY if i < writes else pltpu.VMEM) for i in range(len(outs))
        ),
        scratch_shapes=list(scratch),
        input_output_aliases=aliases or {},
        name=name,
        compiler_params=pltpu.CompilerParams(vmem_limit_bytes=24 * 1024 * 1024),
        cost_estimate=pl.CostEstimate(flops=flops, bytes_accessed=moved, transcendentals=0),
    )(*args)


def iota(dims, dim):
    return lax.broadcasted_iota(jnp.int32, dims, dim)


def aligned(index):
    return pl.multiple_of(index, 16)


def to_rows(block_ref, weight, scr, pad):
    channels, rows, cols = block_ref.shape

    def body(c, carry):
        value = block_ref[c].astype(F32)
        if weight is not None:
            value = value * weight
        scr[pl.ds(c, rows, stride=pad), :] = value
        return carry

    lax.fori_loop(0, channels, body, 0, unroll=5 if channels % 5 == 0 else 1)
    for c in range(channels, pad):
        scr[pl.ds(c, rows, stride=pad), :] = jnp.zeros((rows, cols), F32)


def pack_columns(value, ext_row, left, right):
    lane = iota(value.shape, 1)
    here = (lane == 2 * ext_row) | (lane == 2 * ext_row + 1)
    size = value.shape[1]
    left = jnp.where(here, pltpu.roll(value, (2 * ext_row) % size, 1), left)
    right = jnp.where(here, pltpu.roll(value, (2 * ext_row + 2) % size, 1), right)
    return left, right


def mirrored(value):
    size = value.shape[1]
    flip = (iota((size, size), 0) + iota((size, size), 1) == size - 1).astype(BF)
    return jnp.dot(value, flip, preferred_element_type=F32).astype(BF)


def emit_strips(read, rows, pad, fold_ref, left_ref, right_ref):
    for t in range(DIL):
        fold_ref[t] = mirrored(read(rows - 1 - t))
    left = jnp.zeros((pad, LANES), F32)
    right = jnp.zeros((pad, LANES), F32)
    for r in range(rows):
        left, right = pack_columns(read(r).astype(F32), r + DIL, left, right)
    left_ref[...] = left.astype(BF)
    right_ref[...] = right.astype(BF)


def strip_shapes(pad):
    return [shape((DIL, pad, LANES), BF)] + [shape((pad, LANES), BF)] * 2


def outer_shapes(pad, swap):
    return [shape((DIL, pad, LANES), BF)] * (1 if swap else 2)


def emit_outer(low, high, t, swap, outer):
    if swap:
        outer[0][t] = jnp.where(lax.axis_index("lat") == 0, high, low).astype(BF)
    else:
        outer[0][t] = low.astype(BF)
        outer[1][t] = high.astype(BF)


def prepare_state(state_ref, mask_ref, rows_ref, fold_ref, left_ref, right_ref, scr):
    rows, pad = rows_ref.shape[:2]
    to_rows(state_ref, mask_ref[...].astype(F32), scr, pad)
    for r in range(rows):
        rows_ref[r] = scr[r * pad : (r + 1) * pad, :].astype(BF)
    emit_strips(lambda r: rows_ref[r], rows, pad, fold_ref, left_ref, right_ref)


def add_swath(scr, stride, rows, start, offset_ref, value_ref, cols):
    offset = offset_ref[...]
    points = offset.shape[1]
    value = value_ref[...]
    total = jnp.zeros((rows, cols), F32)
    row_hot = iota((rows, points), 0) + start == lax.shift_right_logical(offset, LANES.bit_length() - 1)
    col_hot = (iota((cols, points), 0) == (offset & (LANES - 1))).astype(BF)
    for _ in range(3):
        part = value.astype(BF)
        value = value - part.astype(F32)
        lhs = jnp.where(row_hot, part.astype(F32), 0.0).astype(BF)
        total = total + lax.dot_general(
            lhs, col_hot, (((1,), (1,)), ((), ())), preferred_element_type=F32
        )
    total = jnp.where(lax.axis_index("ch") == 0, total, 0.0)
    first = scr[pl.ds(0, rows, stride=stride), :]
    scr[pl.ds(0, rows, stride=stride), :] = first + total


def prepare_outer(swap, count, *refs):
    outs, (row_scr, sems) = refs[count:-2], refs[-2:]
    outer, held = outs[:-count], outs[-count:]
    state_ref, mask_ref = held[0:2]
    copies = [pltpu.make_async_copy(refs[k], held[k], sems.at[k]) for k in range(count)]
    for copy in copies:
        copy.start()
    pad = outer[0].shape[1]
    channels, rows, cols = state_ref.shape
    half = rows // 2
    lat = lax.axis_index("lat")
    for c in range(channels, pad):
        row_scr[pl.ds(c, 2 * DIL, stride=pad), :] = jnp.zeros((2 * DIL, cols), F32)
    copies[1].wait()
    copies[0].wait()
    if swap:
        start = aligned((1 - lat) * half)
        mask = mask_ref[pl.ds(start, half), :].astype(F32)

        def body(c, carry):
            value = state_ref[c, pl.ds(start, half), :].astype(F32) * mask
            row_scr[pl.ds(c, DIL, stride=pad), :] = jnp.where(
                lat == 0, value[half - DIL :, :], value[0:DIL, :]
            )
            return carry

    else:
        mask = mask_ref[...].astype(F32)

        def body(c, carry):
            value = state_ref[c].astype(F32) * mask
            row_scr[pl.ds(c, DIL, stride=pad), :] = value[0:DIL, :]
            row_scr[pl.ds(DIL * pad + c, DIL, stride=pad), :] = value[rows - DIL :, :]
            return carry

    lax.fori_loop(0, channels, body, 0, unroll=5 if channels % 5 == 0 else 1)
    for k, to in enumerate(outer):
        for t in range(DIL):
            at = (k * DIL + t) * pad
            to[t] = row_scr[at : at + pad, :].astype(BF)
    for copy in copies[2:]:
        copy.wait()


def prepare_far(part, *refs):
    (mask_ref, grad_ref, offset_ref, value_ref), weights = refs[0:4], refs[4:8]
    far_ref, tiles_ref, taps_ref = refs[8:11]
    scr, weights_scr, turn_scr, pick_e, pick_p = refs[11:]
    channels, rows, cols = grad_ref.shape
    pad = taps_ref.shape[0]
    weight_picks(part, pad, weights_scr.shape[1], pick_e.shape[0], pick_e, pick_p)
    pack_weights(part, pad, *weights, pick_e, pick_p, weights_scr, taps_ref, turn_scr)
    hid = weights_scr.shape[0]
    full = tiles_ref.shape[0]
    for t in range(full // hid):
        tiles_ref[t * hid : (t + 1) * hid, :] = weights_scr[:, t * LANES : (t + 1) * LANES]
    far_ref[0:full, :] = tiles_ref[...]
    half = rows // 2
    me = lax.axis_index("ch")
    start = aligned((1 - me // 2) * half)

    def body(c, carry):
        scr[pl.ds(c, half, stride=pad), :] = grad_ref[c, pl.ds(start, half), :].astype(F32)
        return carry

    lax.fori_loop(0, channels, body, 0, unroll=5 if channels % 5 == 0 else 1)
    for c in range(channels, pad):
        scr[pl.ds(c, half, stride=pad), :] = jnp.zeros((half, cols), F32)
    add_swath(scr, pad, half, start, offset_ref, value_ref, cols)
    mask = mask_ref[pl.ds(start, half), :].astype(F32)
    count_rows = half // 2
    for r in range(half):
        scr[r * pad : (r + 1) * pad, :] = scr[r * pad : (r + 1) * pad, :] * mask[r : r + 1, :]
    for k in range(2):
        first = aligned((((me ^ (2 + k)) % 2) * count_rows) * pad)
        size = count_rows * pad
        far_ref[full + k * size : full + (k + 1) * size, :] = scr[pl.ds(first, size), :].astype(BF)


def prepare_near(mask_ref, grad_ref, offset_ref, value_ref, tiles_ref, rows_ref, own_ref, core_ref, scr):
    rows, pad, cols = rows_ref.shape
    mask = mask_ref[...].astype(F32)
    to_rows(grad_ref, None, scr, pad)
    add_swath(scr, pad, rows, 0, offset_ref, value_ref, cols)
    for r in range(rows):
        rows_ref[r] = (scr[r * pad : (r + 1) * pad, :] * mask[r : r + 1, :]).astype(BF)
    full = tiles_ref.shape[0]
    count = (own_ref.shape[0] - full) // pad
    me = lax.axis_index("ch")
    for k, to in enumerate((own_ref, core_ref)):
        to[0:full, :] = tiles_ref[...]
        for r in range(count):
            at = full + r * pad
            to[at : at + pad, :] = rows_ref[(me ^ k) * count + r]


def second_half(in_ref, out_ref):
    out_ref[...] = in_ref[1]


def relay(in_ref, out_ref):
    del in_ref, out_ref


def ring(count, step):
    return [(i, (i + step) % count) for i in range(count)]


def finish_columns(rows, swap, *refs):
    if swap:
        strip_ref, fold_ref, left_ref, right_ref, halo_ref, left_out, right_out = refs
        low_ref = high_ref = strip_ref
    else:
        low_ref, high_ref, fold_ref, left_ref, right_ref, halo_ref, left_out, right_out = refs
    lat, count = lax.axis_index("lat"), lax.axis_size("lat")
    left, right = left_ref[...].astype(F32), right_ref[...].astype(F32)
    for t in range(DIL):
        south = jnp.where(lat == 0, 0.0, low_ref[t].astype(F32))
        north = jnp.where(lat == count - 1, fold_ref[t].astype(F32), high_ref[t].astype(F32))
        halo_ref[t] = south.astype(BF)
        halo_ref[DIL + t] = north.astype(BF)
        left, right = pack_columns(south, t, left, right)
        left, right = pack_columns(north, rows + DIL + t, left, right)
    left_out[...] = left.astype(BF)
    right_out[...] = right.astype(BF)


def odd_lon():
    return lax.axis_index("lon") % 2 == 1


def pack_for_third(rows, riding, *refs):
    if riding:
        ride_ref, *refs = refs
    got_ref, fold_ref, left_ref, right_ref, out_ref = refs
    low = lax.axis_index("lat") == 0
    left, right = left_ref[...].astype(F32), right_ref[...].astype(F32)
    for t in range(DIL):
        got = got_ref[t].astype(F32)
        left, right = pack_columns(jnp.where(low, 0.0, got), t, left, right)
        left, right = pack_columns(jnp.where(low, got, 0.0), rows + DIL + t, left, right)
        out_ref[t] = fold_ref[t]
    pack = jnp.where(odd_lon(), right, left)
    if riding:
        pack = pack + pltpu.roll(ride_ref[...].astype(F32), RIDE, 1)
    out_ref[DIL] = pack.astype(BF)


def pack_for_first(rows, got_ref, fold_ref, left_ref, right_ref, third_ref, halo_ref, out_ref, side_ref):
    low = lax.axis_index("lat") == 0
    odd = odd_lon()
    left, right = left_ref[...].astype(F32), right_ref[...].astype(F32)
    side = third_ref[DIL].astype(F32)
    size = side.shape[1]
    lane = iota(side.shape, 1)
    for t in range(DIL):
        got = got_ref[t].astype(F32)
        south = jnp.where(low, 0.0, got)
        north = jnp.where(low, got, third_ref[t].astype(F32))
        halo_ref[t] = south.astype(BF)
        halo_ref[DIL + t] = north.astype(BF)
        left, right = pack_columns(south, t, left, right)
        left, right = pack_columns(north, rows + DIL + t, left, right)
        at = 2 * (rows + DIL + t)
        own = fold_ref[t].astype(F32)
        own = jnp.where(
            odd, pltpu.roll(own, at, 1), pltpu.roll(own, (at - (size - DIL)) % size, 1)
        )
        here = jnp.logical_and((lane == at) | (lane == at + 1), jnp.logical_not(low))
        side = jnp.where(here, own, side)
    out_ref[0] = jnp.where(odd, left, right).astype(BF)
    for k in range(1, out_ref.shape[0]):
        out_ref[k] = jnp.zeros(side.shape, BF)
    side_ref[...] = side.astype(BF)


def two_by_four():
    return lax.axis_size("lat") == 2 and lax.axis_size("lon") == 4


def exchange_halo(rows, strips, outer, swap, name, planes=1, riding=(), after=()):
    n_lat, n_lon = lax.axis_size("lat"), lax.axis_size("lon")
    fold, left, right = strips
    pad = left.shape[0]
    halo_shape, pack = shape((2 * DIL, pad, LANES), BF), shape((pad, LANES), BF)
    if two_by_four():
        got = lax.ppermute(outer[0], "lat", [(0, 1), (1, 0)])
        third_out = call(
            functools.partial(pack_for_third, rows, len(riding) > 0),
            [shape((DIL + 1, pad, LANES), BF)],
            [*riding, got, fold, left, right],
            (),
            name + "_third",
            after=after,
        )[0]
        third = lax.ppermute(third_out, "lon", [(lon, lon ^ 3) for lon in range(n_lon)])
        halo, first, side = call(
            functools.partial(pack_for_first, rows),
            [halo_shape, shape((planes, pad, LANES), BF), pack],
            [got, fold, left, right, third],
            (),
            name + "_first",
        )
        got = lax.ppermute(first, "lon", [(lon, lon ^ 1) for lon in range(n_lon)])
        return (halo, got, side), (third_out, third, first)
    top = n_lat - 1
    fold_pairs = [(lon * n_lat + top, (n_lon - 1 - lon) * n_lat + top) for lon in range(n_lon)]
    if swap:
        moved = [lax.ppermute(outer[0], "lat", [(0, 1), (1, 0)])]
    else:
        moved = [
            lax.ppermute(outer[1], "lat", [(i, i + 1) for i in range(n_lat - 1)]),
            lax.ppermute(outer[0], "lat", [(i + 1, i) for i in range(n_lat - 1)]),
        ]
    fold = lax.ppermute(fold, ("lon", "lat"), fold_pairs)
    halo, left, right = call(
        functools.partial(finish_columns, rows, swap),
        [halo_shape, pack, pack],
        [*moved, fold, left, right],
        (),
        name + "_columns",
    )
    from_right = lax.ppermute(left, "lon", ring(n_lon, -1))
    from_left = lax.ppermute(right, "lon", ring(n_lon, 1))
    return (halo, from_left, from_right), ()


def padded_row(block_ref, halo_ref, at, e):
    rows = block_ref.shape[0]
    if e < DIL:
        return halo_ref[e, at, :]
    if e < rows + DIL:
        return block_ref[e - DIL, at, :]
    return halo_ref[e - rows, at, :]


def sides(left_ref, right_ref, at):
    left = (left_ref[0, at, :] if two_by_four() else left_ref[at, :]).astype(F32)
    right = right_ref[at, :].astype(F32)
    if two_by_four():
        odd = odd_lon()
        left, right = jnp.where(odd, left, right), jnp.where(odd, right, left)
    return left, right


def shifted_rows(rows, read, left, right):
    lane = iota((16, LANES), 1)
    for e in range(rows + 2 * DIL):
        row = read(e).astype(F32)
        west = jnp.where(
            lane < DIL, pltpu.roll(left, (-2 * e) % LANES, 1), pltpu.roll(row, DIL, 1)
        )
        east = jnp.where(
            lane >= LANES - DIL,
            pltpu.roll(right, (LANES - DIL - 2 * e) % LANES, 1),
            pltpu.roll(row, LANES - DIL, 1),
        )
        yield e, (west, row, east)


def stencil_rows(rows, read, left, right, taps, north, emit):
    sums = {}
    for e, shifts in shifted_rows(rows, read, left, right):
        for a in (2, 1, 0):
            r = e - DIL * a
            if not 0 <= r < rows:
                continue
            used = north if e >= rows + DIL else taps[a]
            term = used[0] * shifts[0] + used[1] * shifts[1] + used[2] * shifts[2]
            sums[r] = term if r not in sums else sums[r] + term
            if a == 2:
                emit(r, sums.pop(r))


def stencil(block_ref, halo_ref, left_ref, right_ref, group, taps, north, emit):
    at = pl.ds(aligned(group * 16), 16)
    left, right = sides(left_ref, right_ref, at)
    read = functools.partial(padded_row, block_ref, halo_ref, at)
    stencil_rows(block_ref.shape[0], read, left, right, taps, north, emit)


def spread(tap_ref, group):
    values = tap_ref[pl.ds(aligned(group * 16), 16), :]
    return [
        [jnp.broadcast_to(values[:, 3 * a + b : 3 * a + b + 1], (16, LANES)) for b in range(3)]
        for a in range(3)
    ]


def conv_forward(ones_row, away, block_ref, halo_ref, left_ref, right_ref, tap_ref, *rest):
    outs, (row_scr, left_scr, right_scr, scr) = rest[:-4], rest[-4:]
    rows, pad = block_ref.shape[:2]
    half = rows // 2
    me = lax.axis_index("ch")
    upper = (me // 2 + away) % 2
    west, east = sides(left_ref, right_ref, slice(None))
    left_scr[...] = pltpu.roll(west, (LANES - 2 * half * upper) % LANES, 1)
    right_scr[...] = pltpu.roll(east, (LANES - 2 * half * upper) % LANES, 1)
    for t in range(DIL):
        low, high = halo_ref[t].astype(F32), halo_ref[DIL + t].astype(F32)
        before = block_ref[half - DIL + t].astype(F32)
        behind = block_ref[half + t].astype(F32)
        row_scr[t] = jnp.where(upper == 0, low, before).astype(BF)
        row_scr[half + DIL + t] = jnp.where(upper == 0, behind, high).astype(BF)
    for r in range(half):
        row_scr[DIL + r] = block_ref[upper * half + r]

    def body(group, carry):
        taps = spread(tap_ref, group)
        is_one = iota((16, LANES), 0) + group * 16 == ones_row
        at = pl.ds(aligned(group * 16), 16)

        def emit(r, value):
            value = jnp.where(is_one, 1.0, value)
            scr[r, at, :] = value.astype(BF)

        left, right = left_scr[at, :], right_scr[at, :]
        stencil_rows(half, lambda e: row_scr[e, at, :], left, right, taps, taps[2], emit)
        return carry

    lax.fori_loop(0, pad // 16, body, 0)
    count = half // 2
    size = outs[0].shape[0]
    for k, to in enumerate(outs):
        first = ((me + k % 2) % 2) * count
        to[...] = scr[pl.ds(first + k // 2 * size, size)]


def conv_adjoint(
    block_ref, halo_ref, left_ref, right_ref, tap_ref, cotan_ref, mask_ref, out_ref, mark_ref, scr, done_scr, sems
):
    rows, pad = block_ref.shape[:2]
    channels = out_ref.shape[0]
    at_top = lax.axis_index("lat") == lax.axis_size("lat") - 1
    mask = mask_ref[...].astype(F32)

    def copy(group, count):
        at = pl.ds(group * 16, count)
        return pltpu.make_async_copy(done_scr.at[at], out_ref.at[at], sems.at[group])

    def body(group, count):
        taps = spread(tap_ref, group)
        back = [[taps[2 - a][2 - b] for b in range(3)] for a in range(3)]
        north = [jnp.where(at_top, taps[2][b], back[2][b]) for b in range(3)]

        def emit(r, value):
            cotan = cotan_ref[r, pl.ds(aligned(group * 16), 16), :].astype(F32)
            scr[pl.ds(r, 16, stride=rows + 8), :] = (cotan + value) * mask[r : r + 1, :]

        stencil(block_ref, halo_ref, left_ref, right_ref, group, back, north, emit)
        for c in range(count):
            at = c * (rows + 8)
            done_scr[group * 16 + c] = scr[at : at + rows, :].astype(BF)
        copy(group, count).start()

    whole = channels // 16

    def each(group, carry):
        body(group, 16)
        return carry

    lax.fori_loop(0, whole, each, 0)
    if channels % 16:
        body(whole, channels % 16)
    mark_ref[...] = jnp.zeros(mark_ref.shape, F32)
    for group in range(whole):
        copy(group, 16).wait()
    if channels % 16:
        copy(whole, channels % 16).wait()


def collect_grad(swap, own, near, far, passed, rows_ref, *rest):
    part_rows = own.shape[0]
    rows, pad = rows_ref.shape[:2]
    me = lax.axis_index("ch")
    for k, quarter in enumerate((own, near, far.at[0], passed)):
        rows_ref[pl.ds((me ^ k) * part_rows, part_rows)] = quarter[...]
    strips, outer = rest[:3], rest[3:]
    for t in range(DIL):
        emit_outer(rows_ref[t].astype(F32), rows_ref[rows - DIL + t].astype(F32), t, swap, outer)
    emit_strips(lambda r: rows_ref[r], rows, pad, *strips)


def shift_columns(block_ref, halo_ref, left_ref, right_ref, west_ref, east_ref):
    def body(group, carry):
        at = pl.ds(aligned(group * 16), 16)
        left, right = sides(left_ref, right_ref, at)
        read = functools.partial(padded_row, block_ref, halo_ref, at)
        for e, shifts in shifted_rows(block_ref.shape[0], read, left, right):
            west_ref[e, at, :] = shifts[0].astype(BF)
            east_ref[e, at, :] = shifts[2].astype(BF)
        return carry

    lax.fori_loop(0, block_ref.shape[1] // 16, body, 0)


def kernel_gradient(grad_ref, block_ref, halo_ref, west_ref, east_ref, out_ref):
    rows, pad = grad_ref.shape[:2]

    def body(group, carry):
        at = pl.ds(aligned(group * 16), 16)
        sums = [[jnp.zeros((16, LANES), F32) for _ in range(3)] for _ in range(3)]
        for e in range(rows + 2 * DIL):
            middle = padded_row(block_ref, halo_ref, at, e)
            shifts = [part.astype(F32) for part in (west_ref[e, at, :], middle, east_ref[e, at, :])]
            for a in range(3):
                r = e - DIL * a
                if 0 <= r < rows:
                    grad = grad_ref[r, at, :].astype(F32)
                    for b in range(3):
                        sums[a][b] = sums[a][b] + grad * shifts[b]
        lane = iota((16, LANES), 1)
        out = jnp.zeros((16, LANES), F32)
        for a in range(3):
            for b in range(3):
                total = jnp.sum(sums[a][b], axis=1, keepdims=True)
                out = jnp.where(lane == 3 * a + b, total, out)
        out_ref[at, :] = out.astype(BF)
        return carry

    lax.fori_loop(0, pad // 16, body, 0)


def channel_of(slot, part, pad):
    block = sum((slot >= pad * b).astype(jnp.int32) for b in range(1, 4))
    inside = slot - block * pad
    return jnp.where((slot >= 0) & (slot < 4 * pad) & (inside < part), block * part + inside, -1)


def expand_slot(lane, pad):
    return jnp.where(lane < 4 * pad, lane, -1)


def project_slot(lane, pad, split):
    tail = 4 * pad - split
    low = LANES - tail
    return jnp.where(lane >= LANES, lane - LANES, jnp.where(lane >= low, lane - low + split, -1))


def weight_picks(part, pad, wide, channels, pick_e_ref, pick_p_ref):
    split = 4 * pad // LANES * LANES
    lane = iota((channels, wide), 1)
    row = iota((channels, wide), 0)
    pick_e_ref[...] = (channel_of(expand_slot(lane, pad), part, pad) == row).astype(BF)
    slot = jnp.where(lane >= split, project_slot(lane - split, pad, split), -1)
    pick_p_ref[...] = (channel_of(slot, part, pad) == row).astype(BF)


def output_picks(part, pad, pick_e_ref, pick_p_ref):
    channels, depth = pick_e_ref.shape
    split = 4 * pad // LANES * LANES
    lane, row = iota((channels, depth), 1), iota((channels, depth), 0)
    pick_e_ref[...] = (channel_of(expand_slot(lane, pad), part, pad) == row).astype(BF)
    pick_p_ref[...] = (channel_of(project_slot(lane, pad, split), part, pad) == row).astype(BF)


def pack_weights(
    part, pad, expand_ref, bias_ref, project_ref, kernel_ref, pick_e_ref, pick_p_ref, out_ref, taps_ref, turn_scr
):
    hidden, channels = expand_ref.shape
    turn_scr[...] = jnp.zeros(turn_scr.shape, F32)
    for a in range(3):
        turn_scr[3 * a : 3 * a + 3, 0:part] = kernel_ref[a]
    taps_ref[...] = jnp.transpose(turn_scr[...])[0:pad, :]
    wide = out_ref.shape[1]
    bias = bias_ref[...]
    parts = jnp.zeros((16, hidden), F32)
    at = iota((16, hidden), 0)
    for k in range(3):
        piece = bias.astype(BF).astype(F32)
        bias = bias - piece
        parts = jnp.where(at == k, piece, parts)
    lane, row = iota((16, wide), 1), iota((16, wide), 0)
    pick_b = ((lane == row * pad + part) & (row < 3)).astype(BF)
    turned = (((0,), (0,)), ((), ()))
    packed = (
        jnp.dot(expand_ref[...], pick_e_ref[...], preferred_element_type=F32)
        + lax.dot_general(parts.astype(BF), pick_b, turned, preferred_element_type=F32)
        + jnp.dot(project_ref[...], pick_p_ref[...], preferred_element_type=F32)
    )
    rows = out_ref.shape[0]
    out_ref[0:hidden, :] = packed.astype(BF)
    out_ref[hidden:rows, :] = jnp.zeros((rows - hidden, wide), BF)


GELU_C = math.sqrt(2.0 / math.pi)


def activation_gradient(part, *refs):
    parts = refs[0:4]
    act_ref, y_scr, w_scr, t_scr, pick_e_ref, pick_p_ref = refs[4:]
    me = lax.axis_index("ch")
    tiles = w_scr.shape[1] // LANES
    hid = w_scr.shape[0] // 4
    depth, cells = y_scr.shape
    part_rows = cells // LANES
    pad = (parts[0].shape[0] - tiles * hid) // part_rows
    split = 4 * pad // LANES * LANES
    output_picks(part, pad, pick_e_ref, pick_p_ref)
    y_scr[0 : depth - 4 * pad, :] = jnp.zeros((depth - 4 * pad, cells), BF)
    for k, ref in enumerate(parts):
        for t in range(tiles):
            w_scr[k * hid : (k + 1) * hid, t * LANES : (t + 1) * LANES] = ref[
                t * hid : (t + 1) * hid, :
            ]
        block = me ^ k
        start = tiles * hid + (part_rows * pad if k == 3 else 0)
        for r in range(part_rows):
            cols = slice(r * LANES, (r + 1) * LANES)
            for u in range(pad // 16):
                slot = block * pad + 16 * u
                to = jnp.where(slot < split, slot + LANES, slot - split + depth - 4 * pad)
                at = start + r * pad + 16 * u
                y_scr[pl.ds(aligned(to), 16), cols] = ref[at : at + 16, :]
    t_scr[...] = jnp.transpose(w_scr[:, 0:depth])
    step = 256
    for start in range(0, cells, step):
        cols = slice(start, start + step)
        act_ref[:, cols] = jnp.dot(
            w_scr[:, split : split + depth], y_scr[:, cols], preferred_element_type=F32
        )


def hidden_gradient(half, *refs):
    xs, (act_ref, y_ref, w_ref), refs = refs[0:4], refs[4:7], refs[7:]
    sums = ()
    if half:
        sums, refs = refs[0:2], refs[2:]
    pre_ref, keep_ref, send_ref, x_scr, value_scr = refs
    part_rows, pad = xs[0].shape[:2]
    hid = w_ref.shape[0] // 4
    split = 4 * pad // LANES * LANES
    depth, cells = x_scr.shape
    offset = half * cells
    me = lax.axis_index("ch")
    x_scr[4 * pad : depth, :] = jnp.zeros((depth - 4 * pad, cells), BF)
    for k in range(4):
        for r in range(part_rows):
            cols = slice(r * LANES, (r + 1) * LANES)
            x_scr[pl.ds(aligned((me ^ k) * pad), pad), cols] = xs[k][r]
    step = 256
    for start in range(0, cells, step):
        cols = slice(start, start + step)
        hidden = jnp.dot(w_ref[:, 0:depth], x_scr[:, cols], preferred_element_type=F32)
        square = hidden * hidden
        tanh = jnp.tanh(hidden * (GELU_C + (0.044715 * GELU_C) * square))
        each = 0.5 + 0.5 * tanh
        slope = each + hidden * (0.5 * GELU_C + (1.5 * 0.044715 * GELU_C) * square) * (
            1.0 - tanh * tanh
        )
        value_scr[:, cols] = (hidden * each).astype(BF)
        pre_ref[:, cols] = (act_ref[:, offset + start : offset + start + step] * slope).astype(BF)
    over_cells = (((1,), (1,)), ((), ()))
    expand = lax.dot_general(pre_ref[...], x_scr[...], over_cells, preferred_element_type=F32)
    project = lax.dot_general(
        value_scr[...], y_ref[:, offset : offset + cells], over_cells, preferred_element_type=F32
    )
    shared = split // LANES
    tiles = [expand[:, t * LANES : (t + 1) * LANES] for t in range(shared)]
    tiles.append(expand[:, split : split + LANES] + project[:, 0:LANES])
    tiles += [project[:, t * LANES : (t + 1) * LANES] for t in range(1, shared + 1)]
    used = len(tiles) * hid
    for ref in (keep_ref, send_ref):
        for k in range(2):
            ref[k, used:, :] = jnp.zeros((ref.shape[1] - used, LANES), ref.dtype)
    for k in range(4):
        to = send_ref if k % 2 else keep_ref
        for t, tile in enumerate(tiles):
            at = (k // 2, slice(t * hid, (t + 1) * hid), slice(None))
            value = tile[k * hid : (k + 1) * hid]
            if half:
                value = value + sums[k % 2][at]
            to[at] = value.astype(to.dtype)


def conv_gradient(away, first_ref, second_ref, t_ref, *rest):
    outs, scr = rest[:-1], rest[-1]
    if away:
        outs = (rest[0].at[0], rest[0].at[1])
    part_rows, pad = outs[0].shape[:2]
    me = lax.axis_index("ch")
    first = ((me // 2 + away) % 2) * 2 * pad
    weights = t_ref[pl.ds(aligned(first), 2 * pad), :]
    step = 256
    half = first_ref.shape[1]
    for start in range(0, 2 * half, step):
        pre = (first_ref if start < half else second_ref)[:, start % half : start % half + step]
        scr[:, start : start + step] = jnp.dot(weights, pre, preferred_element_type=F32).astype(BF)
    for k, to in enumerate(outs):
        at = pl.ds(aligned(((me + k) % 2) * pad), pad)
        for r in range(part_rows):
            to[r] = scr[at, r * LANES : (r + 1) * LANES]


def add_cores(keep_ref, got_ref, own_ref, *sends):
    piece = own_ref.shape[1]
    place = 2 * lax.axis_index("lat") + lax.axis_index("lon") % 2
    for k in range(4):
        at = pl.ds(aligned((place ^ k) * piece), piece)
        for group in range(2):
            total = keep_ref[group, at, :] + got_ref[group, at, :].astype(F32)
            to = sends[k - 1] if k else own_ref
            to[group] = total.astype(to.dtype)


def add_pieces(own_ref, a_ref, b_ref, c_ref, mine_ref, other_ref):
    for group, to in enumerate((mine_ref, other_ref)):
        total = own_ref[group] + (
            a_ref[group].astype(F32) + b_ref[group].astype(F32) + c_ref[group].astype(F32)
        )
        to[...] = total.astype(to.dtype)


def add_across(mine_ref, got_ref, out_ref):
    out_ref[...] = (mine_ref[...] + got_ref[...].astype(F32)).astype(BF)


def finish_pieces(mine_ref, line_ref, kernel_ref, third_ref, out_ref, turn_scr):
    piece, pad = mine_ref.shape[0], kernel_ref.shape[0]
    out_ref[0:piece, :] = (mine_ref[...].astype(F32) + line_ref[...].astype(F32)).astype(BF)
    other = pltpu.roll(third_ref[DIL].astype(F32), LANES - RIDE, 1)
    turn_scr[...] = jnp.zeros(turn_scr.shape, F32)
    turn_scr[0:pad, :] = kernel_ref[...].astype(F32) + other
    out_ref[piece:, :] = jnp.transpose(turn_scr[...])[0:TAP_ROWS, :].astype(BF)


def write_parameters(part, pad, scale, hid, p0, p1, p2, p3, pick_e, pick_p, *rest):
    expand_ref, project_ref, bias_ref, taps_ref, all_scr, taps_scr = rest
    piece = p0.shape[0] - TAP_ROWS
    place = 2 * lax.axis_index("lat") + lax.axis_index("lon") % 2
    for k, ref in enumerate((p0, p1, p2, p3)):
        to = place ^ k
        all_scr[pl.ds(aligned(to * piece), piece), :] = ref[0:piece, :]
        taps_scr[pl.ds(aligned(to * TAP_ROWS), TAP_ROWS), :] = ref[piece:, :].astype(F32)
    unpack(part, pad, scale, hid, all_scr, pick_e, pick_p, expand_ref, project_ref, bias_ref)
    total = taps_scr[0:TAP_ROWS, :]
    for k in range(1, 4):
        total = total + taps_scr[k * TAP_ROWS : (k + 1) * TAP_ROWS, :]
    write_taps(total, scale, taps_ref)


def write_taps(total, scale, taps_ref):
    for a in range(3):
        taps_ref[a] = total[3 * a : 3 * a + 3, 0 : taps_ref.shape[2]] * scale


def unpack(part, pad, scale, hid, all_ref, pick_e, pick_p, expand_ref, project_ref, bias_ref):
    hidden = expand_ref.shape[0]
    split = 4 * pad // LANES * LANES
    shared = split // LANES
    tiles = [all_ref[t * hid : (t + 1) * hid, :] for t in range(2 * shared + 1)]
    depth = (shared + 1) * LANES
    expand = jnp.concatenate(tiles[: shared + 1], axis=1)
    project = jnp.concatenate(tiles[shared:], axis=1)
    pick_b = (iota((16, depth), 1) == part).astype(BF)
    last = (((1,), (1,)), ((), ()))
    dot = functools.partial(lax.dot_general, dimension_numbers=last, preferred_element_type=F32)
    expand_ref[...] = dot(expand, pick_e[...])[0:hidden, :] * scale
    bias_ref[...] = dot(pick_b, expand)[0:1, 0:hidden] * scale
    project_ref[...] = dot(project, pick_p[...])[0:hidden, :] * scale


def unpack_whole(part, pad, scale, hid, all_ref, taps_in, pick_e, pick_p, *rest):
    expand_ref, project_ref, bias_ref, taps_ref, turn_scr = rest
    unpack(part, pad, scale, hid, all_ref, pick_e, pick_p, expand_ref, project_ref, bias_ref)
    turn_scr[...] = jnp.zeros(turn_scr.shape, F32)
    turn_scr[0:pad, :] = taps_in[...]
    write_taps(jnp.transpose(turn_scr[...])[0:TAP_ROWS, :], scale, taps_ref)


def on_device(
    ocean_state,
    land_mask,
    out_grad,
    swath_offset,
    swath_value,
    depth_kernel,
    expand_weight,
    expand_bias,
    project_weight,
):
    part, rows, cols = ocean_state.shape
    n_lon, n_lat, n_ch = lax.axis_size("lon"), lax.axis_size("lat"), lax.axis_size("ch")
    channels, hidden = expand_weight.shape
    assert n_ch == 4 and cols == LANES and rows % n_ch == 0
    pad = (part + 16) // 16 * 16
    hid = (hidden + 15) // 16 * 16
    split = n_ch * pad // LANES * LANES
    tail = n_ch * pad - split
    assert tail == LANES // 2
    wide = 2 * n_ch * pad
    depth = split + LANES
    part_rows = rows // n_ch
    cells = part_rows * cols
    swap = n_lat == 2
    scale = 1.0 / math.sqrt(rows * n_lat * cols * n_lon)
    core = [(i, i ^ 1) for i in range(n_ch)]
    across = [(i, i ^ 2) for i in range(n_ch)]
    block = shape((rows, pad, cols), BF)
    quarter = shape((part_rows, pad, cols), BF)
    flat = pltpu.VMEM((rows * pad, cols), F32)

    turn = pltpu.VMEM((LANES, LANES), F32)

    tile_rows = wide // LANES * hid
    sum_rows = (tile_rows + 63) // 64 * 64
    near_rows, far_rows = tile_rows + part_rows * pad, tile_rows + 2 * part_rows * pad
    fetched = [
        ocean_state,
        land_mask,
        out_grad,
        swath_offset.reshape(1, -1),
        swath_value.reshape(1, -1),
        expand_weight.T,
        expand_bias.reshape(1, hidden),
        project_weight,
        depth_kernel,
    ]
    count = len(fetched)
    outs = call(
        functools.partial(prepare_outer, swap, count),
        outer_shapes(pad, swap) + [shape(a.shape, a.dtype) for a in fetched],
        fetched,
        [pltpu.VMEM((2 * DIL * pad, cols), F32), pltpu.SemaphoreType.DMA((count,))],
        "outer_rows",
        far=True,
    )
    outer, (ocean_state, land_mask, *held) = outs[:-count], outs[-count:]
    to_far, tiles, taps = call(
        functools.partial(prepare_far, part),
        [shape((far_rows, LANES), BF), shape((tile_rows, LANES), BF), shape((pad, LANES), F32)],
        [land_mask, *held],
        [
            pltpu.VMEM((rows // 2 * pad, cols), F32),
            pltpu.VMEM((hid, wide), BF),
            turn,
            pltpu.VMEM((channels, wide), BF),
            pltpu.VMEM((channels, wide), BF),
        ],
        "far_rows",
    )
    masked, *strips = call(
        prepare_state,
        [block] + strip_shapes(pad),
        [ocean_state, land_mask],
        [flat],
        "state_rows",
        after=[taps],
    )
    cotan, own, to_core = call(
        prepare_near,
        [block, shape((near_rows, LANES), BF), shape((near_rows, LANES), BF)],
        [land_mask, *held[0:3], tiles],
        [flat],
        "cotan_rows",
    )
    around, _ = exchange_halo(rows, strips, outer, swap, "state", after=[to_core])
    from_far = lax.ppermute(to_far, "ch", across)
    ones = functools.partial(conv_forward, part)
    conv_operands = [masked, *around, taps]
    conv_scratch = [
        pltpu.VMEM((rows // 2 + 2 * DIL, pad, cols), BF),
        pltpu.VMEM((pad, LANES), F32),
        pltpu.VMEM((pad, LANES), F32),
        pltpu.VMEM((rows // 2, pad, cols), BF),
    ]
    eighth = shape((part_rows // 2, pad, cols), BF)
    conv_far = call(
        functools.partial(ones, 1), [eighth] * 4, conv_operands, conv_scratch, "conv_away"
    )
    from_far = call(
        relay, [from_far], [from_far], (), "cotan_relay", aliases={0: 0}, after=around[1:2]
    )[0]
    passed = lax.ppermute(from_far, "ch", core)
    conv_near = call(
        functools.partial(ones, 0),
        [eighth] * 4,
        conv_operands,
        conv_scratch,
        "conv_here",
        after=[conv_far[0], passed],
    )
    both = [(i, i ^ 3) for i in range(n_ch)]
    halves = [
        [
            conv_near[2 * h],
            lax.ppermute(conv_near[2 * h + 1], "ch", core),
            lax.ppermute(conv_far[2 * h], "ch", across),
            lax.ppermute(conv_far[2 * h + 1], "ch", both),
        ]
        for h in range(2)
    ]
    act_grad, cotan_all, weights_all, weights_turned, *picks = call(
        functools.partial(activation_gradient, part),
        [
            shape((n_ch * hid, cells), F32),
            shape((depth, cells), BF),
            shape((n_ch * hid, wide), BF),
            shape((depth, n_ch * hid), BF),
            shape((channels, depth), BF),
            shape((channels, depth), BF),
        ],
        [own, lax.ppermute(to_core, "ch", core), from_far, passed],
        (),
        "activation_gradient",
    )
    pre_grad, sums = [], ()
    for h in range(2):
        pre, *sums = call(
            functools.partial(hidden_gradient, h),
            [
                shape((n_ch * hid, cells // 2), BF),
                shape((2, sum_rows, LANES), F32),
                shape((2, sum_rows, LANES), BF if h else F32),
            ],
            [*halves[h], act_grad, cotan_all, weights_all, *sums],
            [pltpu.VMEM((depth, cells // 2), BF), pltpu.VMEM((n_ch * hid, cells // 2), BF)],
            "hidden_first" if h == 0 else "hidden_second",
        )
        pre_grad.append(pre)
    keep, send = sums
    got = lax.ppermute(send, "ch", core)
    grad_scratch = [pltpu.VMEM((2 * pad, cells), BF)]
    grad_far = call(
        functools.partial(conv_gradient, 1),
        [shape((2, part_rows, pad, cols), BF)],
        [*pre_grad, weights_turned],
        grad_scratch,
        "gradient_away",
    )[0]
    grad_own, grad_core = call(
        functools.partial(conv_gradient, 0),
        [quarter] * 2,
        [*pre_grad, weights_turned],
        grad_scratch,
        "gradient_here",
        after=[grad_far],
    )
    grad_near = lax.ppermute(grad_core, "ch", core)
    grad_far = lax.ppermute(grad_far, "ch", across)
    staged = two_by_four()
    padded = shape((rows + 2 * DIL, pad, cols), BF)
    if not staged:
        shifted = call(shift_columns, [padded, padded], [masked, *around], (), "shift_columns")
    if staged:
        piece = sum_rows // 4
        mine, *sends = call(
            add_cores,
            [shape((2, piece, LANES), F32)] + [shape((2, piece, LANES), BF)] * 3,
            [keep, got],
            (),
            "add_cores",
        )

        shifted = call(
            shift_columns, [padded, padded], [masked, *around], (), "shift_columns", after=sends[:1]
        )

        def turn_plane(k):
            pairs = []
            for lon in range(n_lon):
                for lat in range(n_lat):
                    pairs.append((lon * n_lat + lat, (lon ^ (k & 1)) * n_lat + (lat ^ (k >> 1))))
            return pairs

        def over_plane(values):
            return [lax.ppermute(values[k - 1], ("lon", "lat"), turn_plane(k)) for k in (1, 2, 3)]

        mine, other = call(
            add_pieces,
            [shape((piece, LANES), F32), shape((piece, LANES), BF)],
            [mine, *over_plane(sends)],
            (),
            "add_pieces",
            after=[grad_near, shifted[0]],
        )
    passed = call(
        second_half, [quarter], [grad_far], (), "grad_half", after=[other] if staged else []
    )[0]
    conv_grad, *grad_strips = call(
        functools.partial(collect_grad, swap),
        [block] + strip_shapes(pad) + outer_shapes(pad, swap),
        [grad_own, grad_near, grad_far, lax.ppermute(passed, "ch", core)],
        (),
        "grad_rows",
    )
    kernel_part = call(
        kernel_gradient,
        [shape((pad, LANES), BF)],
        [conv_grad, masked, around[0], *shifted],
        (),
        "kernel_gradient",
    )[0]
    grad_around, marks = exchange_halo(rows, grad_strips[:3], grad_strips[3:], swap, "grad", planes=4, riding=[kernel_part])
    if staged:
        mine = call(
            add_across,
            [shape((piece, LANES), BF)],
            [mine, lax.ppermute(other, "ch", across)],
            (),
            "add_across",
        )[0]
    state_grad, mark = call(
        conv_adjoint,
        [shape((part, rows, cols), BF), shape((8, LANES), F32)],
        [conv_grad, *grad_around, taps, cotan, land_mask],
        [
            pltpu.VMEM((16 * (rows + 8), cols), F32),
            pltpu.VMEM((part, rows, cols), BF),
            pltpu.SemaphoreType.DMA((-(-part // 16),)),
        ],
        "conv_adjoint",
        writes=1,
    )
    outs = [
        shape((hidden, channels), F32),
        shape((hidden, channels), F32),
        shape((1, hidden), F32),
        shape((3, 3, part), F32),
    ]
    if staged:
        far_lon = [(lon, lon ^ 2) for lon in range(n_lon)]
        summed = call(
            finish_pieces,
            [shape((piece + TAP_ROWS, LANES), BF)],
            [
                mine,
                lax.ppermute(mine, "lon", far_lon),
                kernel_part,
                marks[1],
            ],
            [turn],
            "finish_pieces",
            after=marks[2:],
        )[0]
        expand_grad, project_grad, bias_grad, kernel_grad = call(
            functools.partial(write_parameters, part, pad, scale, hid),
            outs,
            [summed, *over_plane([summed] * 3), *picks],
            [pltpu.VMEM((sum_rows, LANES), BF), pltpu.VMEM((4 * TAP_ROWS, LANES), F32)],
            "write_parameters",
            after=[mark],
        )
    else:
        total = keep + got.astype(F32)
        total = total[0] + lax.ppermute(total[1].astype(BF), "ch", across).astype(F32)
        total, kernel_sum = lax.psum((total, kernel_part.astype(F32)), ("lon", "lat"))
        expand_grad, project_grad, bias_grad, kernel_grad = call(
            functools.partial(unpack_whole, part, pad, scale, hid),
            outs,
            [total.astype(BF), kernel_sum, *picks],
            [turn],
            "write_parameters",
        )
    return (
        state_grad,
        expand_grad.T,
        project_grad,
        bias_grad.reshape(hidden),
        kernel_grad,
    )


def solution(mesh):
    return jax.shard_map(
        on_device,
        mesh=mesh,
        in_specs=(
            P("ch", "lat", "lon"),
            P("lat", "lon"),
            P("ch", "lat", "lon"),
            P("lat", "lon", None),
            P("lat", "lon", None),
            P(None, None, "ch"),
            P(None, "ch"),
            P("ch"),
            P("ch", None),
        ),
        out_specs=(
            P("ch", "lat", "lon"),
            P(None, "ch"),
            P("ch", None),
            P("ch"),
            P(None, None, "ch"),
        ),
        check_vma=False,
    )
```

```python
import functools
import math

import jax
import jax.numpy as jnp
from jax import lax
from jax.experimental import pallas as pl
from jax.experimental.pallas import tpu as pltpu
from jax.sharding import PartitionSpec as P

DIL = 2
LANES = 128
TAP_ROWS = 16
RIDE = 96
BF = jnp.bfloat16
F32 = jnp.float32


def shape(dims, kind):
    return jax.ShapeDtypeStruct(dims, kind)


def call(kernel, outs, args, scratch=(), name=None, flops=0, aliases=None, far=False, after=(), writes=0):
    count = len(args)
    if after:
        body, args = kernel, [*args, *after]

        def kernel(*refs):
            body(*refs[:count], *refs[len(args) :])

    if far:
        args = [pltpu.with_memory_space_constraint(a, pltpu.HBM) for a in args]
    spaces = [pltpu.HBM if far else pl.ANY if i >= count else pltpu.VMEM for i in range(len(args))]
    moved = sum(math.prod(a.shape) * a.dtype.itemsize for a in list(args) + list(outs))
    return pl.pallas_call(
        kernel,
        out_shape=tuple(outs),
        in_specs=[pl.BlockSpec(memory_space=space) for space in spaces],
        out_specs=tuple(
            pl.BlockSpec(memory_space=pl.ANY if i < writes else pltpu.VMEM) for i in range(len(outs))
        ),
        scratch_shapes=list(scratch),
        input_output_aliases=aliases or {},
        name=name,
        compiler_params=pltpu.CompilerParams(vmem_limit_bytes=24 * 1024 * 1024),
        cost_estimate=pl.CostEstimate(flops=flops, bytes_accessed=moved, transcendentals=0),
    )(*args)


def iota(dims, dim):
    return lax.broadcasted_iota(jnp.int32, dims, dim)


def aligned(index):
    return pl.multiple_of(index, 16)


def to_rows(block_ref, weight, scr, pad):
    channels, rows, cols = block_ref.shape

    def body(c, carry):
        value = block_ref[c].astype(F32)
        if weight is not None:
            value = value * weight
        scr[pl.ds(c, rows, stride=pad), :] = value
        return carry

    lax.fori_loop(0, channels, body, 0, unroll=5 if channels % 5 == 0 else 1)
    for c in range(channels, pad):
        scr[pl.ds(c, rows, stride=pad), :] = jnp.zeros((rows, cols), F32)


def pack_columns(value, ext_row, left, right):
    lane = iota(value.shape, 1)
    here = (lane == 2 * ext_row) | (lane == 2 * ext_row + 1)
    size = value.shape[1]
    left = jnp.where(here, pltpu.roll(value, (2 * ext_row) % size, 1), left)
    right = jnp.where(here, pltpu.roll(value, (2 * ext_row + 2) % size, 1), right)
    return left, right


def mirrored(value):
    size = value.shape[1]
    flip = (iota((size, size), 0) + iota((size, size), 1) == size - 1).astype(BF)
    return jnp.dot(value, flip, preferred_element_type=F32).astype(BF)


def emit_strips(read, rows, pad, fold_ref, left_ref, right_ref):
    for t in range(DIL):
        fold_ref[t] = mirrored(read(rows - 1 - t))
    left = jnp.zeros((pad, LANES), F32)
    right = jnp.zeros((pad, LANES), F32)
    for r in range(rows):
        left, right = pack_columns(read(r).astype(F32), r + DIL, left, right)
    left_ref[...] = left.astype(BF)
    right_ref[...] = right.astype(BF)


def strip_shapes(pad):
    return [shape((DIL, pad, LANES), BF)] + [shape((pad, LANES), BF)] * 2


def outer_shapes(pad, swap):
    return [shape((DIL, pad, LANES), BF)] * (1 if swap else 2)


def emit_outer(low, high, t, swap, outer):
    if swap:
        outer[0][t] = jnp.where(lax.axis_index("lat") == 0, high, low).astype(BF)
    else:
        outer[0][t] = low.astype(BF)
        outer[1][t] = high.astype(BF)


def prepare_state(state_ref, mask_ref, rows_ref, fold_ref, left_ref, right_ref, scr):
    rows, pad = rows_ref.shape[:2]
    to_rows(state_ref, mask_ref[...].astype(F32), scr, pad)
    for r in range(rows):
        rows_ref[r] = scr[r * pad : (r + 1) * pad, :].astype(BF)
    emit_strips(lambda r: rows_ref[r], rows, pad, fold_ref, left_ref, right_ref)


def swath_rows(rows, start, offset_ref, value_ref, cols):
    offset = offset_ref[...]
    points = offset.shape[1]
    value = value_ref[...]
    total = jnp.zeros((rows, cols), F32)
    row = lax.shift_right_logical(offset, LANES.bit_length() - 1)
    row_hot = iota((rows, points), 0) + start == row
    col_hot = (iota((cols, points), 0) == (offset & (LANES - 1))).astype(BF)
    for _ in range(3):
        part = value.astype(BF)
        value = value - part.astype(F32)
        lhs = jnp.where(row_hot, part.astype(F32), 0.0).astype(BF)
        total = total + lax.dot_general(
            lhs, col_hot, (((1,), (1,)), ((), ())), preferred_element_type=F32
        )
    return total


def with_first(tile, row):
    lifted = jnp.broadcast_to(row, tile.shape)
    return jnp.where(iota(tile.shape, 0) == 0, tile.astype(F32) + lifted, tile.astype(F32))


def prepare_outer(swap, count, *refs):
    outs, (row_scr, sems) = refs[count:-2], refs[-2:]
    outer, held = outs[:-count], outs[-count:]
    state_ref, mask_ref = held[0:2]
    copies = [pltpu.make_async_copy(refs[k], held[k], sems.at[k]) for k in range(count)]
    for copy in copies:
        copy.start()
    pad = outer[0].shape[1]
    channels, rows, cols = state_ref.shape
    half = rows // 2
    lat = lax.axis_index("lat")
    for c in range(channels, pad):
        row_scr[pl.ds(c, 2 * DIL, stride=pad), :] = jnp.zeros((2 * DIL, cols), F32)
    copies[1].wait()
    copies[0].wait()
    if swap:
        start = aligned((1 - lat) * half)
        mask = mask_ref[pl.ds(start, half), :].astype(F32)

        def body(c, carry):
            value = state_ref[c, pl.ds(start, half), :].astype(F32) * mask
            row_scr[pl.ds(c, DIL, stride=pad), :] = jnp.where(
                lat == 0, value[half - DIL :, :], value[0:DIL, :]
            )
            return carry

    else:
        mask = mask_ref[...].astype(F32)

        def body(c, carry):
            value = state_ref[c].astype(F32) * mask
            row_scr[pl.ds(c, DIL, stride=pad), :] = value[0:DIL, :]
            row_scr[pl.ds(DIL * pad + c, DIL, stride=pad), :] = value[rows - DIL :, :]
            return carry

    lax.fori_loop(0, channels, body, 0, unroll=5 if channels % 5 == 0 else 1)
    for k, to in enumerate(outer):
        for t in range(DIL):
            at = (k * DIL + t) * pad
            to[t] = row_scr[at : at + pad, :].astype(BF)
    for copy in copies[2:]:
        copy.wait()


def prepare_far(part, *refs):
    (mask_ref, grad_ref), weights = refs[0:2], refs[2:6]
    far_ref, tiles_ref, taps_ref = refs[6:9]
    scr, weights_scr, turn_scr, pick_e, pick_p = refs[9:]
    channels, rows, cols = grad_ref.shape
    pad = taps_ref.shape[0]
    weight_picks(part, pad, weights_scr.shape[1], pick_e.shape[0], pick_e, pick_p)
    pack_weights(part, pad, *weights, pick_e, pick_p, weights_scr, taps_ref, turn_scr)
    hid = weights_scr.shape[0]
    full = tiles_ref.shape[0]
    for t in range(full // hid):
        tiles_ref[t * hid : (t + 1) * hid, :] = weights_scr[:, t * LANES : (t + 1) * LANES]
    far_ref[0:full, :] = tiles_ref[...]
    half = rows // 2
    me = lax.axis_index("ch")
    start = aligned((1 - me // 2) * half)

    def body(c, carry):
        scr[pl.ds(c, half, stride=pad), :] = grad_ref[c, pl.ds(start, half), :].astype(F32)
        return carry

    lax.fori_loop(0, channels, body, 0, unroll=5 if channels % 5 == 0 else 1)
    for c in range(channels, pad):
        scr[pl.ds(c, half, stride=pad), :] = jnp.zeros((half, cols), F32)
    mask = mask_ref[pl.ds(start, half), :].astype(F32)
    count_rows = half // 2
    for r in range(half):
        scr[r * pad : (r + 1) * pad, :] = scr[r * pad : (r + 1) * pad, :] * mask[r : r + 1, :]
    for k in range(2):
        first = aligned((((me ^ (2 + k)) % 2) * count_rows) * pad)
        size = count_rows * pad
        far_ref[full + k * size : full + (k + 1) * size, :] = scr[pl.ds(first, size), :].astype(BF)


def prepare_near(mask_ref, grad_ref, offset_ref, value_ref, tiles_ref, rows_ref, own_ref, core_ref, scr):
    rows, pad, cols = rows_ref.shape
    mask = mask_ref[...].astype(F32)
    to_rows(grad_ref, None, scr, pad)
    for r in range(rows):
        rows_ref[r] = (scr[r * pad : (r + 1) * pad, :] * mask[r : r + 1, :]).astype(BF)
    full = tiles_ref.shape[0]
    count = (own_ref.shape[0] - full) // pad
    me = lax.axis_index("ch")
    for k, to in enumerate((own_ref, core_ref)):
        to[0:full, :] = tiles_ref[...]
        for r in range(count):
            at = full + r * pad
            to[at : at + pad, :] = rows_ref[(me ^ k) * count + r]
    swath = swath_rows(rows, 0, offset_ref, value_ref, cols) * mask
    swath = jnp.where(me == 0, swath, 0.0)
    for r in range(rows):
        rows_ref[r, 0:16, :] = with_first(rows_ref[r, 0:16, :], swath[r : r + 1, :]).astype(BF)


def second_half(in_ref, out_ref):
    out_ref[...] = in_ref[1]


def relay(in_ref, out_ref):
    del in_ref, out_ref


def ring(count, step):
    return [(i, (i + step) % count) for i in range(count)]


def finish_columns(rows, swap, *refs):
    if swap:
        strip_ref, fold_ref, left_ref, right_ref, halo_ref, left_out, right_out = refs
        low_ref = high_ref = strip_ref
    else:
        low_ref, high_ref, fold_ref, left_ref, right_ref, halo_ref, left_out, right_out = refs
    lat, count = lax.axis_index("lat"), lax.axis_size("lat")
    left, right = left_ref[...].astype(F32), right_ref[...].astype(F32)
    for t in range(DIL):
        south = jnp.where(lat == 0, 0.0, low_ref[t].astype(F32))
        north = jnp.where(lat == count - 1, fold_ref[t].astype(F32), high_ref[t].astype(F32))
        halo_ref[t] = south.astype(BF)
        halo_ref[DIL + t] = north.astype(BF)
        left, right = pack_columns(south, t, left, right)
        left, right = pack_columns(north, rows + DIL + t, left, right)
    left_out[...] = left.astype(BF)
    right_out[...] = right.astype(BF)


def odd_lon():
    return lax.axis_index("lon") % 2 == 1


def pack_for_third(rows, riding, *refs):
    if riding:
        ride_ref, *refs = refs
    got_ref, fold_ref, left_ref, right_ref, out_ref = refs
    low = lax.axis_index("lat") == 0
    left, right = left_ref[...].astype(F32), right_ref[...].astype(F32)
    for t in range(DIL):
        got = got_ref[t].astype(F32)
        left, right = pack_columns(jnp.where(low, 0.0, got), t, left, right)
        left, right = pack_columns(jnp.where(low, got, 0.0), rows + DIL + t, left, right)
        out_ref[t] = fold_ref[t]
    pack = jnp.where(odd_lon(), right, left)
    if riding:
        pack = pack + pltpu.roll(ride_ref[...].astype(F32), RIDE, 1)
    out_ref[DIL] = pack.astype(BF)


def pack_for_first(rows, got_ref, fold_ref, left_ref, right_ref, third_ref, halo_ref, out_ref, side_ref):
    low = lax.axis_index("lat") == 0
    odd = odd_lon()
    left, right = left_ref[...].astype(F32), right_ref[...].astype(F32)
    side = third_ref[DIL].astype(F32)
    size = side.shape[1]
    lane = iota(side.shape, 1)
    for t in range(DIL):
        got = got_ref[t].astype(F32)
        south = jnp.where(low, 0.0, got)
        north = jnp.where(low, got, third_ref[t].astype(F32))
        halo_ref[t] = south.astype(BF)
        halo_ref[DIL + t] = north.astype(BF)
        left, right = pack_columns(south, t, left, right)
        left, right = pack_columns(north, rows + DIL + t, left, right)
        at = 2 * (rows + DIL + t)
        own = fold_ref[t].astype(F32)
        own = jnp.where(
            odd, pltpu.roll(own, at, 1), pltpu.roll(own, (at - (size - DIL)) % size, 1)
        )
        here = jnp.logical_and((lane == at) | (lane == at + 1), jnp.logical_not(low))
        side = jnp.where(here, own, side)
    out_ref[0] = jnp.where(odd, left, right).astype(BF)
    for k in range(1, out_ref.shape[0]):
        out_ref[k] = jnp.zeros(side.shape, BF)
    side_ref[...] = side.astype(BF)


def two_by_four():
    return lax.axis_size("lat") == 2 and lax.axis_size("lon") == 4


def exchange_halo(rows, strips, outer, swap, name, planes=1, riding=(), after=()):
    n_lat, n_lon = lax.axis_size("lat"), lax.axis_size("lon")
    fold, left, right = strips
    pad = left.shape[0]
    halo_shape, pack = shape((2 * DIL, pad, LANES), BF), shape((pad, LANES), BF)
    if two_by_four():
        got = lax.ppermute(outer[0], "lat", [(0, 1), (1, 0)])
        third_out = call(
            functools.partial(pack_for_third, rows, len(riding) > 0),
            [shape((DIL + 1, pad, LANES), BF)],
            [*riding, got, fold, left, right],
            (),
            name + "_third",
            after=after,
        )[0]
        third = lax.ppermute(third_out, "lon", [(lon, lon ^ 3) for lon in range(n_lon)])
        halo, first, side = call(
            functools.partial(pack_for_first, rows),
            [halo_shape, shape((planes, pad, LANES), BF), pack],
            [got, fold, left, right, third],
            (),
            name + "_first",
        )
        got = lax.ppermute(first, "lon", [(lon, lon ^ 1) for lon in range(n_lon)])
        return (halo, got, side), (third_out, third, first)
    top = n_lat - 1
    fold_pairs = [(lon * n_lat + top, (n_lon - 1 - lon) * n_lat + top) for lon in range(n_lon)]
    if swap:
        moved = [lax.ppermute(outer[0], "lat", [(0, 1), (1, 0)])]
    else:
        moved = [
            lax.ppermute(outer[1], "lat", [(i, i + 1) for i in range(n_lat - 1)]),
            lax.ppermute(outer[0], "lat", [(i + 1, i) for i in range(n_lat - 1)]),
        ]
    fold = lax.ppermute(fold, ("lon", "lat"), fold_pairs)
    halo, left, right = call(
        functools.partial(finish_columns, rows, swap),
        [halo_shape, pack, pack],
        [*moved, fold, left, right],
        (),
        name + "_columns",
    )
    from_right = lax.ppermute(left, "lon", ring(n_lon, -1))
    from_left = lax.ppermute(right, "lon", ring(n_lon, 1))
    return (halo, from_left, from_right), ()


def padded_row(block_ref, halo_ref, at, e):
    rows = block_ref.shape[0]
    if e < DIL:
        return halo_ref[e, at, :]
    if e < rows + DIL:
        return block_ref[e - DIL, at, :]
    return halo_ref[e - rows, at, :]


def sides(left_ref, right_ref, at):
    left = (left_ref[0, at, :] if two_by_four() else left_ref[at, :]).astype(F32)
    right = right_ref[at, :].astype(F32)
    if two_by_four():
        odd = odd_lon()
        left, right = jnp.where(odd, left, right), jnp.where(odd, right, left)
    return left, right


def shifted_rows(rows, read, left, right):
    lane = iota((16, LANES), 1)
    for e in range(rows + 2 * DIL):
        row = read(e).astype(F32)
        west = jnp.where(
            lane < DIL, pltpu.roll(left, (-2 * e) % LANES, 1), pltpu.roll(row, DIL, 1)
        )
        east = jnp.where(
            lane >= LANES - DIL,
            pltpu.roll(right, (LANES - DIL - 2 * e) % LANES, 1),
            pltpu.roll(row, LANES - DIL, 1),
        )
        yield e, (west, row, east)


def stencil_rows(rows, read, left, right, taps, north, emit):
    sums = {}
    for e, shifts in shifted_rows(rows, read, left, right):
        for a in (2, 1, 0):
            r = e - DIL * a
            if not 0 <= r < rows:
                continue
            used = north if e >= rows + DIL else taps[a]
            term = used[0] * shifts[0] + used[1] * shifts[1] + used[2] * shifts[2]
            sums[r] = term if r not in sums else sums[r] + term
            if a == 2:
                emit(r, sums.pop(r))


def stencil(block_ref, halo_ref, left_ref, right_ref, group, taps, north, emit):
    at = pl.ds(aligned(group * 16), 16)
    left, right = sides(left_ref, right_ref, at)
    read = functools.partial(padded_row, block_ref, halo_ref, at)
    stencil_rows(block_ref.shape[0], read, left, right, taps, north, emit)


def spread(tap_ref, group):
    values = tap_ref[pl.ds(aligned(group * 16), 16), :]
    return [
        [jnp.broadcast_to(values[:, 3 * a + b : 3 * a + b + 1], (16, LANES)) for b in range(3)]
        for a in range(3)
    ]


def conv_forward(ones_row, away, block_ref, halo_ref, left_ref, right_ref, tap_ref, *rest):
    outs, (row_scr, left_scr, right_scr, scr) = rest[:-4], rest[-4:]
    rows, pad = block_ref.shape[:2]
    half = rows // 2
    me = lax.axis_index("ch")
    upper = (me // 2 + away) % 2
    west, east = sides(left_ref, right_ref, slice(None))
    left_scr[...] = pltpu.roll(west, (LANES - 2 * half * upper) % LANES, 1)
    right_scr[...] = pltpu.roll(east, (LANES - 2 * half * upper) % LANES, 1)
    for t in range(DIL):
        low, high = halo_ref[t].astype(F32), halo_ref[DIL + t].astype(F32)
        before = block_ref[half - DIL + t].astype(F32)
        behind = block_ref[half + t].astype(F32)
        row_scr[t] = jnp.where(upper == 0, low, before).astype(BF)
        row_scr[half + DIL + t] = jnp.where(upper == 0, behind, high).astype(BF)
    for r in range(half):
        row_scr[DIL + r] = block_ref[upper * half + r]

    def body(group, carry):
        taps = spread(tap_ref, group)
        is_one = iota((16, LANES), 0) + group * 16 == ones_row
        at = pl.ds(aligned(group * 16), 16)

        def emit(r, value):
            value = jnp.where(is_one, 1.0, value)
            scr[r, at, :] = value.astype(BF)

        left, right = left_scr[at, :], right_scr[at, :]
        stencil_rows(half, lambda e: row_scr[e, at, :], left, right, taps, taps[2], emit)
        return carry

    lax.fori_loop(0, pad // 16, body, 0)
    count = half // 2
    size = outs[0].shape[0]
    for k, to in enumerate(outs):
        first = ((me + k % 2) % 2) * count
        to[...] = scr[pl.ds(first + k // 2 * size, size)]


def conv_adjoint(
    block_ref, halo_ref, left_ref, right_ref, tap_ref, cotan_ref, mask_ref, out_ref, mark_ref, scr, done_scr, sems
):
    rows, pad = block_ref.shape[:2]
    channels = out_ref.shape[0]
    at_top = lax.axis_index("lat") == lax.axis_size("lat") - 1
    mask = mask_ref[...].astype(F32)

    def copy(group, count):
        at = pl.ds(group * 16, count)
        return pltpu.make_async_copy(done_scr.at[at], out_ref.at[at], sems.at[group])

    def body(group, count):
        taps = spread(tap_ref, group)
        back = [[taps[2 - a][2 - b] for b in range(3)] for a in range(3)]
        north = [jnp.where(at_top, taps[2][b], back[2][b]) for b in range(3)]

        def emit(r, value):
            cotan = cotan_ref[r, pl.ds(aligned(group * 16), 16), :].astype(F32)
            scr[pl.ds(r, 16, stride=rows + 8), :] = (cotan + value) * mask[r : r + 1, :]

        stencil(block_ref, halo_ref, left_ref, right_ref, group, back, north, emit)
        for c in range(count):
            at = c * (rows + 8)
            done_scr[group * 16 + c] = scr[at : at + rows, :].astype(BF)
        copy(group, count).start()

    whole = channels // 16

    def each(group, carry):
        body(group, 16)
        return carry

    lax.fori_loop(0, whole, each, 0)
    if channels % 16:
        body(whole, channels % 16)
    mark_ref[...] = jnp.zeros(mark_ref.shape, F32)
    for group in range(whole):
        copy(group, 16).wait()
    if channels % 16:
        copy(whole, channels % 16).wait()


def collect_grad(swap, own, near, far, passed, rows_ref, *rest):
    part_rows = own.shape[0]
    rows, pad = rows_ref.shape[:2]
    me = lax.axis_index("ch")
    for k, quarter in enumerate((own, near, far.at[0], passed)):
        rows_ref[pl.ds((me ^ k) * part_rows, part_rows)] = quarter[...]
    strips, outer = rest[:3], rest[3:]
    for t in range(DIL):
        emit_outer(rows_ref[t].astype(F32), rows_ref[rows - DIL + t].astype(F32), t, swap, outer)
    emit_strips(lambda r: rows_ref[r], rows, pad, *strips)


def shift_columns(block_ref, halo_ref, left_ref, right_ref, west_ref, east_ref):
    def body(group, carry):
        at = pl.ds(aligned(group * 16), 16)
        left, right = sides(left_ref, right_ref, at)
        read = functools.partial(padded_row, block_ref, halo_ref, at)
        for e, shifts in shifted_rows(block_ref.shape[0], read, left, right):
            west_ref[e, at, :] = shifts[0].astype(BF)
            east_ref[e, at, :] = shifts[2].astype(BF)
        return carry

    lax.fori_loop(0, block_ref.shape[1] // 16, body, 0)


def kernel_gradient(grad_ref, block_ref, halo_ref, west_ref, east_ref, out_ref):
    rows, pad = grad_ref.shape[:2]

    def body(group, carry):
        at = pl.ds(aligned(group * 16), 16)
        sums = [[jnp.zeros((16, LANES), F32) for _ in range(3)] for _ in range(3)]
        for e in range(rows + 2 * DIL):
            middle = padded_row(block_ref, halo_ref, at, e)
            shifts = [part.astype(F32) for part in (west_ref[e, at, :], middle, east_ref[e, at, :])]
            for a in range(3):
                r = e - DIL * a
                if 0 <= r < rows:
                    grad = grad_ref[r, at, :].astype(F32)
                    for b in range(3):
                        sums[a][b] = sums[a][b] + grad * shifts[b]
        lane = iota((16, LANES), 1)
        out = jnp.zeros((16, LANES), F32)
        for a in range(3):
            for b in range(3):
                total = jnp.sum(sums[a][b], axis=1, keepdims=True)
                out = jnp.where(lane == 3 * a + b, total, out)
        out_ref[at, :] = out.astype(BF)
        return carry

    lax.fori_loop(0, pad // 16, body, 0)


def channel_of(slot, part, pad):
    block = sum((slot >= pad * b).astype(jnp.int32) for b in range(1, 4))
    inside = slot - block * pad
    return jnp.where((slot >= 0) & (slot < 4 * pad) & (inside < part), block * part + inside, -1)


def expand_slot(lane, pad):
    return jnp.where(lane < 4 * pad, lane, -1)


def project_slot(lane, pad, split):
    tail = 4 * pad - split
    low = LANES - tail
    return jnp.where(lane >= LANES, lane - LANES, jnp.where(lane >= low, lane - low + split, -1))


def weight_picks(part, pad, wide, channels, pick_e_ref, pick_p_ref):
    split = 4 * pad // LANES * LANES
    lane = iota((channels, wide), 1)
    row = iota((channels, wide), 0)
    pick_e_ref[...] = (channel_of(expand_slot(lane, pad), part, pad) == row).astype(BF)
    slot = jnp.where(lane >= split, project_slot(lane - split, pad, split), -1)
    pick_p_ref[...] = (channel_of(slot, part, pad) == row).astype(BF)


def output_picks(part, pad, pick_e_ref, pick_p_ref):
    channels, depth = pick_e_ref.shape
    split = 4 * pad // LANES * LANES
    lane, row = iota((channels, depth), 1), iota((channels, depth), 0)
    pick_e_ref[...] = (channel_of(expand_slot(lane, pad), part, pad) == row).astype(BF)
    pick_p_ref[...] = (channel_of(project_slot(lane, pad, split), part, pad) == row).astype(BF)


def pack_weights(
    part, pad, expand_ref, bias_ref, project_ref, kernel_ref, pick_e_ref, pick_p_ref, out_ref, taps_ref, turn_scr
):
    hidden, channels = expand_ref.shape
    turn_scr[...] = jnp.zeros(turn_scr.shape, F32)
    for a in range(3):
        turn_scr[3 * a : 3 * a + 3, 0:part] = kernel_ref[a]
    taps_ref[...] = jnp.transpose(turn_scr[...])[0:pad, :]
    wide = out_ref.shape[1]
    bias = bias_ref[...]
    parts = jnp.zeros((16, hidden), F32)
    at = iota((16, hidden), 0)
    for k in range(3):
        piece = bias.astype(BF).astype(F32)
        bias = bias - piece
        parts = jnp.where(at == k, piece, parts)
    lane, row = iota((16, wide), 1), iota((16, wide), 0)
    pick_b = ((lane == row * pad + part) & (row < 3)).astype(BF)
    turned = (((0,), (0,)), ((), ()))
    packed = (
        jnp.dot(expand_ref[...], pick_e_ref[...], preferred_element_type=F32)
        + lax.dot_general(parts.astype(BF), pick_b, turned, preferred_element_type=F32)
        + jnp.dot(project_ref[...], pick_p_ref[...], preferred_element_type=F32)
    )
    rows = out_ref.shape[0]
    out_ref[0:hidden, :] = packed.astype(BF)
    out_ref[hidden:rows, :] = jnp.zeros((rows - hidden, wide), BF)


GELU_C = math.sqrt(2.0 / math.pi)


def activation_gradient(part, *refs):
    parts, (mask_ref, offset_ref, value_ref) = refs[0:4], refs[4:7]
    act_ref, y_scr, w_scr, t_scr, pick_e_ref, pick_p_ref = refs[7:]
    me = lax.axis_index("ch")
    tiles = w_scr.shape[1] // LANES
    hid = w_scr.shape[0] // 4
    depth, cells = y_scr.shape
    part_rows = cells // LANES
    pad = (parts[0].shape[0] - tiles * hid) // part_rows
    split = 4 * pad // LANES * LANES
    output_picks(part, pad, pick_e_ref, pick_p_ref)
    y_scr[0 : depth - 4 * pad, :] = jnp.zeros((depth - 4 * pad, cells), BF)
    for k, ref in enumerate(parts):
        for t in range(tiles):
            w_scr[k * hid : (k + 1) * hid, t * LANES : (t + 1) * LANES] = ref[
                t * hid : (t + 1) * hid, :
            ]
        block = me ^ k
        start = tiles * hid + (part_rows * pad if k == 3 else 0)
        for r in range(part_rows):
            cols = slice(r * LANES, (r + 1) * LANES)
            for u in range(pad // 16):
                slot = block * pad + 16 * u
                to = jnp.where(slot < split, slot + LANES, slot - split + depth - 4 * pad)
                at = start + r * pad + 16 * u
                y_scr[pl.ds(aligned(to), 16), cols] = ref[at : at + 16, :]
    rows = pl.ds(pl.multiple_of(me * part_rows, part_rows), part_rows)
    swath = swath_rows(part_rows, me * part_rows, offset_ref, value_ref, LANES)
    swath = swath * mask_ref[rows, :].astype(F32)
    for r in range(part_rows):
        at = (slice(LANES, LANES + 16), slice(r * LANES, (r + 1) * LANES))
        y_scr[at] = with_first(y_scr[at], swath[r : r + 1, :]).astype(BF)
    t_scr[...] = jnp.transpose(w_scr[:, 0:depth])
    step = 256
    for start in range(0, cells, step):
        cols = slice(start, start + step)
        act_ref[:, cols] = jnp.dot(
            w_scr[:, split : split + depth], y_scr[:, cols], preferred_element_type=F32
        )


def hidden_gradient(half, *refs):
    xs, (act_ref, y_ref, w_ref), refs = refs[0:4], refs[4:7], refs[7:]
    sums = ()
    if half:
        sums, refs = refs[0:2], refs[2:]
    pre_ref, keep_ref, send_ref, x_scr, value_scr = refs
    part_rows, pad = xs[0].shape[:2]
    hid = w_ref.shape[0] // 4
    split = 4 * pad // LANES * LANES
    depth, cells = x_scr.shape
    offset = half * cells
    me = lax.axis_index("ch")
    x_scr[4 * pad : depth, :] = jnp.zeros((depth - 4 * pad, cells), BF)
    for k in range(4):
        for r in range(part_rows):
            cols = slice(r * LANES, (r + 1) * LANES)
            x_scr[pl.ds(aligned((me ^ k) * pad), pad), cols] = xs[k][r]
    step = 256
    for start in range(0, cells, step):
        cols = slice(start, start + step)
        hidden = jnp.dot(w_ref[:, 0:depth], x_scr[:, cols], preferred_element_type=F32)
        square = hidden * hidden
        tanh = jnp.tanh(hidden * (GELU_C + (0.044715 * GELU_C) * square))
        each = 0.5 + 0.5 * tanh
        slope = each + hidden * (0.5 * GELU_C + (1.5 * 0.044715 * GELU_C) * square) * (
            1.0 - tanh * tanh
        )
        value_scr[:, cols] = (hidden * each).astype(BF)
        pre_ref[:, cols] = (act_ref[:, offset + start : offset + start + step] * slope).astype(BF)
    over_cells = (((1,), (1,)), ((), ()))
    expand = lax.dot_general(pre_ref[...], x_scr[...], over_cells, preferred_element_type=F32)
    project = lax.dot_general(
        value_scr[...], y_ref[:, offset : offset + cells], over_cells, preferred_element_type=F32
    )
    shared = split // LANES
    tiles = [expand[:, t * LANES : (t + 1) * LANES] for t in range(shared)]
    tiles.append(expand[:, split : split + LANES] + project[:, 0:LANES])
    tiles += [project[:, t * LANES : (t + 1) * LANES] for t in range(1, shared + 1)]
    used = len(tiles) * hid
    for ref in (keep_ref, send_ref):
        for k in range(2):
            ref[k, used:, :] = jnp.zeros((ref.shape[1] - used, LANES), ref.dtype)
    for k in range(4):
        to = send_ref if k % 2 else keep_ref
        for t, tile in enumerate(tiles):
            at = (k // 2, slice(t * hid, (t + 1) * hid), slice(None))
            value = tile[k * hid : (k + 1) * hid]
            if half:
                value = value + sums[k % 2][at]
            to[at] = value.astype(to.dtype)


def conv_gradient(away, first_ref, second_ref, t_ref, *rest):
    outs, scr = rest[:-1], rest[-1]
    if away:
        outs = (rest[0].at[0], rest[0].at[1])
    part_rows, pad = outs[0].shape[:2]
    me = lax.axis_index("ch")
    first = ((me // 2 + away) % 2) * 2 * pad
    weights = t_ref[pl.ds(aligned(first), 2 * pad), :]
    step = 256
    half = first_ref.shape[1]
    for start in range(0, 2 * half, step):
        pre = (first_ref if start < half else second_ref)[:, start % half : start % half + step]
        scr[:, start : start + step] = jnp.dot(weights, pre, preferred_element_type=F32).astype(BF)
    for k, to in enumerate(outs):
        at = pl.ds(aligned(((me + k) % 2) * pad), pad)
        for r in range(part_rows):
            to[r] = scr[at, r * LANES : (r + 1) * LANES]


def add_cores(keep_ref, got_ref, own_ref, *sends):
    piece = own_ref.shape[1]
    place = 2 * lax.axis_index("lat") + lax.axis_index("lon") % 2
    for k in range(4):
        at = pl.ds(aligned((place ^ k) * piece), piece)
        for group in range(2):
            total = keep_ref[group, at, :] + got_ref[group, at, :].astype(F32)
            to = sends[k - 1] if k else own_ref
            to[group] = total.astype(to.dtype)


def add_pieces(own_ref, a_ref, b_ref, c_ref, mine_ref, other_ref):
    for group, to in enumerate((mine_ref, other_ref)):
        total = own_ref[group] + (
            a_ref[group].astype(F32) + b_ref[group].astype(F32) + c_ref[group].astype(F32)
        )
        to[...] = total.astype(to.dtype)


def add_across(mine_ref, got_ref, out_ref):
    out_ref[...] = (mine_ref[...] + got_ref[...].astype(F32)).astype(BF)


def finish_pieces(mine_ref, line_ref, kernel_ref, third_ref, out_ref, turn_scr):
    piece, pad = mine_ref.shape[0], kernel_ref.shape[0]
    out_ref[0:piece, :] = (mine_ref[...].astype(F32) + line_ref[...].astype(F32)).astype(BF)
    other = pltpu.roll(third_ref[DIL].astype(F32), LANES - RIDE, 1)
    turn_scr[...] = jnp.zeros(turn_scr.shape, F32)
    turn_scr[0:pad, :] = kernel_ref[...].astype(F32) + other
    out_ref[piece:, :] = jnp.transpose(turn_scr[...])[0:TAP_ROWS, :].astype(BF)


def write_parameters(part, pad, scale, hid, p0, p1, p2, p3, pick_e, pick_p, *rest):
    expand_ref, project_ref, bias_ref, taps_ref, all_scr, taps_scr = rest
    piece = p0.shape[0] - TAP_ROWS
    place = 2 * lax.axis_index("lat") + lax.axis_index("lon") % 2
    for k, ref in enumerate((p0, p1, p2, p3)):
        to = place ^ k
        all_scr[pl.ds(aligned(to * piece), piece), :] = ref[0:piece, :]
        taps_scr[pl.ds(aligned(to * TAP_ROWS), TAP_ROWS), :] = ref[piece:, :].astype(F32)
    unpack(part, pad, scale, hid, all_scr, pick_e, pick_p, expand_ref, project_ref, bias_ref)
    total = taps_scr[0:TAP_ROWS, :]
    for k in range(1, 4):
        total = total + taps_scr[k * TAP_ROWS : (k + 1) * TAP_ROWS, :]
    write_taps(total, scale, taps_ref)


def write_taps(total, scale, taps_ref):
    for a in range(3):
        taps_ref[a] = total[3 * a : 3 * a + 3, 0 : taps_ref.shape[2]] * scale


def unpack(part, pad, scale, hid, all_ref, pick_e, pick_p, expand_ref, project_ref, bias_ref):
    hidden = expand_ref.shape[0]
    split = 4 * pad // LANES * LANES
    shared = split // LANES
    tiles = [all_ref[t * hid : (t + 1) * hid, :] for t in range(2 * shared + 1)]
    depth = (shared + 1) * LANES
    expand = jnp.concatenate(tiles[: shared + 1], axis=1)
    project = jnp.concatenate(tiles[shared:], axis=1)
    pick_b = (iota((16, depth), 1) == part).astype(BF)
    last = (((1,), (1,)), ((), ()))
    dot = functools.partial(lax.dot_general, dimension_numbers=last, preferred_element_type=F32)
    expand_ref[...] = dot(expand, pick_e[...])[0:hidden, :] * scale
    bias_ref[...] = dot(pick_b, expand)[0:1, 0:hidden] * scale
    project_ref[...] = dot(project, pick_p[...])[0:hidden, :] * scale


def unpack_whole(part, pad, scale, hid, all_ref, taps_in, pick_e, pick_p, *rest):
    expand_ref, project_ref, bias_ref, taps_ref, turn_scr = rest
    unpack(part, pad, scale, hid, all_ref, pick_e, pick_p, expand_ref, project_ref, bias_ref)
    turn_scr[...] = jnp.zeros(turn_scr.shape, F32)
    turn_scr[0:pad, :] = taps_in[...]
    write_taps(jnp.transpose(turn_scr[...])[0:TAP_ROWS, :], scale, taps_ref)


def on_device(
    ocean_state,
    land_mask,
    out_grad,
    swath_offset,
    swath_value,
    depth_kernel,
    expand_weight,
    expand_bias,
    project_weight,
):
    part, rows, cols = ocean_state.shape
    n_lon, n_lat, n_ch = lax.axis_size("lon"), lax.axis_size("lat"), lax.axis_size("ch")
    channels, hidden = expand_weight.shape
    assert n_ch == 4 and cols == LANES and rows % n_ch == 0
    pad = (part + 16) // 16 * 16
    hid = (hidden + 15) // 16 * 16
    split = n_ch * pad // LANES * LANES
    tail = n_ch * pad - split
    assert tail == LANES // 2
    wide = 2 * n_ch * pad
    depth = split + LANES
    part_rows = rows // n_ch
    cells = part_rows * cols
    swap = n_lat == 2
    scale = 1.0 / math.sqrt(rows * n_lat * cols * n_lon)
    core = [(i, i ^ 1) for i in range(n_ch)]
    across = [(i, i ^ 2) for i in range(n_ch)]
    block = shape((rows, pad, cols), BF)
    quarter = shape((part_rows, pad, cols), BF)
    flat = pltpu.VMEM((rows * pad, cols), F32)

    turn = pltpu.VMEM((LANES, LANES), F32)

    tile_rows = wide // LANES * hid
    sum_rows = (tile_rows + 63) // 64 * 64
    near_rows, far_rows = tile_rows + part_rows * pad, tile_rows + 2 * part_rows * pad
    fetched = [
        ocean_state,
        land_mask,
        out_grad,
        swath_offset.reshape(1, -1),
        swath_value.reshape(1, -1),
        expand_weight.T,
        expand_bias.reshape(1, hidden),
        project_weight,
        depth_kernel,
    ]
    count = len(fetched)
    outs = call(
        functools.partial(prepare_outer, swap, count),
        outer_shapes(pad, swap) + [shape(a.shape, a.dtype) for a in fetched],
        fetched,
        [pltpu.VMEM((2 * DIL * pad, cols), F32), pltpu.SemaphoreType.DMA((count,))],
        "outer_rows",
        far=True,
    )
    outer, (ocean_state, land_mask, *held) = outs[:-count], outs[-count:]
    to_far, tiles, taps = call(
        functools.partial(prepare_far, part),
        [shape((far_rows, LANES), BF), shape((tile_rows, LANES), BF), shape((pad, LANES), F32)],
        [land_mask, held[0], *held[3:]],
        [
            pltpu.VMEM((rows // 2 * pad, cols), F32),
            pltpu.VMEM((hid, wide), BF),
            turn,
            pltpu.VMEM((channels, wide), BF),
            pltpu.VMEM((channels, wide), BF),
        ],
        "far_rows",
    )
    masked, *strips = call(
        prepare_state,
        [block] + strip_shapes(pad),
        [ocean_state, land_mask],
        [flat],
        "state_rows",
        after=[taps],
    )
    cotan, own, to_core = call(
        prepare_near,
        [block, shape((near_rows, LANES), BF), shape((near_rows, LANES), BF)],
        [land_mask, *held[0:3], tiles],
        [flat],
        "cotan_rows",
    )
    around, _ = exchange_halo(rows, strips, outer, swap, "state", after=[to_core])
    from_far = lax.ppermute(to_far, "ch", across)
    ones = functools.partial(conv_forward, part)
    conv_operands = [masked, *around, taps]
    conv_scratch = [
        pltpu.VMEM((rows // 2 + 2 * DIL, pad, cols), BF),
        pltpu.VMEM((pad, LANES), F32),
        pltpu.VMEM((pad, LANES), F32),
        pltpu.VMEM((rows // 2, pad, cols), BF),
    ]
    eighth = shape((part_rows // 2, pad, cols), BF)
    conv_far = call(
        functools.partial(ones, 1), [eighth] * 4, conv_operands, conv_scratch, "conv_away"
    )
    from_far = call(
        relay, [from_far], [from_far], (), "cotan_relay", aliases={0: 0}, after=around[1:2]
    )[0]
    passed = lax.ppermute(from_far, "ch", core)
    conv_near = call(
        functools.partial(ones, 0),
        [eighth] * 4,
        conv_operands,
        conv_scratch,
        "conv_here",
        after=[conv_far[0], passed],
    )
    both = [(i, i ^ 3) for i in range(n_ch)]
    halves = [
        [
            conv_near[2 * h],
            lax.ppermute(conv_near[2 * h + 1], "ch", core),
            lax.ppermute(conv_far[2 * h], "ch", across),
            lax.ppermute(conv_far[2 * h + 1], "ch", both),
        ]
        for h in range(2)
    ]
    act_grad, cotan_all, weights_all, weights_turned, *picks = call(
        functools.partial(activation_gradient, part),
        [
            shape((n_ch * hid, cells), F32),
            shape((depth, cells), BF),
            shape((n_ch * hid, wide), BF),
            shape((depth, n_ch * hid), BF),
            shape((channels, depth), BF),
            shape((channels, depth), BF),
        ],
        [own, lax.ppermute(to_core, "ch", core), from_far, passed, land_mask, *held[1:3]],
        (),
        "activation_gradient",
    )
    pre_grad, sums = [], ()
    for h in range(2):
        pre, *sums = call(
            functools.partial(hidden_gradient, h),
            [
                shape((n_ch * hid, cells // 2), BF),
                shape((2, sum_rows, LANES), F32),
                shape((2, sum_rows, LANES), BF if h else F32),
            ],
            [*halves[h], act_grad, cotan_all, weights_all, *sums],
            [pltpu.VMEM((depth, cells // 2), BF), pltpu.VMEM((n_ch * hid, cells // 2), BF)],
            "hidden_first" if h == 0 else "hidden_second",
        )
        pre_grad.append(pre)
    keep, send = sums
    got = lax.ppermute(send, "ch", core)
    grad_scratch = [pltpu.VMEM((2 * pad, cells), BF)]
    grad_far = call(
        functools.partial(conv_gradient, 1),
        [shape((2, part_rows, pad, cols), BF)],
        [*pre_grad, weights_turned],
        grad_scratch,
        "gradient_away",
    )[0]
    grad_own, grad_core = call(
        functools.partial(conv_gradient, 0),
        [quarter] * 2,
        [*pre_grad, weights_turned],
        grad_scratch,
        "gradient_here",
        after=[grad_far],
    )
    grad_near = lax.ppermute(grad_core, "ch", core)
    grad_far = lax.ppermute(grad_far, "ch", across)
    staged = two_by_four()
    padded = shape((rows + 2 * DIL, pad, cols), BF)
    if not staged:
        shifted = call(shift_columns, [padded, padded], [masked, *around], (), "shift_columns")
    if staged:
        piece = sum_rows // 4
        mine, *sends = call(
            add_cores,
            [shape((2, piece, LANES), F32)] + [shape((2, piece, LANES), BF)] * 3,
            [keep, got],
            (),
            "add_cores",
        )

        shifted = call(
            shift_columns, [padded, padded], [masked, *around], (), "shift_columns", after=sends[:1]
        )

        def turn_plane(k):
            pairs = []
            for lon in range(n_lon):
                for lat in range(n_lat):
                    pairs.append((lon * n_lat + lat, (lon ^ (k & 1)) * n_lat + (lat ^ (k >> 1))))
            return pairs

        def over_plane(values):
            return [lax.ppermute(values[k - 1], ("lon", "lat"), turn_plane(k)) for k in (1, 2, 3)]

        mine, other = call(
            add_pieces,
            [shape((piece, LANES), F32), shape((piece, LANES), BF)],
            [mine, *over_plane(sends)],
            (),
            "add_pieces",
            after=[grad_near, shifted[0]],
        )
    passed = call(
        second_half, [quarter], [grad_far], (), "grad_half", after=[other] if staged else []
    )[0]
    conv_grad, *grad_strips = call(
        functools.partial(collect_grad, swap),
        [block] + strip_shapes(pad) + outer_shapes(pad, swap),
        [grad_own, grad_near, grad_far, lax.ppermute(passed, "ch", core)],
        (),
        "grad_rows",
    )
    kernel_part = call(
        kernel_gradient,
        [shape((pad, LANES), BF)],
        [conv_grad, masked, around[0], *shifted],
        (),
        "kernel_gradient",
    )[0]
    grad_around, marks = exchange_halo(rows, grad_strips[:3], grad_strips[3:], swap, "grad", planes=4, riding=[kernel_part])
    if staged:
        mine = call(
            add_across,
            [shape((piece, LANES), BF)],
            [mine, lax.ppermute(other, "ch", across)],
            (),
            "add_across",
        )[0]
    state_grad, mark = call(
        conv_adjoint,
        [shape((part, rows, cols), BF), shape((8, LANES), F32)],
        [conv_grad, *grad_around, taps, cotan, land_mask],
        [
            pltpu.VMEM((16 * (rows + 8), cols), F32),
            pltpu.VMEM((part, rows, cols), BF),
            pltpu.SemaphoreType.DMA((-(-part // 16),)),
        ],
        "conv_adjoint",
        writes=1,
    )
    outs = [
        shape((hidden, channels), F32),
        shape((hidden, channels), F32),
        shape((1, hidden), F32),
        shape((3, 3, part), F32),
    ]
    if staged:
        far_lon = [(lon, lon ^ 2) for lon in range(n_lon)]
        summed = call(
            finish_pieces,
            [shape((piece + TAP_ROWS, LANES), BF)],
            [
                mine,
                lax.ppermute(mine, "lon", far_lon),
                kernel_part,
                marks[1],
            ],
            [turn],
            "finish_pieces",
            after=marks[2:],
        )[0]
        expand_grad, project_grad, bias_grad, kernel_grad = call(
            functools.partial(write_parameters, part, pad, scale, hid),
            outs,
            [summed, *over_plane([summed] * 3), *picks],
            [pltpu.VMEM((sum_rows, LANES), BF), pltpu.VMEM((4 * TAP_ROWS, LANES), F32)],
            "write_parameters",
            after=[mark],
        )
    else:
        total = keep + got.astype(F32)
        total = total[0] + lax.ppermute(total[1].astype(BF), "ch", across).astype(F32)
        total, kernel_sum = lax.psum((total, kernel_part.astype(F32)), ("lon", "lat"))
        expand_grad, project_grad, bias_grad, kernel_grad = call(
            functools.partial(unpack_whole, part, pad, scale, hid),
            outs,
            [total.astype(BF), kernel_sum, *picks],
            [turn],
            "write_parameters",
        )
    return (
        state_grad,
        expand_grad.T,
        project_grad,
        bias_grad.reshape(hidden),
        kernel_grad,
    )


def solution(mesh):
    return jax.shard_map(
        on_device,
        mesh=mesh,
        in_specs=(
            P("ch", "lat", "lon"),
            P("lat", "lon"),
            P("ch", "lat", "lon"),
            P("lat", "lon", None),
            P("lat", "lon", None),
            P(None, None, "ch"),
            P(None, "ch"),
            P("ch"),
            P("ch", None),
        ),
        out_specs=(
            P("ch", "lat", "lon"),
            P(None, "ch"),
            P("ch", None),
            P("ch"),
            P(None, None, "ch"),
        ),
        check_vma=False,
    )
```

```python
import functools
import math

import jax
import jax.numpy as jnp
from jax import lax
from jax.experimental import pallas as pl
from jax.experimental.pallas import tpu as pltpu
from jax.sharding import PartitionSpec as P

DIL = 2
LANES = 128
TAP_ROWS = 16
RIDE = 96
BF = jnp.bfloat16
F32 = jnp.float32


def shape(dims, kind):
    return jax.ShapeDtypeStruct(dims, kind)


def call(kernel, outs, args, scratch=(), name=None, flops=0, aliases=None, far=False, after=(), writes=0):
    count = len(args)
    if after:
        body, args = kernel, [*args, *after]

        def kernel(*refs):
            body(*refs[:count], *refs[len(args) :])

    if far:
        args = [pltpu.with_memory_space_constraint(a, pltpu.HBM) for a in args]
    spaces = [pltpu.HBM if far else pl.ANY if i >= count else pltpu.VMEM for i in range(len(args))]
    moved = sum(math.prod(a.shape) * a.dtype.itemsize for a in list(args) + list(outs))
    return pl.pallas_call(
        kernel,
        out_shape=tuple(outs),
        in_specs=[pl.BlockSpec(memory_space=space) for space in spaces],
        out_specs=tuple(
            pl.BlockSpec(memory_space=pl.ANY if i < writes else pltpu.VMEM) for i in range(len(outs))
        ),
        scratch_shapes=list(scratch),
        input_output_aliases=aliases or {},
        name=name,
        compiler_params=pltpu.CompilerParams(vmem_limit_bytes=24 * 1024 * 1024),
        cost_estimate=pl.CostEstimate(flops=flops, bytes_accessed=moved, transcendentals=0),
    )(*args)


def iota(dims, dim):
    return lax.broadcasted_iota(jnp.int32, dims, dim)


def aligned(index):
    return pl.multiple_of(index, 16)


def to_rows(block_ref, weight, scr, pad):
    channels, rows, cols = block_ref.shape

    def body(c, carry):
        value = block_ref[c].astype(F32)
        if weight is not None:
            value = value * weight
        scr[pl.ds(c, rows, stride=pad), :] = value
        return carry

    lax.fori_loop(0, channels, body, 0, unroll=5 if channels % 5 == 0 else 1)
    for c in range(channels, pad):
        scr[pl.ds(c, rows, stride=pad), :] = jnp.zeros((rows, cols), F32)


def pack_columns(value, ext_row, left, right):
    lane = iota(value.shape, 1)
    here = (lane == 2 * ext_row) | (lane == 2 * ext_row + 1)
    size = value.shape[1]
    left = jnp.where(here, pltpu.roll(value, (2 * ext_row) % size, 1), left)
    right = jnp.where(here, pltpu.roll(value, (2 * ext_row + 2) % size, 1), right)
    return left, right


def mirrored(value):
    size = value.shape[1]
    flip = (iota((size, size), 0) + iota((size, size), 1) == size - 1).astype(BF)
    return jnp.dot(value, flip, preferred_element_type=F32).astype(BF)


def emit_strips(read, rows, pad, fold_ref, left_ref, right_ref):
    for t in range(DIL):
        fold_ref[t] = mirrored(read(rows - 1 - t))
    left = jnp.zeros((pad, LANES), F32)
    right = jnp.zeros((pad, LANES), F32)
    for r in range(rows):
        left, right = pack_columns(read(r).astype(F32), r + DIL, left, right)
    left_ref[...] = left.astype(BF)
    right_ref[...] = right.astype(BF)


def strip_shapes(pad):
    return [shape((DIL, pad, LANES), BF)] + [shape((pad, LANES), BF)] * 2


def outer_shapes(pad, swap):
    return [shape((DIL, pad, LANES), BF)] * (1 if swap else 2)


def emit_outer(low, high, t, swap, outer):
    if swap:
        outer[0][t] = jnp.where(lax.axis_index("lat") == 0, high, low).astype(BF)
    else:
        outer[0][t] = low.astype(BF)
        outer[1][t] = high.astype(BF)


def prepare_state(state_ref, mask_ref, rows_ref, fold_ref, left_ref, right_ref, scr):
    rows, pad = rows_ref.shape[:2]
    to_rows(state_ref, mask_ref[...].astype(F32), scr, pad)
    for r in range(rows):
        rows_ref[r] = scr[r * pad : (r + 1) * pad, :].astype(BF)
    emit_strips(lambda r: rows_ref[r], rows, pad, fold_ref, left_ref, right_ref)


def swath_rows(rows, start, offset_ref, value_ref, cols):
    offset = offset_ref[...]
    points = offset.shape[1]
    value = value_ref[...]
    total = jnp.zeros((rows, cols), F32)
    row = lax.shift_right_logical(offset, LANES.bit_length() - 1)
    row_hot = iota((rows, points), 0) + start == row
    col_hot = (iota((cols, points), 0) == (offset & (LANES - 1))).astype(BF)
    for _ in range(3):
        part = value.astype(BF)
        value = value - part.astype(F32)
        lhs = jnp.where(row_hot, part.astype(F32), 0.0).astype(BF)
        total = total + lax.dot_general(
            lhs, col_hot, (((1,), (1,)), ((), ())), preferred_element_type=F32
        )
    return total


def with_first(tile, row):
    lifted = jnp.broadcast_to(row, tile.shape)
    return jnp.where(iota(tile.shape, 0) == 0, tile.astype(F32) + lifted, tile.astype(F32))


def prepare_outer(swap, count, *refs):
    outs, (row_scr, sems) = refs[count:-2], refs[-2:]
    outer, held = outs[:-count], outs[-count:]
    state_ref, mask_ref = held[0:2]
    copies = [pltpu.make_async_copy(refs[k], held[k], sems.at[k]) for k in range(count)]
    for copy in copies:
        copy.start()
    pad = outer[0].shape[1]
    channels, rows, cols = state_ref.shape
    half = rows // 2
    lat = lax.axis_index("lat")
    for c in range(channels, pad):
        row_scr[pl.ds(c, 2 * DIL, stride=pad), :] = jnp.zeros((2 * DIL, cols), F32)
    copies[1].wait()
    copies[0].wait()
    if swap:
        start = aligned((1 - lat) * half)
        mask = mask_ref[pl.ds(start, half), :].astype(F32)

        def body(c, carry):
            value = state_ref[c, pl.ds(start, half), :].astype(F32) * mask
            row_scr[pl.ds(c, DIL, stride=pad), :] = jnp.where(
                lat == 0, value[half - DIL :, :], value[0:DIL, :]
            )
            return carry

    else:
        mask = mask_ref[...].astype(F32)

        def body(c, carry):
            value = state_ref[c].astype(F32) * mask
            row_scr[pl.ds(c, DIL, stride=pad), :] = value[0:DIL, :]
            row_scr[pl.ds(DIL * pad + c, DIL, stride=pad), :] = value[rows - DIL :, :]
            return carry

    lax.fori_loop(0, channels, body, 0, unroll=5 if channels % 5 == 0 else 1)
    for k, to in enumerate(outer):
        for t in range(DIL):
            at = (k * DIL + t) * pad
            to[t] = row_scr[at : at + pad, :].astype(BF)
    for copy in copies[2:]:
        copy.wait()


def prepare_far(part, *refs):
    (mask_ref, grad_ref), weights = refs[0:2], refs[2:6]
    far_ref, tiles_ref, taps_ref = refs[6:9]
    scr, weights_scr, turn_scr, pick_e, pick_p = refs[9:]
    channels, rows, cols = grad_ref.shape
    pad = taps_ref.shape[0]
    weight_picks(part, pad, weights_scr.shape[1], pick_e.shape[0], pick_e, pick_p)
    pack_weights(part, pad, *weights, pick_e, pick_p, weights_scr, taps_ref, turn_scr)
    hid = weights_scr.shape[0]
    full = tiles_ref.shape[0]
    for t in range(full // hid):
        tiles_ref[t * hid : (t + 1) * hid, :] = weights_scr[:, t * LANES : (t + 1) * LANES]
    far_ref[0:full, :] = tiles_ref[...]
    half = rows // 2
    me = lax.axis_index("ch")
    start = aligned((1 - me // 2) * half)

    def body(c, carry):
        scr[pl.ds(c, half, stride=pad), :] = grad_ref[c, pl.ds(start, half), :].astype(F32)
        return carry

    lax.fori_loop(0, channels, body, 0, unroll=5 if channels % 5 == 0 else 1)
    for c in range(channels, pad):
        scr[pl.ds(c, half, stride=pad), :] = jnp.zeros((half, cols), F32)
    mask = mask_ref[pl.ds(start, half), :].astype(F32)
    count_rows = half // 2
    for r in range(half):
        scr[r * pad : (r + 1) * pad, :] = scr[r * pad : (r + 1) * pad, :] * mask[r : r + 1, :]
    for k in range(2):
        first = aligned((((me ^ (2 + k)) % 2) * count_rows) * pad)
        size = count_rows * pad
        far_ref[full + k * size : full + (k + 1) * size, :] = scr[pl.ds(first, size), :].astype(BF)


def prepare_near(mask_ref, grad_ref, offset_ref, value_ref, tiles_ref, rows_ref, own_ref, core_ref, scr):
    rows, pad, cols = rows_ref.shape
    mask = mask_ref[...].astype(F32)
    to_rows(grad_ref, None, scr, pad)
    for r in range(rows):
        rows_ref[r] = (scr[r * pad : (r + 1) * pad, :] * mask[r : r + 1, :]).astype(BF)
    full = tiles_ref.shape[0]
    count = (own_ref.shape[0] - full) // pad
    me = lax.axis_index("ch")
    for k, to in enumerate((own_ref, core_ref)):
        to[0:full, :] = tiles_ref[...]
        for r in range(count):
            at = full + r * pad
            to[at : at + pad, :] = rows_ref[(me ^ k) * count + r]
    swath = swath_rows(rows, 0, offset_ref, value_ref, cols) * mask
    swath = jnp.where(me == 0, swath, 0.0)
    for r in range(rows):
        rows_ref[r, 0:16, :] = with_first(rows_ref[r, 0:16, :], swath[r : r + 1, :]).astype(BF)


def second_half(in_ref, out_ref):
    out_ref[...] = in_ref[1]


def relay(in_ref, out_ref):
    del in_ref, out_ref


def ring(count, step):
    return [(i, (i + step) % count) for i in range(count)]


def finish_columns(rows, swap, *refs):
    if swap:
        strip_ref, fold_ref, left_ref, right_ref, halo_ref, left_out, right_out = refs
        low_ref = high_ref = strip_ref
    else:
        low_ref, high_ref, fold_ref, left_ref, right_ref, halo_ref, left_out, right_out = refs
    lat, count = lax.axis_index("lat"), lax.axis_size("lat")
    left, right = left_ref[...].astype(F32), right_ref[...].astype(F32)
    for t in range(DIL):
        south = jnp.where(lat == 0, 0.0, low_ref[t].astype(F32))
        north = jnp.where(lat == count - 1, fold_ref[t].astype(F32), high_ref[t].astype(F32))
        halo_ref[t] = south.astype(BF)
        halo_ref[DIL + t] = north.astype(BF)
        left, right = pack_columns(south, t, left, right)
        left, right = pack_columns(north, rows + DIL + t, left, right)
    left_out[...] = left.astype(BF)
    right_out[...] = right.astype(BF)


def odd_lon():
    return lax.axis_index("lon") % 2 == 1


def pack_for_third(rows, riding, *refs):
    if riding:
        ride_ref, *refs = refs
    got_ref, fold_ref, left_ref, right_ref, out_ref = refs
    low = lax.axis_index("lat") == 0
    left, right = left_ref[...].astype(F32), right_ref[...].astype(F32)
    for t in range(DIL):
        got = got_ref[t].astype(F32)
        left, right = pack_columns(jnp.where(low, 0.0, got), t, left, right)
        left, right = pack_columns(jnp.where(low, got, 0.0), rows + DIL + t, left, right)
        out_ref[t] = fold_ref[t]
    pack = jnp.where(odd_lon(), right, left)
    if riding:
        pack = pack + pltpu.roll(ride_ref[...].astype(F32), RIDE, 1)
    out_ref[DIL] = pack.astype(BF)


def pack_for_first(rows, got_ref, fold_ref, left_ref, right_ref, third_ref, halo_ref, out_ref, side_ref):
    low = lax.axis_index("lat") == 0
    odd = odd_lon()
    left, right = left_ref[...].astype(F32), right_ref[...].astype(F32)
    side = third_ref[DIL].astype(F32)
    size = side.shape[1]
    lane = iota(side.shape, 1)
    for t in range(DIL):
        got = got_ref[t].astype(F32)
        south = jnp.where(low, 0.0, got)
        north = jnp.where(low, got, third_ref[t].astype(F32))
        halo_ref[t] = south.astype(BF)
        halo_ref[DIL + t] = north.astype(BF)
        left, right = pack_columns(south, t, left, right)
        left, right = pack_columns(north, rows + DIL + t, left, right)
        at = 2 * (rows + DIL + t)
        own = fold_ref[t].astype(F32)
        own = jnp.where(
            odd, pltpu.roll(own, at, 1), pltpu.roll(own, (at - (size - DIL)) % size, 1)
        )
        here = jnp.logical_and((lane == at) | (lane == at + 1), jnp.logical_not(low))
        side = jnp.where(here, own, side)
    out_ref[0] = jnp.where(odd, left, right).astype(BF)
    for k in range(1, out_ref.shape[0]):
        out_ref[k] = jnp.zeros(side.shape, BF)
    side_ref[...] = side.astype(BF)


def two_by_four():
    return lax.axis_size("lat") == 2 and lax.axis_size("lon") == 4


def exchange_halo(rows, strips, outer, swap, name, planes=1, riding=(), after=()):
    n_lat, n_lon = lax.axis_size("lat"), lax.axis_size("lon")
    fold, left, right = strips
    pad = left.shape[0]
    halo_shape, pack = shape((2 * DIL, pad, LANES), BF), shape((pad, LANES), BF)
    if two_by_four():
        got = lax.ppermute(outer[0], "lat", [(0, 1), (1, 0)])
        third_out = call(
            functools.partial(pack_for_third, rows, len(riding) > 0),
            [shape((DIL + 1, pad, LANES), BF)],
            [*riding, got, fold, left, right],
            (),
            name + "_third",
            after=after,
        )[0]
        third = lax.ppermute(third_out, "lon", [(lon, lon ^ 3) for lon in range(n_lon)])
        halo, first, side = call(
            functools.partial(pack_for_first, rows),
            [halo_shape, shape((planes, pad, LANES), BF), pack],
            [got, fold, left, right, third],
            (),
            name + "_first",
        )
        got = lax.ppermute(first, "lon", [(lon, lon ^ 1) for lon in range(n_lon)])
        return (halo, got, side), (third_out, third, first)
    top = n_lat - 1
    fold_pairs = [(lon * n_lat + top, (n_lon - 1 - lon) * n_lat + top) for lon in range(n_lon)]
    if swap:
        moved = [lax.ppermute(outer[0], "lat", [(0, 1), (1, 0)])]
    else:
        moved = [
            lax.ppermute(outer[1], "lat", [(i, i + 1) for i in range(n_lat - 1)]),
            lax.ppermute(outer[0], "lat", [(i + 1, i) for i in range(n_lat - 1)]),
        ]
    fold = lax.ppermute(fold, ("lon", "lat"), fold_pairs)
    halo, left, right = call(
        functools.partial(finish_columns, rows, swap),
        [halo_shape, pack, pack],
        [*moved, fold, left, right],
        (),
        name + "_columns",
    )
    from_right = lax.ppermute(left, "lon", ring(n_lon, -1))
    from_left = lax.ppermute(right, "lon", ring(n_lon, 1))
    return (halo, from_left, from_right), ()


def padded_row(block_ref, halo_ref, at, e):
    rows = block_ref.shape[0]
    if e < DIL:
        return halo_ref[e, at, :]
    if e < rows + DIL:
        return block_ref[e - DIL, at, :]
    return halo_ref[e - rows, at, :]


def sides(left_ref, right_ref, at):
    left = (left_ref[0, at, :] if two_by_four() else left_ref[at, :]).astype(F32)
    right = right_ref[at, :].astype(F32)
    if two_by_four():
        odd = odd_lon()
        left, right = jnp.where(odd, left, right), jnp.where(odd, right, left)
    return left, right


def shifted_rows(rows, read, left, right):
    lane = iota((16, LANES), 1)
    for e in range(rows + 2 * DIL):
        row = read(e).astype(F32)
        west = jnp.where(
            lane < DIL, pltpu.roll(left, (-2 * e) % LANES, 1), pltpu.roll(row, DIL, 1)
        )
        east = jnp.where(
            lane >= LANES - DIL,
            pltpu.roll(right, (LANES - DIL - 2 * e) % LANES, 1),
            pltpu.roll(row, LANES - DIL, 1),
        )
        yield e, (west, row, east)


def stencil_rows(rows, read, left, right, taps, north, emit):
    sums = {}
    for e, shifts in shifted_rows(rows, read, left, right):
        for a in (2, 1, 0):
            r = e - DIL * a
            if not 0 <= r < rows:
                continue
            used = north if e >= rows + DIL else taps[a]
            term = used[0] * shifts[0] + used[1] * shifts[1] + used[2] * shifts[2]
            sums[r] = term if r not in sums else sums[r] + term
            if a == 2:
                emit(r, sums.pop(r))


def stencil(block_ref, halo_ref, left_ref, right_ref, group, taps, north, emit):
    at = pl.ds(aligned(group * 16), 16)
    left, right = sides(left_ref, right_ref, at)
    read = functools.partial(padded_row, block_ref, halo_ref, at)
    stencil_rows(block_ref.shape[0], read, left, right, taps, north, emit)


def spread(tap_ref, group):
    values = tap_ref[pl.ds(aligned(group * 16), 16), :]
    return [
        [jnp.broadcast_to(values[:, 3 * a + b : 3 * a + b + 1], (16, LANES)) for b in range(3)]
        for a in range(3)
    ]


def conv_forward(ones_row, away, block_ref, halo_ref, left_ref, right_ref, tap_ref, *rest):
    outs, (row_scr, left_scr, right_scr, scr) = rest[:-4], rest[-4:]
    rows, pad = block_ref.shape[:2]
    half = rows // 2
    me = lax.axis_index("ch")
    upper = (me // 2 + away) % 2
    west, east = sides(left_ref, right_ref, slice(None))
    left_scr[...] = pltpu.roll(west, (LANES - 2 * half * upper) % LANES, 1)
    right_scr[...] = pltpu.roll(east, (LANES - 2 * half * upper) % LANES, 1)
    for t in range(DIL):
        low, high = halo_ref[t].astype(F32), halo_ref[DIL + t].astype(F32)
        before = block_ref[half - DIL + t].astype(F32)
        behind = block_ref[half + t].astype(F32)
        row_scr[t] = jnp.where(upper == 0, low, before).astype(BF)
        row_scr[half + DIL + t] = jnp.where(upper == 0, behind, high).astype(BF)
    for r in range(half):
        row_scr[DIL + r] = block_ref[upper * half + r]

    def body(group, carry):
        taps = spread(tap_ref, group)
        is_one = iota((16, LANES), 0) + group * 16 == ones_row
        at = pl.ds(aligned(group * 16), 16)

        def emit(r, value):
            value = jnp.where(is_one, 1.0, value)
            scr[r, at, :] = value.astype(BF)

        left, right = left_scr[at, :], right_scr[at, :]
        stencil_rows(half, lambda e: row_scr[e, at, :], left, right, taps, taps[2], emit)
        return carry

    lax.fori_loop(0, pad // 16, body, 0)
    count = half // 2
    size = outs[0].shape[0]
    for k, to in enumerate(outs):
        first = ((me + k % 2) % 2) * count
        to[...] = scr[pl.ds(first + k // 2 * size, size)]


def conv_adjoint(
    block_ref, halo_ref, left_ref, right_ref, tap_ref, cotan_ref, mask_ref, out_ref, mark_ref, scr, done_scr, sems
):
    rows, pad = block_ref.shape[:2]
    channels = out_ref.shape[0]
    at_top = lax.axis_index("lat") == lax.axis_size("lat") - 1
    mask = mask_ref[...].astype(F32)

    def copy(group, count):
        at = pl.ds(group * 16, count)
        return pltpu.make_async_copy(done_scr.at[at], out_ref.at[at], sems.at[group])

    def body(group, count):
        taps = spread(tap_ref, group)
        back = [[taps[2 - a][2 - b] for b in range(3)] for a in range(3)]
        north = [jnp.where(at_top, taps[2][b], back[2][b]) for b in range(3)]

        def emit(r, value):
            cotan = cotan_ref[r, pl.ds(aligned(group * 16), 16), :].astype(F32)
            scr[pl.ds(r, 16, stride=rows + 8), :] = (cotan + value) * mask[r : r + 1, :]

        stencil(block_ref, halo_ref, left_ref, right_ref, group, back, north, emit)
        for c in range(count):
            at = c * (rows + 8)
            done_scr[group * 16 + c] = scr[at : at + rows, :].astype(BF)
        copy(group, count).start()

    whole = channels // 16

    def each(group, carry):
        body(group, 16)
        return carry

    lax.fori_loop(0, whole, each, 0)
    if channels % 16:
        body(whole, channels % 16)
    mark_ref[...] = jnp.zeros(mark_ref.shape, F32)
    for group in range(whole):
        copy(group, 16).wait()
    if channels % 16:
        copy(whole, channels % 16).wait()


def collect_grad(swap, own, near, far, passed, rows_ref, *rest):
    part_rows = own.shape[0]
    rows, pad = rows_ref.shape[:2]
    me = lax.axis_index("ch")
    for k, quarter in enumerate((own, near, far.at[0], passed)):
        rows_ref[pl.ds((me ^ k) * part_rows, part_rows)] = quarter[...]
    strips, outer = rest[:3], rest[3:]
    for t in range(DIL):
        emit_outer(rows_ref[t].astype(F32), rows_ref[rows - DIL + t].astype(F32), t, swap, outer)
    emit_strips(lambda r: rows_ref[r], rows, pad, *strips)


def shift_columns(block_ref, halo_ref, left_ref, right_ref, west_ref, east_ref):
    def body(group, carry):
        at = pl.ds(aligned(group * 16), 16)
        left, right = sides(left_ref, right_ref, at)
        read = functools.partial(padded_row, block_ref, halo_ref, at)
        for e, shifts in shifted_rows(block_ref.shape[0], read, left, right):
            west_ref[e, at, :] = shifts[0].astype(BF)
            east_ref[e, at, :] = shifts[2].astype(BF)
        return carry

    lax.fori_loop(0, block_ref.shape[1] // 16, body, 0)


def kernel_gradient(grad_ref, block_ref, halo_ref, west_ref, east_ref, out_ref):
    rows, pad = grad_ref.shape[:2]

    def body(group, carry):
        at = pl.ds(aligned(group * 16), 16)
        sums = [[jnp.zeros((16, LANES), F32) for _ in range(3)] for _ in range(3)]
        for e in range(rows + 2 * DIL):
            middle = padded_row(block_ref, halo_ref, at, e)
            shifts = [part.astype(F32) for part in (west_ref[e, at, :], middle, east_ref[e, at, :])]
            for a in range(3):
                r = e - DIL * a
                if 0 <= r < rows:
                    grad = grad_ref[r, at, :].astype(F32)
                    for b in range(3):
                        sums[a][b] = sums[a][b] + grad * shifts[b]
        lane = iota((16, LANES), 1)
        out = jnp.zeros((16, LANES), F32)
        for a in range(3):
            for b in range(3):
                total = jnp.sum(sums[a][b], axis=1, keepdims=True)
                out = jnp.where(lane == 3 * a + b, total, out)
        out_ref[at, :] = out.astype(BF)
        return carry

    lax.fori_loop(0, pad // 16, body, 0)


def channel_of(slot, part, pad):
    block = sum((slot >= pad * b).astype(jnp.int32) for b in range(1, 4))
    inside = slot - block * pad
    return jnp.where((slot >= 0) & (slot < 4 * pad) & (inside < part), block * part + inside, -1)


def expand_slot(lane, pad):
    return jnp.where(lane < 4 * pad, lane, -1)


def project_slot(lane, pad, split):
    tail = 4 * pad - split
    low = LANES - tail
    return jnp.where(lane >= LANES, lane - LANES, jnp.where(lane >= low, lane - low + split, -1))


def weight_picks(part, pad, wide, channels, pick_e_ref, pick_p_ref):
    split = 4 * pad // LANES * LANES
    lane = iota((channels, wide), 1)
    row = iota((channels, wide), 0)
    pick_e_ref[...] = (channel_of(expand_slot(lane, pad), part, pad) == row).astype(BF)
    slot = jnp.where(lane >= split, project_slot(lane - split, pad, split), -1)
    pick_p_ref[...] = (channel_of(slot, part, pad) == row).astype(BF)


def output_picks(part, pad, pick_e_ref, pick_p_ref):
    channels, depth = pick_e_ref.shape
    split = 4 * pad // LANES * LANES
    lane, row = iota((channels, depth), 1), iota((channels, depth), 0)
    pick_e_ref[...] = (channel_of(expand_slot(lane, pad), part, pad) == row).astype(BF)
    pick_p_ref[...] = (channel_of(project_slot(lane, pad, split), part, pad) == row).astype(BF)


def pack_weights(
    part, pad, expand_ref, bias_ref, project_ref, kernel_ref, pick_e_ref, pick_p_ref, out_ref, taps_ref, turn_scr
):
    hidden, channels = expand_ref.shape
    turn_scr[...] = jnp.zeros(turn_scr.shape, F32)
    for a in range(3):
        turn_scr[3 * a : 3 * a + 3, 0:part] = kernel_ref[a]
    taps_ref[...] = jnp.transpose(turn_scr[...])[0:pad, :]
    wide = out_ref.shape[1]
    bias = bias_ref[...]
    parts = jnp.zeros((16, hidden), F32)
    at = iota((16, hidden), 0)
    for k in range(3):
        piece = bias.astype(BF).astype(F32)
        bias = bias - piece
        parts = jnp.where(at == k, piece, parts)
    lane, row = iota((16, wide), 1), iota((16, wide), 0)
    pick_b = ((lane == row * pad + part) & (row < 3)).astype(BF)
    turned = (((0,), (0,)), ((), ()))
    packed = (
        jnp.dot(expand_ref[...], pick_e_ref[...], preferred_element_type=F32)
        + lax.dot_general(parts.astype(BF), pick_b, turned, preferred_element_type=F32)
        + jnp.dot(project_ref[...], pick_p_ref[...], preferred_element_type=F32)
    )
    rows = out_ref.shape[0]
    out_ref[0:hidden, :] = packed.astype(BF)
    out_ref[hidden:rows, :] = jnp.zeros((rows - hidden, wide), BF)


GELU_C = math.sqrt(2.0 / math.pi)


def activation_gradient(part, *refs):
    parts, (mask_ref, offset_ref, value_ref) = refs[0:4], refs[4:7]
    act_ref, y_scr, w_scr, t_scr, pick_e_ref, pick_p_ref = refs[7:]
    me = lax.axis_index("ch")
    tiles = w_scr.shape[1] // LANES
    hid = w_scr.shape[0] // 4
    depth, cells = y_scr.shape
    part_rows = cells // LANES
    pad = (parts[0].shape[0] - tiles * hid) // part_rows
    split = 4 * pad // LANES * LANES
    output_picks(part, pad, pick_e_ref, pick_p_ref)
    y_scr[0 : depth - 4 * pad, :] = jnp.zeros((depth - 4 * pad, cells), BF)
    for k, ref in enumerate(parts):
        for t in range(tiles):
            w_scr[k * hid : (k + 1) * hid, t * LANES : (t + 1) * LANES] = ref[
                t * hid : (t + 1) * hid, :
            ]
        block = me ^ k
        start = tiles * hid + (part_rows * pad if k == 3 else 0)
        for r in range(part_rows):
            cols = slice(r * LANES, (r + 1) * LANES)
            for u in range(pad // 16):
                slot = block * pad + 16 * u
                to = jnp.where(slot < split, slot + LANES, slot - split + depth - 4 * pad)
                at = start + r * pad + 16 * u
                y_scr[pl.ds(aligned(to), 16), cols] = ref[at : at + 16, :]
    rows = pl.ds(pl.multiple_of(me * part_rows, part_rows), part_rows)
    swath = swath_rows(part_rows, me * part_rows, offset_ref, value_ref, LANES)
    swath = swath * mask_ref[rows, :].astype(F32)
    for r in range(part_rows):
        at = (slice(LANES, LANES + 16), slice(r * LANES, (r + 1) * LANES))
        y_scr[at] = with_first(y_scr[at], swath[r : r + 1, :]).astype(BF)
    t_scr[...] = jnp.transpose(w_scr[:, 0:depth])
    step = 256
    for start in range(0, cells, step):
        cols = slice(start, start + step)
        act_ref[:, cols] = jnp.dot(
            w_scr[:, split : split + depth], y_scr[:, cols], preferred_element_type=F32
        )


def hidden_gradient(half, *refs):
    xs, (act_ref, y_ref, w_ref), refs = refs[0:4], refs[4:7], refs[7:]
    sums = ()
    if half:
        sums, refs = refs[0:2], refs[2:]
    pre_ref, keep_ref, send_ref, x_scr, value_scr = refs
    part_rows, pad = xs[0].shape[:2]
    hid = w_ref.shape[0] // 4
    split = 4 * pad // LANES * LANES
    depth, cells = x_scr.shape
    offset = half * cells
    me = lax.axis_index("ch")
    x_scr[4 * pad : depth, :] = jnp.zeros((depth - 4 * pad, cells), BF)
    for k in range(4):
        for r in range(part_rows):
            cols = slice(r * LANES, (r + 1) * LANES)
            x_scr[pl.ds(aligned((me ^ k) * pad), pad), cols] = xs[k][r]
    step = 256
    for start in range(0, cells, step):
        cols = slice(start, start + step)
        hidden = jnp.dot(w_ref[:, 0:depth], x_scr[:, cols], preferred_element_type=F32)
        square = hidden * hidden
        tanh = jnp.tanh(hidden * (GELU_C + (0.044715 * GELU_C) * square))
        each = 0.5 + 0.5 * tanh
        slope = each + hidden * (0.5 * GELU_C + (1.5 * 0.044715 * GELU_C) * square) * (
            1.0 - tanh * tanh
        )
        value_scr[:, cols] = (hidden * each).astype(BF)
        pre_ref[:, cols] = (act_ref[:, offset + start : offset + start + step] * slope).astype(BF)
    over_cells = (((1,), (1,)), ((), ()))
    expand = lax.dot_general(pre_ref[...], x_scr[...], over_cells, preferred_element_type=F32)
    project = lax.dot_general(
        value_scr[...], y_ref[:, offset : offset + cells], over_cells, preferred_element_type=F32
    )
    shared = split // LANES
    tiles = [expand[:, t * LANES : (t + 1) * LANES] for t in range(shared)]
    tiles.append(expand[:, split : split + LANES] + project[:, 0:LANES])
    tiles += [project[:, t * LANES : (t + 1) * LANES] for t in range(1, shared + 1)]
    used = len(tiles) * hid
    for ref in (keep_ref, send_ref):
        for k in range(2):
            ref[k, used:, :] = jnp.zeros((ref.shape[1] - used, LANES), ref.dtype)
    for k in range(4):
        to = send_ref if k % 2 else keep_ref
        for t, tile in enumerate(tiles):
            at = (k // 2, slice(t * hid, (t + 1) * hid), slice(None))
            value = tile[k * hid : (k + 1) * hid]
            if half:
                value = value + sums[k % 2][at]
            to[at] = value.astype(to.dtype)


def conv_gradient(away, first_ref, second_ref, t_ref, *rest):
    outs, scr = rest[:-1], rest[-1]
    if away:
        outs = (rest[0].at[0], rest[0].at[1])
    part_rows, pad = outs[0].shape[:2]
    me = lax.axis_index("ch")
    first = ((me // 2 + away) % 2) * 2 * pad
    weights = t_ref[pl.ds(aligned(first), 2 * pad), :]
    step = 256
    half = first_ref.shape[1]
    for start in range(0, 2 * half, step):
        pre = (first_ref if start < half else second_ref)[:, start % half : start % half + step]
        scr[:, start : start + step] = jnp.dot(weights, pre, preferred_element_type=F32).astype(BF)
    for k, to in enumerate(outs):
        at = pl.ds(aligned(((me + k) % 2) * pad), pad)
        for r in range(part_rows):
            to[r] = scr[at, r * LANES : (r + 1) * LANES]


def add_cores(keep_ref, got_ref, own_ref, *sends):
    piece = own_ref.shape[1]
    place = 2 * lax.axis_index("lat") + lax.axis_index("lon") % 2
    for k in range(4):
        at = pl.ds(aligned((place ^ k) * piece), piece)
        for group in range(2):
            total = keep_ref[group, at, :] + got_ref[group, at, :].astype(F32)
            to = sends[k - 1] if k else own_ref
            to[group] = total.astype(to.dtype)


def add_pieces(own_ref, a_ref, b_ref, c_ref, mine_ref, other_ref):
    for group, to in enumerate((mine_ref, other_ref)):
        total = own_ref[group] + (
            a_ref[group].astype(F32) + b_ref[group].astype(F32) + c_ref[group].astype(F32)
        )
        to[...] = total.astype(to.dtype)


def add_across(mine_ref, got_ref, out_ref):
    out_ref[...] = (mine_ref[...] + got_ref[...].astype(F32)).astype(BF)


def finish_pieces(mine_ref, line_ref, kernel_ref, third_ref, out_ref, turn_scr):
    piece, pad = mine_ref.shape[0], kernel_ref.shape[0]
    out_ref[0:piece, :] = (mine_ref[...].astype(F32) + line_ref[...].astype(F32)).astype(BF)
    other = pltpu.roll(third_ref[DIL].astype(F32), LANES - RIDE, 1)
    turn_scr[...] = jnp.zeros(turn_scr.shape, F32)
    turn_scr[0:pad, :] = kernel_ref[...].astype(F32) + other
    out_ref[piece:, :] = jnp.transpose(turn_scr[...])[0:TAP_ROWS, :].astype(BF)


def write_parameters(part, pad, scale, hid, p0, p1, p2, p3, pick_e, pick_p, *rest):
    expand_ref, project_ref, bias_ref, taps_ref, all_scr, taps_scr = rest
    piece = p0.shape[0] - TAP_ROWS
    place = 2 * lax.axis_index("lat") + lax.axis_index("lon") % 2
    for k, ref in enumerate((p0, p1, p2, p3)):
        to = place ^ k
        all_scr[pl.ds(aligned(to * piece), piece), :] = ref[0:piece, :]
        taps_scr[pl.ds(aligned(to * TAP_ROWS), TAP_ROWS), :] = ref[piece:, :].astype(F32)
    unpack(part, pad, scale, hid, all_scr, pick_e, pick_p, expand_ref, project_ref, bias_ref)
    total = taps_scr[0:TAP_ROWS, :]
    for k in range(1, 4):
        total = total + taps_scr[k * TAP_ROWS : (k + 1) * TAP_ROWS, :]
    write_taps(total, scale, taps_ref)


def write_taps(total, scale, taps_ref):
    for a in range(3):
        taps_ref[a] = total[3 * a : 3 * a + 3, 0 : taps_ref.shape[2]] * scale


def unpack(part, pad, scale, hid, all_ref, pick_e, pick_p, expand_ref, project_ref, bias_ref):
    hidden = expand_ref.shape[0]
    split = 4 * pad // LANES * LANES
    shared = split // LANES
    tiles = [all_ref[t * hid : (t + 1) * hid, :] for t in range(2 * shared + 1)]
    depth = (shared + 1) * LANES
    expand = jnp.concatenate(tiles[: shared + 1], axis=1)
    project = jnp.concatenate(tiles[shared:], axis=1)
    pick_b = (iota((16, depth), 1) == part).astype(BF)
    last = (((1,), (1,)), ((), ()))
    dot = functools.partial(lax.dot_general, dimension_numbers=last, preferred_element_type=F32)
    expand_ref[...] = dot(expand, pick_e[...])[0:hidden, :] * scale
    bias_ref[...] = dot(pick_b, expand)[0:1, 0:hidden] * scale
    project_ref[...] = dot(project, pick_p[...])[0:hidden, :] * scale


def unpack_whole(part, pad, scale, hid, all_ref, taps_in, pick_e, pick_p, *rest):
    expand_ref, project_ref, bias_ref, taps_ref, turn_scr = rest
    unpack(part, pad, scale, hid, all_ref, pick_e, pick_p, expand_ref, project_ref, bias_ref)
    turn_scr[...] = jnp.zeros(turn_scr.shape, F32)
    turn_scr[0:pad, :] = taps_in[...]
    write_taps(jnp.transpose(turn_scr[...])[0:TAP_ROWS, :], scale, taps_ref)


def on_device(
    ocean_state,
    land_mask,
    out_grad,
    swath_offset,
    swath_value,
    depth_kernel,
    expand_weight,
    expand_bias,
    project_weight,
):
    part, rows, cols = ocean_state.shape
    n_lon, n_lat, n_ch = lax.axis_size("lon"), lax.axis_size("lat"), lax.axis_size("ch")
    channels, hidden = expand_weight.shape
    assert n_ch == 4 and cols == LANES and rows % n_ch == 0
    pad = (part + 16) // 16 * 16
    hid = (hidden + 15) // 16 * 16
    split = n_ch * pad // LANES * LANES
    tail = n_ch * pad - split
    assert tail == LANES // 2
    wide = 2 * n_ch * pad
    depth = split + LANES
    part_rows = rows // n_ch
    cells = part_rows * cols
    swap = n_lat == 2
    scale = 1.0 / math.sqrt(rows * n_lat * cols * n_lon)
    core = [(i, i ^ 1) for i in range(n_ch)]
    across = [(i, i ^ 2) for i in range(n_ch)]
    block = shape((rows, pad, cols), BF)
    quarter = shape((part_rows, pad, cols), BF)
    flat = pltpu.VMEM(((rows + 1) * pad, cols), F32)

    turn = pltpu.VMEM((LANES, LANES), F32)

    tile_rows = wide // LANES * hid
    sum_rows = (tile_rows + 63) // 64 * 64
    near_rows, far_rows = tile_rows + part_rows * pad, tile_rows + 2 * part_rows * pad
    fetched = [
        ocean_state,
        land_mask,
        out_grad,
        swath_offset.reshape(1, -1),
        swath_value.reshape(1, -1),
        expand_weight.T,
        expand_bias.reshape(1, hidden),
        project_weight,
        depth_kernel,
    ]
    count = len(fetched)
    outs = call(
        functools.partial(prepare_outer, swap, count),
        outer_shapes(pad, swap) + [shape(a.shape, a.dtype) for a in fetched],
        fetched,
        [pltpu.VMEM(((2 * DIL + 1) * pad, cols), F32), pltpu.SemaphoreType.DMA((count,))],
        "outer_rows",
        far=True,
    )
    outer, (ocean_state, land_mask, *held) = outs[:-count], outs[-count:]
    to_far, tiles, taps = call(
        functools.partial(prepare_far, part),
        [shape((far_rows, LANES), BF), shape((tile_rows, LANES), BF), shape((pad, LANES), F32)],
        [land_mask, held[0], *held[3:]],
        [
            pltpu.VMEM(((rows // 2 + 1) * pad, cols), F32),
            pltpu.VMEM((hid, wide), BF),
            turn,
            pltpu.VMEM((channels, wide), BF),
            pltpu.VMEM((channels, wide), BF),
        ],
        "far_rows",
    )
    masked, *strips = call(
        prepare_state,
        [block] + strip_shapes(pad),
        [ocean_state, land_mask],
        [flat],
        "state_rows",
        after=[taps],
    )
    cotan, own, to_core = call(
        prepare_near,
        [block, shape((near_rows, LANES), BF), shape((near_rows, LANES), BF)],
        [land_mask, *held[0:3], tiles],
        [flat],
        "cotan_rows",
    )
    around, _ = exchange_halo(rows, strips, outer, swap, "state", after=[to_core])
    from_far = lax.ppermute(to_far, "ch", across)
    ones = functools.partial(conv_forward, part)
    conv_operands = [masked, *around, taps]
    conv_scratch = [
        pltpu.VMEM((rows // 2 + 2 * DIL, pad, cols), BF),
        pltpu.VMEM((pad, LANES), F32),
        pltpu.VMEM((pad, LANES), F32),
        pltpu.VMEM((rows // 2, pad, cols), BF),
    ]
    eighth = shape((part_rows // 2, pad, cols), BF)
    conv_far = call(
        functools.partial(ones, 1), [eighth] * 4, conv_operands, conv_scratch, "conv_away"
    )
    from_far = call(
        relay, [from_far], [from_far], (), "cotan_relay", aliases={0: 0}, after=around[1:2]
    )[0]
    passed = lax.ppermute(from_far, "ch", core)
    conv_near = call(
        functools.partial(ones, 0),
        [eighth] * 4,
        conv_operands,
        conv_scratch,
        "conv_here",
        after=[conv_far[0], passed],
    )
    both = [(i, i ^ 3) for i in range(n_ch)]
    halves = [
        [
            conv_near[2 * h],
            lax.ppermute(conv_near[2 * h + 1], "ch", core),
            lax.ppermute(conv_far[2 * h], "ch", across),
            lax.ppermute(conv_far[2 * h + 1], "ch", both),
        ]
        for h in range(2)
    ]
    act_grad, cotan_all, weights_all, weights_turned, *picks = call(
        functools.partial(activation_gradient, part),
        [
            shape((n_ch * hid, cells), F32),
            shape((depth, cells), BF),
            shape((n_ch * hid, wide), BF),
            shape((depth, n_ch * hid), BF),
            shape((channels, depth), BF),
            shape((channels, depth), BF),
        ],
        [own, lax.ppermute(to_core, "ch", core), from_far, passed, land_mask, *held[1:3]],
        (),
        "activation_gradient",
    )
    pre_grad, sums = [], ()
    for h in range(2):
        pre, *sums = call(
            functools.partial(hidden_gradient, h),
            [
                shape((n_ch * hid, cells // 2), BF),
                shape((2, sum_rows, LANES), F32),
                shape((2, sum_rows, LANES), BF if h else F32),
            ],
            [*halves[h], act_grad, cotan_all, weights_all, *sums],
            [pltpu.VMEM((depth, cells // 2), BF), pltpu.VMEM((n_ch * hid, cells // 2), BF)],
            "hidden_first" if h == 0 else "hidden_second",
        )
        pre_grad.append(pre)
    keep, send = sums
    got = lax.ppermute(send, "ch", core)
    grad_scratch = [pltpu.VMEM((2 * pad, cells), BF)]
    grad_far = call(
        functools.partial(conv_gradient, 1),
        [shape((2, part_rows, pad, cols), BF)],
        [*pre_grad, weights_turned],
        grad_scratch,
        "gradient_away",
    )[0]
    grad_own, grad_core = call(
        functools.partial(conv_gradient, 0),
        [quarter] * 2,
        [*pre_grad, weights_turned],
        grad_scratch,
        "gradient_here",
        after=[grad_far],
    )
    grad_near = lax.ppermute(grad_core, "ch", core)
    grad_far = lax.ppermute(grad_far, "ch", across)
    staged = two_by_four()
    padded = shape((rows + 2 * DIL, pad, cols), BF)
    if not staged:
        shifted = call(shift_columns, [padded, padded], [masked, *around], (), "shift_columns")
    if staged:
        piece = sum_rows // 4
        mine, *sends = call(
            add_cores,
            [shape((2, piece, LANES), F32)] + [shape((2, piece, LANES), BF)] * 3,
            [keep, got],
            (),
            "add_cores",
        )

        shifted = call(
            shift_columns, [padded, padded], [masked, *around], (), "shift_columns", after=sends[:1]
        )

        def turn_plane(k):
            pairs = []
            for lon in range(n_lon):
                for lat in range(n_lat):
                    pairs.append((lon * n_lat + lat, (lon ^ (k & 1)) * n_lat + (lat ^ (k >> 1))))
            return pairs

        def over_plane(values):
            return [lax.ppermute(values[k - 1], ("lon", "lat"), turn_plane(k)) for k in (1, 2, 3)]

        mine, other = call(
            add_pieces,
            [shape((piece, LANES), F32), shape((piece, LANES), BF)],
            [mine, *over_plane(sends)],
            (),
            "add_pieces",
            after=[grad_near, shifted[0]],
        )
    passed = call(
        second_half, [quarter], [grad_far], (), "grad_half", after=[other] if staged else []
    )[0]
    conv_grad, *grad_strips = call(
        functools.partial(collect_grad, swap),
        [block] + strip_shapes(pad) + outer_shapes(pad, swap),
        [grad_own, grad_near, grad_far, lax.ppermute(passed, "ch", core)],
        (),
        "grad_rows",
    )
    kernel_part = call(
        kernel_gradient,
        [shape((pad, LANES), BF)],
        [conv_grad, masked, around[0], *shifted],
        (),
        "kernel_gradient",
    )[0]
    grad_around, marks = exchange_halo(rows, grad_strips[:3], grad_strips[3:], swap, "grad", planes=4, riding=[kernel_part])
    if staged:
        mine = call(
            add_across,
            [shape((piece, LANES), BF)],
            [mine, lax.ppermute(other, "ch", across)],
            (),
            "add_across",
        )[0]
    state_grad, mark = call(
        conv_adjoint,
        [shape((part, rows, cols), BF), shape((8, LANES), F32)],
        [conv_grad, *grad_around, taps, cotan, land_mask],
        [
            pltpu.VMEM((17 * (rows + 8), cols), F32),
            pltpu.VMEM((part, rows, cols), BF),
            pltpu.SemaphoreType.DMA((-(-part // 16),)),
        ],
        "conv_adjoint",
        writes=1,
    )
    outs = [
        shape((hidden, channels), F32),
        shape((hidden, channels), F32),
        shape((1, hidden), F32),
        shape((3, 3, part), F32),
    ]
    if staged:
        far_lon = [(lon, lon ^ 2) for lon in range(n_lon)]
        summed = call(
            finish_pieces,
            [shape((piece + TAP_ROWS, LANES), BF)],
            [
                mine,
                lax.ppermute(mine, "lon", far_lon),
                kernel_part,
                marks[1],
            ],
            [turn],
            "finish_pieces",
            after=marks[2:],
        )[0]
        expand_grad, project_grad, bias_grad, kernel_grad = call(
            functools.partial(write_parameters, part, pad, scale, hid),
            outs,
            [summed, *over_plane([summed] * 3), *picks],
            [pltpu.VMEM((sum_rows, LANES), BF), pltpu.VMEM((4 * TAP_ROWS, LANES), F32)],
            "write_parameters",
            after=[mark],
        )
    else:
        total = keep + got.astype(F32)
        total = total[0] + lax.ppermute(total[1].astype(BF), "ch", across).astype(F32)
        total, kernel_sum = lax.psum((total, kernel_part.astype(F32)), ("lon", "lat"))
        expand_grad, project_grad, bias_grad, kernel_grad = call(
            functools.partial(unpack_whole, part, pad, scale, hid),
            outs,
            [total.astype(BF), kernel_sum, *picks],
            [turn],
            "write_parameters",
        )
    return (
        state_grad,
        expand_grad.T,
        project_grad,
        bias_grad.reshape(hidden),
        kernel_grad,
    )


def solution(mesh):
    return jax.shard_map(
        on_device,
        mesh=mesh,
        in_specs=(
            P("ch", "lat", "lon"),
            P("lat", "lon"),
            P("ch", "lat", "lon"),
            P("lat", "lon", None),
            P("lat", "lon", None),
            P(None, None, "ch"),
            P(None, "ch"),
            P("ch"),
            P("ch", None),
        ),
        out_specs=(
            P("ch", "lat", "lon"),
            P(None, "ch"),
            P("ch", None),
            P("ch"),
            P(None, None, "ch"),
        ),
        check_vma=False,
    )
```

```python
import functools
import math

import jax
import jax.numpy as jnp
from jax import lax
from jax.experimental import pallas as pl
from jax.experimental.pallas import tpu as pltpu
from jax.sharding import PartitionSpec as P

DIL = 2
LANES = 128
TAP_ROWS = 16
RIDE = 96
BF = jnp.bfloat16
F32 = jnp.float32


def shape(dims, kind):
    return jax.ShapeDtypeStruct(dims, kind)


def call(kernel, outs, args, scratch=(), name=None, flops=0, aliases=None, far=False, after=(), writes=0):
    count = len(args)
    if after:
        body, args = kernel, [*args, *after]

        def kernel(*refs):
            body(*refs[:count], *refs[len(args) :])

    if far:
        args = [pltpu.with_memory_space_constraint(a, pltpu.HBM) for a in args]
    spaces = [pltpu.HBM if far else pl.ANY if i >= count else pltpu.VMEM for i in range(len(args))]
    moved = sum(math.prod(a.shape) * a.dtype.itemsize for a in list(args) + list(outs))
    return pl.pallas_call(
        kernel,
        out_shape=tuple(outs),
        in_specs=[pl.BlockSpec(memory_space=space) for space in spaces],
        out_specs=tuple(
            pl.BlockSpec(memory_space=pl.ANY if i < writes else pltpu.VMEM) for i in range(len(outs))
        ),
        scratch_shapes=list(scratch),
        input_output_aliases=aliases or {},
        name=name,
        compiler_params=pltpu.CompilerParams(vmem_limit_bytes=24 * 1024 * 1024),
        cost_estimate=pl.CostEstimate(flops=flops, bytes_accessed=moved, transcendentals=0),
    )(*args)


def iota(dims, dim):
    return lax.broadcasted_iota(jnp.int32, dims, dim)


def aligned(index):
    return pl.multiple_of(index, 16)


def to_rows(block_ref, weight, scr, pad):
    channels, rows, cols = block_ref.shape

    def body(c, carry):
        value = block_ref[c].astype(F32)
        if weight is not None:
            value = value * weight
        scr[pl.ds(c, rows, stride=pad), :] = value
        return carry

    lax.fori_loop(0, channels, body, 0, unroll=5 if channels % 5 == 0 else 1)
    for c in range(channels, pad):
        scr[pl.ds(c, rows, stride=pad), :] = jnp.zeros((rows, cols), F32)


def pack_columns(value, ext_row, left, right):
    lane = iota(value.shape, 1)
    here = (lane == 2 * ext_row) | (lane == 2 * ext_row + 1)
    size = value.shape[1]
    left = jnp.where(here, pltpu.roll(value, (2 * ext_row) % size, 1), left)
    right = jnp.where(here, pltpu.roll(value, (2 * ext_row + 2) % size, 1), right)
    return left, right


def mirrored(value):
    size = value.shape[1]
    flip = (iota((size, size), 0) + iota((size, size), 1) == size - 1).astype(BF)
    return jnp.dot(value, flip, preferred_element_type=F32).astype(BF)


def emit_strips(read, rows, pad, fold_ref, left_ref, right_ref):
    for t in range(DIL):
        fold_ref[t] = mirrored(read(rows - 1 - t))
    left = jnp.zeros((pad, LANES), F32)
    right = jnp.zeros((pad, LANES), F32)
    for r in range(rows):
        left, right = pack_columns(read(r).astype(F32), r + DIL, left, right)
    left_ref[...] = left.astype(BF)
    right_ref[...] = right.astype(BF)


def strip_shapes(pad):
    return [shape((DIL, pad, LANES), BF)] + [shape((pad, LANES), BF)] * 2


def outer_shapes(pad, swap):
    return [shape((DIL, pad, LANES), BF)] * (1 if swap else 2)


def emit_outer(low, high, t, swap, outer):
    if swap:
        outer[0][t] = jnp.where(lax.axis_index("lat") == 0, high, low).astype(BF)
    else:
        outer[0][t] = low.astype(BF)
        outer[1][t] = high.astype(BF)


def prepare_state(state_ref, mask_ref, rows_ref, fold_ref, left_ref, right_ref, scr):
    rows, pad = rows_ref.shape[:2]
    to_rows(state_ref, mask_ref[...].astype(F32), scr, pad)
    for r in range(rows):
        rows_ref[r] = scr[r * pad : (r + 1) * pad, :].astype(BF)
    emit_strips(lambda r: rows_ref[r], rows, pad, fold_ref, left_ref, right_ref)


def swath_rows(rows, start, offset_ref, value_ref, cols):
    offset = offset_ref[...]
    points = offset.shape[1]
    value = value_ref[...]
    total = jnp.zeros((rows, cols), F32)
    row = lax.shift_right_logical(offset, LANES.bit_length() - 1)
    row_hot = iota((rows, points), 0) + start == row
    col_hot = (iota((cols, points), 0) == (offset & (LANES - 1))).astype(BF)
    for _ in range(3):
        part = value.astype(BF)
        value = value - part.astype(F32)
        lhs = jnp.where(row_hot, part.astype(F32), 0.0).astype(BF)
        total = total + lax.dot_general(
            lhs, col_hot, (((1,), (1,)), ((), ())), preferred_element_type=F32
        )
    return total


def with_first(tile, row):
    lifted = jnp.broadcast_to(row, tile.shape)
    return jnp.where(iota(tile.shape, 0) == 0, tile.astype(F32) + lifted, tile.astype(F32))


def prepare_outer(swap, count, *refs):
    outs, (row_scr, sems) = refs[count:-2], refs[-2:]
    outer, held = outs[:-count], outs[-count:]
    state_ref, mask_ref = held[0:2]
    copies = [pltpu.make_async_copy(refs[k], held[k], sems.at[k]) for k in range(count)]
    for copy in copies:
        copy.start()
    pad = outer[0].shape[1]
    channels, rows, cols = state_ref.shape
    half = rows // 2
    lat = lax.axis_index("lat")
    for c in range(channels, pad):
        row_scr[pl.ds(c, 2 * DIL, stride=pad), :] = jnp.zeros((2 * DIL, cols), F32)
    copies[1].wait()
    copies[0].wait()
    if swap:
        start = aligned((1 - lat) * half)
        mask = mask_ref[pl.ds(start, half), :].astype(F32)

        def body(c, carry):
            value = state_ref[c, pl.ds(start, half), :].astype(F32) * mask
            row_scr[pl.ds(c, DIL, stride=pad), :] = jnp.where(
                lat == 0, value[half - DIL :, :], value[0:DIL, :]
            )
            return carry

    else:
        mask = mask_ref[...].astype(F32)

        def body(c, carry):
            value = state_ref[c].astype(F32) * mask
            row_scr[pl.ds(c, DIL, stride=pad), :] = value[0:DIL, :]
            row_scr[pl.ds(DIL * pad + c, DIL, stride=pad), :] = value[rows - DIL :, :]
            return carry

    lax.fori_loop(0, channels, body, 0, unroll=5 if channels % 5 == 0 else 1)
    for k, to in enumerate(outer):
        for t in range(DIL):
            at = (k * DIL + t) * pad
            to[t] = row_scr[at : at + pad, :].astype(BF)
    for copy in copies[2:]:
        copy.wait()


def prepare_far(part, *refs):
    (mask_ref, grad_ref), weights = refs[0:2], refs[2:6]
    far_ref, tiles_ref, taps_ref = refs[6:9]
    scr, weights_scr, turn_scr, pick_e, pick_p = refs[9:]
    channels, rows, cols = grad_ref.shape
    pad = taps_ref.shape[0]
    weight_picks(part, pad, weights_scr.shape[1], pick_e.shape[0], pick_e, pick_p)
    pack_weights(part, pad, *weights, pick_e, pick_p, weights_scr, taps_ref, turn_scr)
    hid = weights_scr.shape[0]
    full = tiles_ref.shape[0]
    for t in range(full // hid):
        tiles_ref[t * hid : (t + 1) * hid, :] = weights_scr[:, t * LANES : (t + 1) * LANES]
    far_ref[0:full, :] = tiles_ref[...]
    half = rows // 2
    me = lax.axis_index("ch")
    start = aligned((1 - me // 2) * half)

    def body(c, carry):
        scr[pl.ds(c, half, stride=pad), :] = grad_ref[c, pl.ds(start, half), :].astype(F32)
        return carry

    lax.fori_loop(0, channels, body, 0, unroll=5 if channels % 5 == 0 else 1)
    for c in range(channels, pad):
        scr[pl.ds(c, half, stride=pad), :] = jnp.zeros((half, cols), F32)
    mask = mask_ref[pl.ds(start, half), :].astype(F32)
    count_rows = half // 2
    for r in range(half):
        scr[r * pad : (r + 1) * pad, :] = scr[r * pad : (r + 1) * pad, :] * mask[r : r + 1, :]
    for k in range(2):
        first = aligned((((me ^ (2 + k)) % 2) * count_rows) * pad)
        size = count_rows * pad
        far_ref[full + k * size : full + (k + 1) * size, :] = scr[pl.ds(first, size), :].astype(BF)


def prepare_near(mask_ref, grad_ref, offset_ref, value_ref, tiles_ref, rows_ref, own_ref, core_ref, scr):
    rows, pad, cols = rows_ref.shape
    mask = mask_ref[...].astype(F32)
    to_rows(grad_ref, None, scr, pad)
    for r in range(rows):
        rows_ref[r] = (scr[r * pad : (r + 1) * pad, :] * mask[r : r + 1, :]).astype(BF)
    full = tiles_ref.shape[0]
    count = (own_ref.shape[0] - full) // pad
    me = lax.axis_index("ch")
    for k, to in enumerate((own_ref, core_ref)):
        to[0:full, :] = tiles_ref[...]
        for r in range(count):
            at = full + r * pad
            to[at : at + pad, :] = rows_ref[(me ^ k) * count + r]
    swath = swath_rows(rows, 0, offset_ref, value_ref, cols) * mask
    swath = jnp.where(me == 0, swath, 0.0)
    for r in range(rows):
        rows_ref[r, 0:16, :] = with_first(rows_ref[r, 0:16, :], swath[r : r + 1, :]).astype(BF)


def second_half(in_ref, out_ref):
    out_ref[...] = in_ref[1]


def relay(in_ref, out_ref):
    del in_ref, out_ref


def ring(count, step):
    return [(i, (i + step) % count) for i in range(count)]


def finish_columns(rows, swap, *refs):
    if swap:
        strip_ref, fold_ref, left_ref, right_ref, halo_ref, left_out, right_out = refs
        low_ref = high_ref = strip_ref
    else:
        low_ref, high_ref, fold_ref, left_ref, right_ref, halo_ref, left_out, right_out = refs
    lat, count = lax.axis_index("lat"), lax.axis_size("lat")
    left, right = left_ref[...].astype(F32), right_ref[...].astype(F32)
    for t in range(DIL):
        south = jnp.where(lat == 0, 0.0, low_ref[t].astype(F32))
        north = jnp.where(lat == count - 1, fold_ref[t].astype(F32), high_ref[t].astype(F32))
        halo_ref[t] = south.astype(BF)
        halo_ref[DIL + t] = north.astype(BF)
        left, right = pack_columns(south, t, left, right)
        left, right = pack_columns(north, rows + DIL + t, left, right)
    left_out[...] = left.astype(BF)
    right_out[...] = right.astype(BF)


def odd_lon():
    return lax.axis_index("lon") % 2 == 1


def pack_for_third(rows, riding, *refs):
    if riding:
        ride_ref, *refs = refs
    got_ref, fold_ref, left_ref, right_ref, out_ref = refs
    low = lax.axis_index("lat") == 0
    left, right = left_ref[...].astype(F32), right_ref[...].astype(F32)
    for t in range(DIL):
        got = got_ref[t].astype(F32)
        left, right = pack_columns(jnp.where(low, 0.0, got), t, left, right)
        left, right = pack_columns(jnp.where(low, got, 0.0), rows + DIL + t, left, right)
        out_ref[t] = fold_ref[t]
    pack = jnp.where(odd_lon(), right, left)
    if riding:
        pack = pack + pltpu.roll(ride_ref[...].astype(F32), RIDE, 1)
    out_ref[DIL] = pack.astype(BF)


def pack_for_first(rows, got_ref, fold_ref, left_ref, right_ref, third_ref, halo_ref, out_ref, side_ref):
    low = lax.axis_index("lat") == 0
    odd = odd_lon()
    left, right = left_ref[...].astype(F32), right_ref[...].astype(F32)
    side = third_ref[DIL].astype(F32)
    size = side.shape[1]
    lane = iota(side.shape, 1)
    for t in range(DIL):
        got = got_ref[t].astype(F32)
        south = jnp.where(low, 0.0, got)
        north = jnp.where(low, got, third_ref[t].astype(F32))
        halo_ref[t] = south.astype(BF)
        halo_ref[DIL + t] = north.astype(BF)
        left, right = pack_columns(south, t, left, right)
        left, right = pack_columns(north, rows + DIL + t, left, right)
        at = 2 * (rows + DIL + t)
        own = fold_ref[t].astype(F32)
        own = jnp.where(
            odd, pltpu.roll(own, at, 1), pltpu.roll(own, (at - (size - DIL)) % size, 1)
        )
        here = jnp.logical_and((lane == at) | (lane == at + 1), jnp.logical_not(low))
        side = jnp.where(here, own, side)
    out_ref[0] = jnp.where(odd, left, right).astype(BF)
    for k in range(1, out_ref.shape[0]):
        out_ref[k] = jnp.zeros(side.shape, BF)
    side_ref[...] = side.astype(BF)


def two_by_four():
    return lax.axis_size("lat") == 2 and lax.axis_size("lon") == 4


def exchange_halo(rows, strips, outer, swap, name, planes=1, riding=(), after=()):
    n_lat, n_lon = lax.axis_size("lat"), lax.axis_size("lon")
    fold, left, right = strips
    pad = left.shape[0]
    halo_shape, pack = shape((2 * DIL, pad, LANES), BF), shape((pad, LANES), BF)
    if two_by_four():
        got = lax.ppermute(outer[0], "lat", [(0, 1), (1, 0)])
        third_out = call(
            functools.partial(pack_for_third, rows, len(riding) > 0),
            [shape((DIL + 1, pad, LANES), BF)],
            [*riding, got, fold, left, right],
            (),
            name + "_third",
            after=after,
        )[0]
        third = lax.ppermute(third_out, "lon", [(lon, lon ^ 3) for lon in range(n_lon)])
        halo, first, side = call(
            functools.partial(pack_for_first, rows),
            [halo_shape, shape((planes, pad, LANES), BF), pack],
            [got, fold, left, right, third],
            (),
            name + "_first",
        )
        got = lax.ppermute(first, "lon", [(lon, lon ^ 1) for lon in range(n_lon)])
        return (halo, got, side), (third_out, third, first)
    top = n_lat - 1
    fold_pairs = [(lon * n_lat + top, (n_lon - 1 - lon) * n_lat + top) for lon in range(n_lon)]
    if swap:
        moved = [lax.ppermute(outer[0], "lat", [(0, 1), (1, 0)])]
    else:
        moved = [
            lax.ppermute(outer[1], "lat", [(i, i + 1) for i in range(n_lat - 1)]),
            lax.ppermute(outer[0], "lat", [(i + 1, i) for i in range(n_lat - 1)]),
        ]
    fold = lax.ppermute(fold, ("lon", "lat"), fold_pairs)
    halo, left, right = call(
        functools.partial(finish_columns, rows, swap),
        [halo_shape, pack, pack],
        [*moved, fold, left, right],
        (),
        name + "_columns",
    )
    from_right = lax.ppermute(left, "lon", ring(n_lon, -1))
    from_left = lax.ppermute(right, "lon", ring(n_lon, 1))
    return (halo, from_left, from_right), ()


def padded_row(block_ref, halo_ref, at, e):
    rows = block_ref.shape[0]
    if e < DIL:
        return halo_ref[e, at, :]
    if e < rows + DIL:
        return block_ref[e - DIL, at, :]
    return halo_ref[e - rows, at, :]


def sides(left_ref, right_ref, at):
    left = (left_ref[0, at, :] if two_by_four() else left_ref[at, :]).astype(F32)
    right = right_ref[at, :].astype(F32)
    if two_by_four():
        odd = odd_lon()
        left, right = jnp.where(odd, left, right), jnp.where(odd, right, left)
    return left, right


def shifted_rows(rows, read, left, right):
    lane = iota((16, LANES), 1)
    for e in range(rows + 2 * DIL):
        row = read(e).astype(F32)
        west = jnp.where(
            lane < DIL, pltpu.roll(left, (-2 * e) % LANES, 1), pltpu.roll(row, DIL, 1)
        )
        east = jnp.where(
            lane >= LANES - DIL,
            pltpu.roll(right, (LANES - DIL - 2 * e) % LANES, 1),
            pltpu.roll(row, LANES - DIL, 1),
        )
        yield e, (west, row, east)


def stencil_rows(rows, read, left, right, taps, north, emit):
    sums = {}
    for e, shifts in shifted_rows(rows, read, left, right):
        for a in (2, 1, 0):
            r = e - DIL * a
            if not 0 <= r < rows:
                continue
            used = north if e >= rows + DIL else taps[a]
            term = used[0] * shifts[0] + used[1] * shifts[1] + used[2] * shifts[2]
            sums[r] = term if r not in sums else sums[r] + term
            if a == 2:
                emit(r, sums.pop(r))


def stencil(block_ref, halo_ref, left_ref, right_ref, group, taps, north, emit):
    at = pl.ds(aligned(group * 16), 16)
    left, right = sides(left_ref, right_ref, at)
    read = functools.partial(padded_row, block_ref, halo_ref, at)
    stencil_rows(block_ref.shape[0], read, left, right, taps, north, emit)


def spread(tap_ref, group):
    values = tap_ref[pl.ds(aligned(group * 16), 16), :]
    return [
        [jnp.broadcast_to(values[:, 3 * a + b : 3 * a + b + 1], (16, LANES)) for b in range(3)]
        for a in range(3)
    ]


def conv_forward(ones_row, away, block_ref, halo_ref, left_ref, right_ref, tap_ref, *rest):
    outs, (row_scr, left_scr, right_scr, scr) = rest[:-4], rest[-4:]
    rows, pad = block_ref.shape[:2]
    half = rows // 2
    me = lax.axis_index("ch")
    upper = (me // 2 + away) % 2
    west, east = sides(left_ref, right_ref, slice(None))
    left_scr[...] = pltpu.roll(west, (LANES - 2 * half * upper) % LANES, 1)
    right_scr[...] = pltpu.roll(east, (LANES - 2 * half * upper) % LANES, 1)
    for t in range(DIL):
        low, high = halo_ref[t].astype(F32), halo_ref[DIL + t].astype(F32)
        before = block_ref[half - DIL + t].astype(F32)
        behind = block_ref[half + t].astype(F32)
        row_scr[t] = jnp.where(upper == 0, low, before).astype(BF)
        row_scr[half + DIL + t] = jnp.where(upper == 0, behind, high).astype(BF)
    for r in range(half):
        row_scr[DIL + r] = block_ref[upper * half + r]

    def body(group, carry):
        taps = spread(tap_ref, group)
        is_one = iota((16, LANES), 0) + group * 16 == ones_row
        at = pl.ds(aligned(group * 16), 16)

        def emit(r, value):
            value = jnp.where(is_one, 1.0, value)
            scr[r, at, :] = value.astype(BF)

        left, right = left_scr[at, :], right_scr[at, :]
        stencil_rows(half, lambda e: row_scr[e, at, :], left, right, taps, taps[2], emit)
        return carry

    lax.fori_loop(0, pad // 16, body, 0)
    count = half // 2
    size = outs[0].shape[0]
    for k, to in enumerate(outs):
        first = ((me + k % 2) % 2) * count
        to[...] = scr[pl.ds(first + k // 2 * size, size)]


def conv_adjoint(
    block_ref, halo_ref, left_ref, right_ref, tap_ref, cotan_ref, mask_ref, out_ref, mark_ref, scr, done_scr, sems
):
    rows, pad = block_ref.shape[:2]
    channels = out_ref.shape[0]
    at_top = lax.axis_index("lat") == lax.axis_size("lat") - 1
    mask = mask_ref[...].astype(F32)

    def copy(group, count):
        at = pl.ds(group * 16, count)
        return pltpu.make_async_copy(done_scr.at[at], out_ref.at[at], sems.at[group])

    def body(group, count):
        taps = spread(tap_ref, group)
        back = [[taps[2 - a][2 - b] for b in range(3)] for a in range(3)]
        north = [jnp.where(at_top, taps[2][b], back[2][b]) for b in range(3)]

        def emit(r, value):
            cotan = cotan_ref[r, pl.ds(aligned(group * 16), 16), :].astype(F32)
            scr[pl.ds(r, 16, stride=rows + 8), :] = (cotan + value) * mask[r : r + 1, :]

        stencil(block_ref, halo_ref, left_ref, right_ref, group, back, north, emit)
        for c in range(count):
            at = c * (rows + 8)
            done_scr[group * 16 + c] = scr[at : at + rows, :].astype(BF)
        copy(group, count).start()

    whole = channels // 16

    def each(group, carry):
        body(group, 16)
        return carry

    lax.fori_loop(0, whole, each, 0)
    if channels % 16:
        body(whole, channels % 16)
    mark_ref[...] = jnp.zeros(mark_ref.shape, F32)
    for group in range(whole):
        copy(group, 16).wait()
    if channels % 16:
        copy(whole, channels % 16).wait()


def collect_grad(swap, own, near, far, passed, rows_ref, *rest):
    part_rows = own.shape[0]
    rows, pad = rows_ref.shape[:2]
    me = lax.axis_index("ch")
    for k, quarter in enumerate((own, near, far.at[0], passed)):
        rows_ref[pl.ds((me ^ k) * part_rows, part_rows)] = quarter[...]
    strips, outer = rest[:3], rest[3:]
    for t in range(DIL):
        emit_outer(rows_ref[t].astype(F32), rows_ref[rows - DIL + t].astype(F32), t, swap, outer)
    emit_strips(lambda r: rows_ref[r], rows, pad, *strips)


def shift_columns(block_ref, halo_ref, left_ref, right_ref, west_ref, east_ref):
    def body(group, carry):
        at = pl.ds(aligned(group * 16), 16)
        left, right = sides(left_ref, right_ref, at)
        read = functools.partial(padded_row, block_ref, halo_ref, at)
        for e, shifts in shifted_rows(block_ref.shape[0], read, left, right):
            west_ref[e, at, :] = shifts[0].astype(BF)
            east_ref[e, at, :] = shifts[2].astype(BF)
        return carry

    lax.fori_loop(0, block_ref.shape[1] // 16, body, 0)


def kernel_gradient(grad_ref, block_ref, halo_ref, west_ref, east_ref, out_ref):
    rows, pad = grad_ref.shape[:2]

    def body(group, carry):
        at = pl.ds(aligned(group * 16), 16)
        sums = [[jnp.zeros((16, LANES), F32) for _ in range(3)] for _ in range(3)]
        for e in range(rows + 2 * DIL):
            middle = padded_row(block_ref, halo_ref, at, e)
            shifts = [part.astype(F32) for part in (west_ref[e, at, :], middle, east_ref[e, at, :])]
            for a in range(3):
                r = e - DIL * a
                if 0 <= r < rows:
                    grad = grad_ref[r, at, :].astype(F32)
                    for b in range(3):
                        sums[a][b] = sums[a][b] + grad * shifts[b]
        lane = iota((16, LANES), 1)
        out = jnp.zeros((16, LANES), F32)
        for a in range(3):
            for b in range(3):
                total = jnp.sum(sums[a][b], axis=1, keepdims=True)
                out = jnp.where(lane == 3 * a + b, total, out)
        out_ref[at, :] = out.astype(BF)
        return carry

    lax.fori_loop(0, pad // 16, body, 0)


def channel_of(slot, part, pad):
    block = sum((slot >= pad * b).astype(jnp.int32) for b in range(1, 4))
    inside = slot - block * pad
    return jnp.where((slot >= 0) & (slot < 4 * pad) & (inside < part), block * part + inside, -1)


def expand_slot(lane, pad):
    return jnp.where(lane < 4 * pad, lane, -1)


def project_slot(lane, pad, split):
    tail = 4 * pad - split
    low = LANES - tail
    return jnp.where(lane >= LANES, lane - LANES, jnp.where(lane >= low, lane - low + split, -1))


def weight_picks(part, pad, wide, channels, pick_e_ref, pick_p_ref):
    split = 4 * pad // LANES * LANES
    lane = iota((channels, wide), 1)
    row = iota((channels, wide), 0)
    pick_e_ref[...] = (channel_of(expand_slot(lane, pad), part, pad) == row).astype(BF)
    slot = jnp.where(lane >= split, project_slot(lane - split, pad, split), -1)
    pick_p_ref[...] = (channel_of(slot, part, pad) == row).astype(BF)


def output_picks(part, pad, pick_e_ref, pick_p_ref):
    channels, depth = pick_e_ref.shape
    split = 4 * pad // LANES * LANES
    lane, row = iota((channels, depth), 1), iota((channels, depth), 0)
    pick_e_ref[...] = (channel_of(expand_slot(lane, pad), part, pad) == row).astype(BF)
    pick_p_ref[...] = (channel_of(project_slot(lane, pad, split), part, pad) == row).astype(BF)


def pack_weights(
    part, pad, expand_ref, bias_ref, project_ref, kernel_ref, pick_e_ref, pick_p_ref, out_ref, taps_ref, turn_scr
):
    hidden, channels = expand_ref.shape
    turn_scr[...] = jnp.zeros(turn_scr.shape, F32)
    for a in range(3):
        turn_scr[3 * a : 3 * a + 3, 0:part] = kernel_ref[a]
    taps_ref[...] = jnp.transpose(turn_scr[...])[0:pad, :]
    wide = out_ref.shape[1]
    bias = bias_ref[...]
    parts = jnp.zeros((16, hidden), F32)
    at = iota((16, hidden), 0)
    for k in range(3):
        piece = bias.astype(BF).astype(F32)
        bias = bias - piece
        parts = jnp.where(at == k, piece, parts)
    lane, row = iota((16, wide), 1), iota((16, wide), 0)
    pick_b = ((lane == row * pad + part) & (row < 3)).astype(BF)
    turned = (((0,), (0,)), ((), ()))
    packed = (
        jnp.dot(expand_ref[...], pick_e_ref[...], preferred_element_type=F32)
        + lax.dot_general(parts.astype(BF), pick_b, turned, preferred_element_type=F32)
        + jnp.dot(project_ref[...], pick_p_ref[...], preferred_element_type=F32)
    )
    rows = out_ref.shape[0]
    out_ref[0:hidden, :] = packed.astype(BF)
    out_ref[hidden:rows, :] = jnp.zeros((rows - hidden, wide), BF)


GELU_C = math.sqrt(2.0 / math.pi)


def activation_gradient(part, *refs):
    parts, (mask_ref, offset_ref, value_ref) = refs[0:4], refs[4:7]
    act_ref, y_scr, w_scr, t_scr, pick_e_ref, pick_p_ref = refs[7:]
    me = lax.axis_index("ch")
    tiles = w_scr.shape[1] // LANES
    hid = w_scr.shape[0] // 4
    depth, cells = y_scr.shape
    part_rows = cells // LANES
    pad = (parts[0].shape[0] - tiles * hid) // part_rows
    split = 4 * pad // LANES * LANES
    output_picks(part, pad, pick_e_ref, pick_p_ref)
    y_scr[0 : depth - 4 * pad, :] = jnp.zeros((depth - 4 * pad, cells), BF)
    for k, ref in enumerate(parts):
        for t in range(tiles):
            w_scr[k * hid : (k + 1) * hid, t * LANES : (t + 1) * LANES] = ref[
                t * hid : (t + 1) * hid, :
            ]
        block = me ^ k
        start = tiles * hid + (part_rows * pad if k == 3 else 0)
        for r in range(part_rows):
            cols = slice(r * LANES, (r + 1) * LANES)
            for u in range(pad // 16):
                slot = block * pad + 16 * u
                to = jnp.where(slot < split, slot + LANES, slot - split + depth - 4 * pad)
                at = start + r * pad + 16 * u
                y_scr[pl.ds(aligned(to), 16), cols] = ref[at : at + 16, :]
    rows = pl.ds(pl.multiple_of(me * part_rows, part_rows), part_rows)
    swath = swath_rows(part_rows, me * part_rows, offset_ref, value_ref, LANES)
    swath = swath * mask_ref[rows, :].astype(F32)
    for r in range(part_rows):
        at = (slice(LANES, LANES + 16), slice(r * LANES, (r + 1) * LANES))
        y_scr[at] = with_first(y_scr[at], swath[r : r + 1, :]).astype(BF)
    t_scr[...] = jnp.transpose(w_scr[:, 0:depth])
    step = 256
    for start in range(0, cells, step):
        cols = slice(start, start + step)
        act_ref[:, cols] = jnp.dot(
            w_scr[:, split : split + depth], y_scr[:, cols], preferred_element_type=F32
        )


def hidden_gradient(half, *refs):
    xs, (act_ref, y_ref, w_ref), refs = refs[0:4], refs[4:7], refs[7:]
    sums = ()
    if half:
        sums, refs = refs[0:2], refs[2:]
    pre_ref, keep_ref, send_ref, x_scr, value_scr = refs
    part_rows, pad = xs[0].shape[:2]
    hid = w_ref.shape[0] // 4
    split = 4 * pad // LANES * LANES
    depth, cells = x_scr.shape
    offset = half * cells
    me = lax.axis_index("ch")
    x_scr[4 * pad : depth, :] = jnp.zeros((depth - 4 * pad, cells), BF)
    for k in range(4):
        for r in range(part_rows):
            cols = slice(r * LANES, (r + 1) * LANES)
            x_scr[pl.ds(aligned((me ^ k) * pad), pad), cols] = xs[k][r]
    step = 256
    for start in range(0, cells, step):
        cols = slice(start, start + step)
        hidden = jnp.dot(w_ref[:, 0:depth], x_scr[:, cols], preferred_element_type=F32)
        square = hidden * hidden
        tanh = jnp.tanh(hidden * (GELU_C + (0.044715 * GELU_C) * square))
        each = 0.5 + 0.5 * tanh
        slope = each + hidden * (0.5 * GELU_C + (1.5 * 0.044715 * GELU_C) * square) * (
            1.0 - tanh * tanh
        )
        value_scr[:, cols] = (hidden * each).astype(BF)
        pre_ref[:, cols] = (act_ref[:, offset + start : offset + start + step] * slope).astype(BF)
    over_cells = (((1,), (1,)), ((), ()))
    expand = lax.dot_general(pre_ref[...], x_scr[...], over_cells, preferred_element_type=F32)
    project = lax.dot_general(
        value_scr[...], y_ref[:, offset : offset + cells], over_cells, preferred_element_type=F32
    )
    shared = split // LANES
    tiles = [expand[:, t * LANES : (t + 1) * LANES] for t in range(shared)]
    tiles.append(expand[:, split : split + LANES] + project[:, 0:LANES])
    tiles += [project[:, t * LANES : (t + 1) * LANES] for t in range(1, shared + 1)]
    used = len(tiles) * hid
    for ref in (keep_ref, send_ref):
        for k in range(2):
            ref[k, used:, :] = jnp.zeros((ref.shape[1] - used, LANES), ref.dtype)
    for k in range(4):
        to = send_ref if k % 2 else keep_ref
        for t, tile in enumerate(tiles):
            at = (k // 2, slice(t * hid, (t + 1) * hid), slice(None))
            value = tile[k * hid : (k + 1) * hid]
            if half:
                value = value + sums[k % 2][at]
            to[at] = value.astype(to.dtype)


def conv_gradient(away, first_ref, second_ref, t_ref, *rest):
    outs, scr = rest[:-1], rest[-1]
    if away:
        outs = (rest[0].at[0], rest[0].at[1])
    part_rows, pad = outs[0].shape[:2]
    me = lax.axis_index("ch")
    first = ((me // 2 + away) % 2) * 2 * pad
    weights = t_ref[pl.ds(aligned(first), 2 * pad), :]
    step = 256
    half = first_ref.shape[1]
    for start in range(0, 2 * half, step):
        pre = (first_ref if start < half else second_ref)[:, start % half : start % half + step]
        scr[:, start : start + step] = jnp.dot(weights, pre, preferred_element_type=F32).astype(BF)
    for k, to in enumerate(outs):
        at = pl.ds(aligned(((me + k) % 2) * pad), pad)
        for r in range(part_rows):
            to[r] = scr[at, r * LANES : (r + 1) * LANES]


def add_cores(keep_ref, got_ref, own_ref, *sends):
    piece = own_ref.shape[1]
    place = 2 * lax.axis_index("lat") + lax.axis_index("lon") % 2
    for k in range(4):
        at = pl.ds(aligned((place ^ k) * piece), piece)
        for group in range(2):
            total = keep_ref[group, at, :] + got_ref[group, at, :].astype(F32)
            to = sends[k - 1] if k else own_ref
            to[group] = total.astype(to.dtype)


def add_pieces(own_ref, a_ref, b_ref, c_ref, mine_ref, other_ref):
    for group, to in enumerate((mine_ref, other_ref)):
        total = own_ref[group] + (
            a_ref[group].astype(F32) + b_ref[group].astype(F32) + c_ref[group].astype(F32)
        )
        piece = total.shape[0]
        to[0:piece, :] = total.astype(to.dtype)
        if to.shape[0] > piece:
            to[piece:, :] = jnp.zeros((to.shape[0] - piece, LANES), to.dtype)


def add_across(mine_ref, got_ref, out_ref):
    piece = mine_ref.shape[0]
    out_ref[...] = (mine_ref[...] + got_ref[0:piece, :].astype(F32)).astype(BF)


def finish_pieces(mine_ref, line_ref, kernel_ref, third_ref, out_ref, turn_scr):
    piece, pad = mine_ref.shape[0], kernel_ref.shape[0]
    out_ref[0:piece, :] = (mine_ref[...].astype(F32) + line_ref[...].astype(F32)).astype(BF)
    other = pltpu.roll(third_ref[DIL].astype(F32), LANES - RIDE, 1)
    turn_scr[...] = jnp.zeros(turn_scr.shape, F32)
    turn_scr[0:pad, :] = kernel_ref[...].astype(F32) + other
    out_ref[piece:, :] = jnp.transpose(turn_scr[...])[0:TAP_ROWS, :].astype(BF)


def write_parameters(part, pad, scale, hid, p0, p1, p2, p3, pick_e, pick_p, *rest):
    expand_ref, project_ref, bias_ref, taps_ref, all_scr, taps_scr = rest
    piece = p0.shape[0] - TAP_ROWS
    place = 2 * lax.axis_index("lat") + lax.axis_index("lon") % 2
    for k, ref in enumerate((p0, p1, p2, p3)):
        to = place ^ k
        all_scr[pl.ds(aligned(to * piece), piece), :] = ref[0:piece, :]
        taps_scr[pl.ds(aligned(to * TAP_ROWS), TAP_ROWS), :] = ref[piece:, :].astype(F32)
    unpack(part, pad, scale, hid, all_scr, pick_e, pick_p, expand_ref, project_ref, bias_ref)
    total = taps_scr[0:TAP_ROWS, :]
    for k in range(1, 4):
        total = total + taps_scr[k * TAP_ROWS : (k + 1) * TAP_ROWS, :]
    write_taps(total, scale, taps_ref)


def write_taps(total, scale, taps_ref):
    for a in range(3):
        taps_ref[a] = total[3 * a : 3 * a + 3, 0 : taps_ref.shape[2]] * scale


def unpack(part, pad, scale, hid, all_ref, pick_e, pick_p, expand_ref, project_ref, bias_ref):
    hidden = expand_ref.shape[0]
    split = 4 * pad // LANES * LANES
    shared = split // LANES
    tiles = [all_ref[t * hid : (t + 1) * hid, :] for t in range(2 * shared + 1)]
    depth = (shared + 1) * LANES
    expand = jnp.concatenate(tiles[: shared + 1], axis=1)
    project = jnp.concatenate(tiles[shared:], axis=1)
    pick_b = (iota((16, depth), 1) == part).astype(BF)
    last = (((1,), (1,)), ((), ()))
    dot = functools.partial(lax.dot_general, dimension_numbers=last, preferred_element_type=F32)
    expand_ref[...] = dot(expand, pick_e[...])[0:hidden, :] * scale
    bias_ref[...] = dot(pick_b, expand)[0:1, 0:hidden] * scale
    project_ref[...] = dot(project, pick_p[...])[0:hidden, :] * scale


def unpack_whole(part, pad, scale, hid, all_ref, taps_in, pick_e, pick_p, *rest):
    expand_ref, project_ref, bias_ref, taps_ref, turn_scr = rest
    unpack(part, pad, scale, hid, all_ref, pick_e, pick_p, expand_ref, project_ref, bias_ref)
    turn_scr[...] = jnp.zeros(turn_scr.shape, F32)
    turn_scr[0:pad, :] = taps_in[...]
    write_taps(jnp.transpose(turn_scr[...])[0:TAP_ROWS, :], scale, taps_ref)


def on_device(
    ocean_state,
    land_mask,
    out_grad,
    swath_offset,
    swath_value,
    depth_kernel,
    expand_weight,
    expand_bias,
    project_weight,
):
    part, rows, cols = ocean_state.shape
    n_lon, n_lat, n_ch = lax.axis_size("lon"), lax.axis_size("lat"), lax.axis_size("ch")
    channels, hidden = expand_weight.shape
    assert n_ch == 4 and cols == LANES and rows % n_ch == 0
    pad = (part + 16) // 16 * 16
    hid = (hidden + 15) // 16 * 16
    split = n_ch * pad // LANES * LANES
    tail = n_ch * pad - split
    assert tail == LANES // 2
    wide = 2 * n_ch * pad
    depth = split + LANES
    part_rows = rows // n_ch
    cells = part_rows * cols
    swap = n_lat == 2
    scale = 1.0 / math.sqrt(rows * n_lat * cols * n_lon)
    core = [(i, i ^ 1) for i in range(n_ch)]
    across = [(i, i ^ 2) for i in range(n_ch)]
    block = shape((rows, pad, cols), BF)
    quarter = shape((part_rows, pad, cols), BF)
    flat = pltpu.VMEM(((rows + 1) * pad, cols), F32)

    turn = pltpu.VMEM((LANES, LANES), F32)

    tile_rows = wide // LANES * hid
    sum_rows = (tile_rows + 63) // 64 * 64
    near_rows, far_rows = tile_rows + part_rows * pad, tile_rows + 2 * part_rows * pad
    fetched = [
        ocean_state,
        land_mask,
        out_grad,
        swath_offset.reshape(1, -1),
        swath_value.reshape(1, -1),
        expand_weight.T,
        expand_bias.reshape(1, hidden),
        project_weight,
        depth_kernel,
    ]
    count = len(fetched)
    outs = call(
        functools.partial(prepare_outer, swap, count),
        outer_shapes(pad, swap) + [shape(a.shape, a.dtype) for a in fetched],
        fetched,
        [pltpu.VMEM(((2 * DIL + 1) * pad, cols), F32), pltpu.SemaphoreType.DMA((count,))],
        "outer_rows",
        far=True,
    )
    outer, (ocean_state, land_mask, *held) = outs[:-count], outs[-count:]
    to_far, tiles, taps = call(
        functools.partial(prepare_far, part),
        [shape((far_rows, LANES), BF), shape((tile_rows, LANES), BF), shape((pad, LANES), F32)],
        [land_mask, held[0], *held[3:]],
        [
            pltpu.VMEM(((rows // 2 + 1) * pad, cols), F32),
            pltpu.VMEM((hid, wide), BF),
            turn,
            pltpu.VMEM((channels, wide), BF),
            pltpu.VMEM((channels, wide), BF),
        ],
        "far_rows",
    )
    masked, *strips = call(
        prepare_state,
        [block] + strip_shapes(pad),
        [ocean_state, land_mask],
        [flat],
        "state_rows",
        after=[taps],
    )
    cotan, own, to_core = call(
        prepare_near,
        [block, shape((near_rows, LANES), BF), shape((near_rows, LANES), BF)],
        [land_mask, *held[0:3], tiles],
        [flat],
        "cotan_rows",
    )
    around, _ = exchange_halo(rows, strips, outer, swap, "state", after=[to_core])
    from_far = lax.ppermute(to_far, "ch", across)
    ones = functools.partial(conv_forward, part)
    conv_operands = [masked, *around, taps]
    conv_scratch = [
        pltpu.VMEM((rows // 2 + 2 * DIL, pad, cols), BF),
        pltpu.VMEM((pad, LANES), F32),
        pltpu.VMEM((pad, LANES), F32),
        pltpu.VMEM((rows // 2, pad, cols), BF),
    ]
    eighth = shape((part_rows // 2, pad, cols), BF)
    conv_far = call(
        functools.partial(ones, 1), [eighth] * 4, conv_operands, conv_scratch, "conv_away"
    )
    from_far = call(
        relay, [from_far], [from_far], (), "cotan_relay", aliases={0: 0}, after=around[1:2]
    )[0]
    passed = lax.ppermute(from_far, "ch", core)
    conv_near = call(
        functools.partial(ones, 0),
        [eighth] * 4,
        conv_operands,
        conv_scratch,
        "conv_here",
        after=[conv_far[0], passed],
    )
    both = [(i, i ^ 3) for i in range(n_ch)]
    halves = [
        [
            conv_near[2 * h],
            lax.ppermute(conv_near[2 * h + 1], "ch", core),
            lax.ppermute(conv_far[2 * h], "ch", across),
            lax.ppermute(conv_far[2 * h + 1], "ch", both),
        ]
        for h in range(2)
    ]
    act_grad, cotan_all, weights_all, weights_turned, *picks = call(
        functools.partial(activation_gradient, part),
        [
            shape((n_ch * hid, cells), F32),
            shape((depth, cells), BF),
            shape((n_ch * hid, wide), BF),
            shape((depth, n_ch * hid), BF),
            shape((channels, depth), BF),
            shape((channels, depth), BF),
        ],
        [own, lax.ppermute(to_core, "ch", core), from_far, passed, land_mask, *held[1:3]],
        (),
        "activation_gradient",
    )
    pre_grad, sums = [], ()
    for h in range(2):
        pre, *sums = call(
            functools.partial(hidden_gradient, h),
            [
                shape((n_ch * hid, cells // 2), BF),
                shape((2, sum_rows, LANES), F32),
                shape((2, sum_rows, LANES), BF if h else F32),
            ],
            [*halves[h], act_grad, cotan_all, weights_all, *sums],
            [pltpu.VMEM((depth, cells // 2), BF), pltpu.VMEM((n_ch * hid, cells // 2), BF)],
            "hidden_first" if h == 0 else "hidden_second",
        )
        pre_grad.append(pre)
    keep, send = sums
    got = lax.ppermute(send, "ch", core)
    grad_scratch = [pltpu.VMEM((2 * pad, cells), BF)]
    grad_far = call(
        functools.partial(conv_gradient, 1),
        [shape((2, part_rows, pad, cols), BF)],
        [*pre_grad, weights_turned],
        grad_scratch,
        "gradient_away",
    )[0]
    grad_own, grad_core = call(
        functools.partial(conv_gradient, 0),
        [quarter] * 2,
        [*pre_grad, weights_turned],
        grad_scratch,
        "gradient_here",
        after=[grad_far],
    )
    grad_near = lax.ppermute(grad_core, "ch", core)
    grad_far = lax.ppermute(grad_far, "ch", across)
    staged = two_by_four()
    padded = shape((rows + 2 * DIL, pad, cols), BF)
    if not staged:
        shifted = call(shift_columns, [padded, padded], [masked, *around], (), "shift_columns")
    if staged:
        piece = sum_rows // 4
        mine, *sends = call(
            add_cores,
            [shape((2, piece, LANES), F32)] + [shape((2, piece, LANES), BF)] * 3,
            [keep, got],
            (),
            "add_cores",
        )

        shifted = call(
            shift_columns, [padded, padded], [masked, *around], (), "shift_columns", after=sends[:1]
        )

        def turn_plane(k):
            pairs = []
            for lon in range(n_lon):
                for lat in range(n_lat):
                    pairs.append((lon * n_lat + lat, (lon ^ (k & 1)) * n_lat + (lat ^ (k >> 1))))
            return pairs

        def over_plane(values):
            return [lax.ppermute(values[k - 1], ("lon", "lat"), turn_plane(k)) for k in (1, 2, 3)]

        mine, other = call(
            add_pieces,
            [shape((piece, LANES), F32), shape((piece + 112, LANES), BF)],
            [mine, *over_plane(sends)],
            (),
            "add_pieces",
            after=[grad_near, shifted[0]],
        )
    passed = call(
        second_half, [quarter], [grad_far], (), "grad_half", after=[other] if staged else []
    )[0]
    conv_grad, *grad_strips = call(
        functools.partial(collect_grad, swap),
        [block] + strip_shapes(pad) + outer_shapes(pad, swap),
        [grad_own, grad_near, grad_far, lax.ppermute(passed, "ch", core)],
        (),
        "grad_rows",
    )
    kernel_part = call(
        kernel_gradient,
        [shape((pad, LANES), BF)],
        [conv_grad, masked, around[0], *shifted],
        (),
        "kernel_gradient",
    )[0]
    grad_around, marks = exchange_halo(rows, grad_strips[:3], grad_strips[3:], swap, "grad", planes=4, riding=[kernel_part])
    if staged:
        mine = call(
            add_across,
            [shape((piece, LANES), BF)],
            [mine, lax.ppermute(other, "ch", across)],
            (),
            "add_across",
        )[0]
    state_grad, mark = call(
        conv_adjoint,
        [shape((part, rows, cols), BF), shape((8, LANES), F32)],
        [conv_grad, *grad_around, taps, cotan, land_mask],
        [
            pltpu.VMEM((17 * (rows + 8), cols), F32),
            pltpu.VMEM((part, rows, cols), BF),
            pltpu.SemaphoreType.DMA((-(-part // 16),)),
        ],
        "conv_adjoint",
        writes=1,
    )
    outs = [
        shape((hidden, channels), F32),
        shape((hidden, channels), F32),
        shape((1, hidden), F32),
        shape((3, 3, part), F32),
    ]
    if staged:
        far_lon = [(lon, lon ^ 2) for lon in range(n_lon)]
        summed = call(
            finish_pieces,
            [shape((piece + TAP_ROWS, LANES), BF)],
            [
                mine,
                lax.ppermute(mine, "lon", far_lon),
                kernel_part,
                marks[1],
            ],
            [turn],
            "finish_pieces",
            after=marks[2:],
        )[0]
        expand_grad, project_grad, bias_grad, kernel_grad = call(
            functools.partial(write_parameters, part, pad, scale, hid),
            outs,
            [summed, *over_plane([summed] * 3), *picks],
            [pltpu.VMEM((sum_rows, LANES), BF), pltpu.VMEM((4 * TAP_ROWS, LANES), F32)],
            "write_parameters",
            after=[mark],
        )
    else:
        total = keep + got.astype(F32)
        total = total[0] + lax.ppermute(total[1].astype(BF), "ch", across).astype(F32)
        total, kernel_sum = lax.psum((total, kernel_part.astype(F32)), ("lon", "lat"))
        expand_grad, project_grad, bias_grad, kernel_grad = call(
            functools.partial(unpack_whole, part, pad, scale, hid),
            outs,
            [total.astype(BF), kernel_sum, *picks],
            [turn],
            "write_parameters",
        )
    return (
        state_grad,
        expand_grad.T,
        project_grad,
        bias_grad.reshape(hidden),
        kernel_grad,
    )


def solution(mesh):
    return jax.shard_map(
        on_device,
        mesh=mesh,
        in_specs=(
            P("ch", "lat", "lon"),
            P("lat", "lon"),
            P("ch", "lat", "lon"),
            P("lat", "lon", None),
            P("lat", "lon", None),
            P(None, None, "ch"),
            P(None, "ch"),
            P("ch"),
            P("ch", None),
        ),
        out_specs=(
            P("ch", "lat", "lon"),
            P(None, "ch"),
            P("ch", None),
            P("ch"),
            P(None, None, "ch"),
        ),
        check_vma=False,
    )
```

```python
import functools
import math

import jax
import jax.numpy as jnp
from jax import lax
from jax.experimental import pallas as pl
from jax.experimental.pallas import tpu as pltpu
from jax.sharding import PartitionSpec as P

DIL = 2
LANES = 128
TAP_ROWS = 16
RIDE = 96
BF = jnp.bfloat16
F32 = jnp.float32


def shape(dims, kind):
    return jax.ShapeDtypeStruct(dims, kind)


def call(kernel, outs, args, scratch=(), name=None, flops=0, aliases=None, far=False, after=(), writes=0):
    count = len(args)
    if after:
        body, args = kernel, [*args, *after]

        def kernel(*refs):
            body(*refs[:count], *refs[len(args) :])

    if far:
        args = [pltpu.with_memory_space_constraint(a, pltpu.HBM) for a in args]
    spaces = [pltpu.HBM if far else pl.ANY if i >= count else pltpu.VMEM for i in range(len(args))]
    moved = sum(math.prod(a.shape) * a.dtype.itemsize for a in list(args) + list(outs))
    return pl.pallas_call(
        kernel,
        out_shape=tuple(outs),
        in_specs=[pl.BlockSpec(memory_space=space) for space in spaces],
        out_specs=tuple(
            pl.BlockSpec(memory_space=pl.ANY if i < writes else pltpu.VMEM) for i in range(len(outs))
        ),
        scratch_shapes=list(scratch),
        input_output_aliases=aliases or {},
        name=name,
        compiler_params=pltpu.CompilerParams(vmem_limit_bytes=24 * 1024 * 1024),
        cost_estimate=pl.CostEstimate(flops=flops, bytes_accessed=moved, transcendentals=0),
    )(*args)


def iota(dims, dim):
    return lax.broadcasted_iota(jnp.int32, dims, dim)


def aligned(index):
    return pl.multiple_of(index, 16)


def to_rows(block_ref, weight, scr, pad):
    channels, rows, cols = block_ref.shape

    def body(c, carry):
        value = block_ref[c].astype(F32)
        if weight is not None:
            value = value * weight
        scr[pl.ds(c, rows, stride=pad), :] = value
        return carry

    lax.fori_loop(0, channels, body, 0, unroll=5 if channels % 5 == 0 else 1)
    for c in range(channels, pad):
        scr[pl.ds(c, rows, stride=pad), :] = jnp.zeros((rows, cols), F32)


def pack_columns(value, ext_row, left, right):
    lane = iota(value.shape, 1)
    here = (lane == 2 * ext_row) | (lane == 2 * ext_row + 1)
    size = value.shape[1]
    left = jnp.where(here, pltpu.roll(value, (2 * ext_row) % size, 1), left)
    right = jnp.where(here, pltpu.roll(value, (2 * ext_row + 2) % size, 1), right)
    return left, right


def mirrored(value):
    size = value.shape[1]
    flip = (iota((size, size), 0) + iota((size, size), 1) == size - 1).astype(BF)
    return jnp.dot(value, flip, preferred_element_type=F32).astype(BF)


def emit_strips(read, rows, pad, fold_ref, left_ref, right_ref):
    for t in range(DIL):
        fold_ref[t] = mirrored(read(rows - 1 - t))
    left = jnp.zeros((pad, LANES), F32)
    right = jnp.zeros((pad, LANES), F32)
    for r in range(rows):
        left, right = pack_columns(read(r).astype(F32), r + DIL, left, right)
    left_ref[...] = left.astype(BF)
    right_ref[...] = right.astype(BF)


def strip_shapes(pad):
    return [shape((DIL, pad, LANES), BF)] + [shape((pad, LANES), BF)] * 2


def outer_shapes(pad, swap):
    return [shape((DIL, pad, LANES), BF)] * (1 if swap else 2)


def emit_outer(low, high, t, swap, outer):
    if swap:
        outer[0][t] = jnp.where(lax.axis_index("lat") == 0, high, low).astype(BF)
    else:
        outer[0][t] = low.astype(BF)
        outer[1][t] = high.astype(BF)


def prepare_state(state_ref, mask_ref, rows_ref, fold_ref, left_ref, right_ref, scr):
    rows, pad = rows_ref.shape[:2]
    to_rows(state_ref, mask_ref[...].astype(F32), scr, pad)
    for r in range(rows):
        rows_ref[r] = scr[r * pad : (r + 1) * pad, :].astype(BF)
    emit_strips(lambda r: rows_ref[r], rows, pad, fold_ref, left_ref, right_ref)


def swath_rows(rows, start, offset_ref, value_ref, cols):
    offset = offset_ref[...]
    points = offset.shape[1]
    value = value_ref[...]
    total = jnp.zeros((rows, cols), F32)
    row = lax.shift_right_logical(offset, LANES.bit_length() - 1)
    row_hot = iota((rows, points), 0) + start == row
    col_hot = (iota((cols, points), 0) == (offset & (LANES - 1))).astype(BF)
    for _ in range(3):
        part = value.astype(BF)
        value = value - part.astype(F32)
        lhs = jnp.where(row_hot, part.astype(F32), 0.0).astype(BF)
        total = total + lax.dot_general(
            lhs, col_hot, (((1,), (1,)), ((), ())), preferred_element_type=F32
        )
    return total


def with_first(tile, row):
    lifted = jnp.broadcast_to(row, tile.shape)
    return jnp.where(iota(tile.shape, 0) == 0, tile.astype(F32) + lifted, tile.astype(F32))


def prepare_outer(part, swap, count, *refs):
    outs, (row_scr, sems) = refs[count:-2], refs[-2:]
    (*outer, pick_e, pick_p), held = outs[:-count], outs[-count:]
    state_ref, mask_ref = held[0:2]
    copies = [pltpu.make_async_copy(refs[k], held[k], sems.at[k]) for k in range(count)]
    for copy in copies:
        copy.start()
    pad = outer[0].shape[1]
    channels, rows, cols = state_ref.shape
    half = rows // 2
    lat = lax.axis_index("lat")
    for c in range(channels, pad):
        row_scr[pl.ds(c, 2 * DIL, stride=pad), :] = jnp.zeros((2 * DIL, cols), F32)
    weight_picks(part, pad, pick_e.shape[1], pick_e.shape[0], pick_e, pick_p)
    copies[1].wait()
    copies[0].wait()
    if swap:
        start = aligned((1 - lat) * half)
        mask = mask_ref[pl.ds(start, half), :].astype(F32)

        def body(c, carry):
            value = state_ref[c, pl.ds(start, half), :].astype(F32) * mask
            row_scr[pl.ds(c, DIL, stride=pad), :] = jnp.where(
                lat == 0, value[half - DIL :, :], value[0:DIL, :]
            )
            return carry

    else:
        mask = mask_ref[...].astype(F32)

        def body(c, carry):
            value = state_ref[c].astype(F32) * mask
            row_scr[pl.ds(c, DIL, stride=pad), :] = value[0:DIL, :]
            row_scr[pl.ds(DIL * pad + c, DIL, stride=pad), :] = value[rows - DIL :, :]
            return carry

    lax.fori_loop(0, channels, body, 0, unroll=5 if channels % 5 == 0 else 1)
    for k, to in enumerate(outer):
        for t in range(DIL):
            at = (k * DIL + t) * pad
            to[t] = row_scr[at : at + pad, :].astype(BF)
    for copy in copies[2:]:
        copy.wait()


def prepare_far(part, *refs):
    (mask_ref, grad_ref), weights, (pick_e, pick_p) = refs[0:2], refs[2:6], refs[6:8]
    far_ref, tiles_ref, taps_ref = refs[8:11]
    scr, weights_scr, turn_scr = refs[11:]
    channels, rows, cols = grad_ref.shape
    pad = taps_ref.shape[0]
    pack_weights(part, pad, *weights, pick_e, pick_p, weights_scr, taps_ref, turn_scr)
    hid = weights_scr.shape[0]
    full = tiles_ref.shape[0]
    for t in range(full // hid):
        tiles_ref[t * hid : (t + 1) * hid, :] = weights_scr[:, t * LANES : (t + 1) * LANES]
    far_ref[0:full, :] = tiles_ref[...]
    half = rows // 2
    me = lax.axis_index("ch")
    start = aligned((1 - me // 2) * half)

    def body(c, carry):
        scr[pl.ds(c, half, stride=pad), :] = grad_ref[c, pl.ds(start, half), :].astype(F32)
        return carry

    lax.fori_loop(0, channels, body, 0, unroll=5 if channels % 5 == 0 else 1)
    for c in range(channels, pad):
        scr[pl.ds(c, half, stride=pad), :] = jnp.zeros((half, cols), F32)
    mask = mask_ref[pl.ds(start, half), :].astype(F32)
    count_rows = half // 2
    for r in range(half):
        scr[r * pad : (r + 1) * pad, :] = scr[r * pad : (r + 1) * pad, :] * mask[r : r + 1, :]
    for k in range(2):
        first = aligned((((me ^ (2 + k)) % 2) * count_rows) * pad)
        size = count_rows * pad
        far_ref[full + k * size : full + (k + 1) * size, :] = scr[pl.ds(first, size), :].astype(BF)


def prepare_near(mask_ref, grad_ref, offset_ref, value_ref, tiles_ref, rows_ref, own_ref, core_ref, scr):
    rows, pad, cols = rows_ref.shape
    mask = mask_ref[...].astype(F32)
    to_rows(grad_ref, None, scr, pad)
    for r in range(rows):
        rows_ref[r] = (scr[r * pad : (r + 1) * pad, :] * mask[r : r + 1, :]).astype(BF)
    full = tiles_ref.shape[0]
    count = (own_ref.shape[0] - full) // pad
    me = lax.axis_index("ch")
    for k, to in enumerate((own_ref, core_ref)):
        to[0:full, :] = tiles_ref[...]
        for r in range(count):
            at = full + r * pad
            to[at : at + pad, :] = rows_ref[(me ^ k) * count + r]
    swath = swath_rows(rows, 0, offset_ref, value_ref, cols) * mask
    swath = jnp.where(me == 0, swath, 0.0)
    for r in range(rows):
        rows_ref[r, 0:16, :] = with_first(rows_ref[r, 0:16, :], swath[r : r + 1, :]).astype(BF)


def second_half(in_ref, out_ref):
    out_ref[...] = in_ref[1]


def relay(in_ref, out_ref):
    del in_ref, out_ref


def ring(count, step):
    return [(i, (i + step) % count) for i in range(count)]


def finish_columns(rows, swap, *refs):
    if swap:
        strip_ref, fold_ref, left_ref, right_ref, halo_ref, left_out, right_out = refs
        low_ref = high_ref = strip_ref
    else:
        low_ref, high_ref, fold_ref, left_ref, right_ref, halo_ref, left_out, right_out = refs
    lat, count = lax.axis_index("lat"), lax.axis_size("lat")
    left, right = left_ref[...].astype(F32), right_ref[...].astype(F32)
    for t in range(DIL):
        south = jnp.where(lat == 0, 0.0, low_ref[t].astype(F32))
        north = jnp.where(lat == count - 1, fold_ref[t].astype(F32), high_ref[t].astype(F32))
        halo_ref[t] = south.astype(BF)
        halo_ref[DIL + t] = north.astype(BF)
        left, right = pack_columns(south, t, left, right)
        left, right = pack_columns(north, rows + DIL + t, left, right)
    left_out[...] = left.astype(BF)
    right_out[...] = right.astype(BF)


def odd_lon():
    return lax.axis_index("lon") % 2 == 1


def pack_for_third(rows, riding, *refs):
    if riding:
        ride_ref, *refs = refs
    got_ref, fold_ref, left_ref, right_ref, out_ref = refs
    low = lax.axis_index("lat") == 0
    left, right = left_ref[...].astype(F32), right_ref[...].astype(F32)
    for t in range(DIL):
        got = got_ref[t].astype(F32)
        left, right = pack_columns(jnp.where(low, 0.0, got), t, left, right)
        left, right = pack_columns(jnp.where(low, got, 0.0), rows + DIL + t, left, right)
        out_ref[t] = fold_ref[t]
    pack = jnp.where(odd_lon(), right, left)
    if riding:
        pack = pack + pltpu.roll(ride_ref[...].astype(F32), RIDE, 1)
    out_ref[DIL] = pack.astype(BF)


def pack_for_first(rows, got_ref, fold_ref, left_ref, right_ref, third_ref, halo_ref, out_ref, side_ref):
    low = lax.axis_index("lat") == 0
    odd = odd_lon()
    left, right = left_ref[...].astype(F32), right_ref[...].astype(F32)
    side = third_ref[DIL].astype(F32)
    size = side.shape[1]
    lane = iota(side.shape, 1)
    for t in range(DIL):
        got = got_ref[t].astype(F32)
        south = jnp.where(low, 0.0, got)
        north = jnp.where(low, got, third_ref[t].astype(F32))
        halo_ref[t] = south.astype(BF)
        halo_ref[DIL + t] = north.astype(BF)
        left, right = pack_columns(south, t, left, right)
        left, right = pack_columns(north, rows + DIL + t, left, right)
        at = 2 * (rows + DIL + t)
        own = fold_ref[t].astype(F32)
        own = jnp.where(
            odd, pltpu.roll(own, at, 1), pltpu.roll(own, (at - (size - DIL)) % size, 1)
        )
        here = jnp.logical_and((lane == at) | (lane == at + 1), jnp.logical_not(low))
        side = jnp.where(here, own, side)
    out_ref[0] = jnp.where(odd, left, right).astype(BF)
    for k in range(1, out_ref.shape[0]):
        out_ref[k] = jnp.zeros(side.shape, BF)
    side_ref[...] = side.astype(BF)


def two_by_four():
    return lax.axis_size("lat") == 2 and lax.axis_size("lon") == 4


def exchange_halo(rows, strips, outer, swap, name, planes=1, riding=(), after=()):
    n_lat, n_lon = lax.axis_size("lat"), lax.axis_size("lon")
    fold, left, right = strips
    pad = left.shape[0]
    halo_shape, pack = shape((2 * DIL, pad, LANES), BF), shape((pad, LANES), BF)
    if two_by_four():
        got = lax.ppermute(outer[0], "lat", [(0, 1), (1, 0)])
        third_out = call(
            functools.partial(pack_for_third, rows, len(riding) > 0),
            [shape((DIL + 1, pad, LANES), BF)],
            [*riding, got, fold, left, right],
            (),
            name + "_third",
            after=after,
        )[0]
        third = lax.ppermute(third_out, "lon", [(lon, lon ^ 3) for lon in range(n_lon)])
        halo, first, side = call(
            functools.partial(pack_for_first, rows),
            [halo_shape, shape((planes, pad, LANES), BF), pack],
            [got, fold, left, right, third],
            (),
            name + "_first",
        )
        got = lax.ppermute(first, "lon", [(lon, lon ^ 1) for lon in range(n_lon)])
        return (halo, got, side), (third_out, third, first)
    top = n_lat - 1
    fold_pairs = [(lon * n_lat + top, (n_lon - 1 - lon) * n_lat + top) for lon in range(n_lon)]
    if swap:
        moved = [lax.ppermute(outer[0], "lat", [(0, 1), (1, 0)])]
    else:
        moved = [
            lax.ppermute(outer[1], "lat", [(i, i + 1) for i in range(n_lat - 1)]),
            lax.ppermute(outer[0], "lat", [(i + 1, i) for i in range(n_lat - 1)]),
        ]
    fold = lax.ppermute(fold, ("lon", "lat"), fold_pairs)
    halo, left, right = call(
        functools.partial(finish_columns, rows, swap),
        [halo_shape, pack, pack],
        [*moved, fold, left, right],
        (),
        name + "_columns",
    )
    from_right = lax.ppermute(left, "lon", ring(n_lon, -1))
    from_left = lax.ppermute(right, "lon", ring(n_lon, 1))
    return (halo, from_left, from_right), ()


def padded_row(block_ref, halo_ref, at, e):
    rows = block_ref.shape[0]
    if e < DIL:
        return halo_ref[e, at, :]
    if e < rows + DIL:
        return block_ref[e - DIL, at, :]
    return halo_ref[e - rows, at, :]


def sides(left_ref, right_ref, at):
    left = (left_ref[0, at, :] if two_by_four() else left_ref[at, :]).astype(F32)
    right = right_ref[at, :].astype(F32)
    if two_by_four():
        odd = odd_lon()
        left, right = jnp.where(odd, left, right), jnp.where(odd, right, left)
    return left, right


def shifted_rows(rows, read, left, right):
    lane = iota((16, LANES), 1)
    for e in range(rows + 2 * DIL):
        row = read(e).astype(F32)
        west = jnp.where(
            lane < DIL, pltpu.roll(left, (-2 * e) % LANES, 1), pltpu.roll(row, DIL, 1)
        )
        east = jnp.where(
            lane >= LANES - DIL,
            pltpu.roll(right, (LANES - DIL - 2 * e) % LANES, 1),
            pltpu.roll(row, LANES - DIL, 1),
        )
        yield e, (west, row, east)


def stencil_rows(rows, read, left, right, taps, north, emit):
    sums = {}
    for e, shifts in shifted_rows(rows, read, left, right):
        for a in (2, 1, 0):
            r = e - DIL * a
            if not 0 <= r < rows:
                continue
            used = north if e >= rows + DIL else taps[a]
            term = used[0] * shifts[0] + used[1] * shifts[1] + used[2] * shifts[2]
            sums[r] = term if r not in sums else sums[r] + term
            if a == 2:
                emit(r, sums.pop(r))


def stencil(block_ref, halo_ref, left_ref, right_ref, group, taps, north, emit):
    at = pl.ds(aligned(group * 16), 16)
    left, right = sides(left_ref, right_ref, at)
    read = functools.partial(padded_row, block_ref, halo_ref, at)
    stencil_rows(block_ref.shape[0], read, left, right, taps, north, emit)


def spread(tap_ref, group):
    values = tap_ref[pl.ds(aligned(group * 16), 16), :]
    return [
        [jnp.broadcast_to(values[:, 3 * a + b : 3 * a + b + 1], (16, LANES)) for b in range(3)]
        for a in range(3)
    ]


def conv_forward(ones_row, away, block_ref, halo_ref, left_ref, right_ref, tap_ref, *rest):
    outs, (row_scr, left_scr, right_scr, scr) = rest[:-4], rest[-4:]
    rows, pad = block_ref.shape[:2]
    half = rows // 2
    me = lax.axis_index("ch")
    upper = (me // 2 + away) % 2
    west, east = sides(left_ref, right_ref, slice(None))
    left_scr[...] = pltpu.roll(west, (LANES - 2 * half * upper) % LANES, 1)
    right_scr[...] = pltpu.roll(east, (LANES - 2 * half * upper) % LANES, 1)
    for t in range(DIL):
        low, high = halo_ref[t].astype(F32), halo_ref[DIL + t].astype(F32)
        before = block_ref[half - DIL + t].astype(F32)
        behind = block_ref[half + t].astype(F32)
        row_scr[t] = jnp.where(upper == 0, low, before).astype(BF)
        row_scr[half + DIL + t] = jnp.where(upper == 0, behind, high).astype(BF)
    for r in range(half):
        row_scr[DIL + r] = block_ref[upper * half + r]

    def body(group, carry):
        taps = spread(tap_ref, group)
        is_one = iota((16, LANES), 0) + group * 16 == ones_row
        at = pl.ds(aligned(group * 16), 16)

        def emit(r, value):
            value = jnp.where(is_one, 1.0, value)
            scr[r, at, :] = value.astype(BF)

        left, right = left_scr[at, :], right_scr[at, :]
        stencil_rows(half, lambda e: row_scr[e, at, :], left, right, taps, taps[2], emit)
        return carry

    lax.fori_loop(0, pad // 16, body, 0)
    count = half // 2
    size = outs[0].shape[0]
    for k, to in enumerate(outs):
        first = ((me + k % 2) % 2) * count
        to[...] = scr[pl.ds(first + k // 2 * size, size)]


def conv_adjoint(
    block_ref, halo_ref, left_ref, right_ref, tap_ref, cotan_ref, mask_ref, out_ref, mark_ref, scr, done_scr, sems
):
    rows, pad = block_ref.shape[:2]
    channels = out_ref.shape[0]
    at_top = lax.axis_index("lat") == lax.axis_size("lat") - 1
    mask = mask_ref[...].astype(F32)

    def copy(group, count):
        at = pl.ds(group * 16, count)
        return pltpu.make_async_copy(done_scr.at[at], out_ref.at[at], sems.at[group])

    def body(group, count):
        taps = spread(tap_ref, group)
        back = [[taps[2 - a][2 - b] for b in range(3)] for a in range(3)]
        north = [jnp.where(at_top, taps[2][b], back[2][b]) for b in range(3)]

        def emit(r, value):
            cotan = cotan_ref[r, pl.ds(aligned(group * 16), 16), :].astype(F32)
            scr[pl.ds(r, 16, stride=rows + 8), :] = (cotan + value) * mask[r : r + 1, :]

        stencil(block_ref, halo_ref, left_ref, right_ref, group, back, north, emit)
        for c in range(count):
            at = c * (rows + 8)
            done_scr[group * 16 + c] = scr[at : at + rows, :].astype(BF)
        copy(group, count).start()

    whole = channels // 16

    def each(group, carry):
        body(group, 16)
        return carry

    lax.fori_loop(0, whole, each, 0)
    if channels % 16:
        body(whole, channels % 16)
    mark_ref[...] = jnp.zeros(mark_ref.shape, F32)
    for group in range(whole):
        copy(group, 16).wait()
    if channels % 16:
        copy(whole, channels % 16).wait()


def collect_grad(swap, own, near, far, passed, rows_ref, *rest):
    part_rows = own.shape[0]
    rows, pad = rows_ref.shape[:2]
    me = lax.axis_index("ch")
    for k, quarter in enumerate((own, near, far.at[0], passed)):
        rows_ref[pl.ds((me ^ k) * part_rows, part_rows)] = quarter[...]
    strips, outer = rest[:3], rest[3:]
    for t in range(DIL):
        emit_outer(rows_ref[t].astype(F32), rows_ref[rows - DIL + t].astype(F32), t, swap, outer)
    emit_strips(lambda r: rows_ref[r], rows, pad, *strips)


def shift_columns(block_ref, halo_ref, left_ref, right_ref, west_ref, east_ref):
    def body(group, carry):
        at = pl.ds(aligned(group * 16), 16)
        left, right = sides(left_ref, right_ref, at)
        read = functools.partial(padded_row, block_ref, halo_ref, at)
        for e, shifts in shifted_rows(block_ref.shape[0], read, left, right):
            west_ref[e, at, :] = shifts[0].astype(BF)
            east_ref[e, at, :] = shifts[2].astype(BF)
        return carry

    lax.fori_loop(0, block_ref.shape[1] // 16, body, 0)


def kernel_gradient(grad_ref, block_ref, halo_ref, west_ref, east_ref, out_ref):
    rows, pad = grad_ref.shape[:2]

    def body(group, carry):
        at = pl.ds(aligned(group * 16), 16)
        sums = [[jnp.zeros((16, LANES), F32) for _ in range(3)] for _ in range(3)]
        for e in range(rows + 2 * DIL):
            middle = padded_row(block_ref, halo_ref, at, e)
            shifts = [part.astype(F32) for part in (west_ref[e, at, :], middle, east_ref[e, at, :])]
            for a in range(3):
                r = e - DIL * a
                if 0 <= r < rows:
                    grad = grad_ref[r, at, :].astype(F32)
                    for b in range(3):
                        sums[a][b] = sums[a][b] + grad * shifts[b]
        lane = iota((16, LANES), 1)
        out = jnp.zeros((16, LANES), F32)
        for a in range(3):
            for b in range(3):
                total = jnp.sum(sums[a][b], axis=1, keepdims=True)
                out = jnp.where(lane == 3 * a + b, total, out)
        out_ref[at, :] = out.astype(BF)
        return carry

    lax.fori_loop(0, pad // 16, body, 0)


def channel_of(slot, part, pad):
    block = sum((slot >= pad * b).astype(jnp.int32) for b in range(1, 4))
    inside = slot - block * pad
    return jnp.where((slot >= 0) & (slot < 4 * pad) & (inside < part), block * part + inside, -1)


def expand_slot(lane, pad):
    return jnp.where(lane < 4 * pad, lane, -1)


def project_slot(lane, pad, split):
    tail = 4 * pad - split
    low = LANES - tail
    return jnp.where(lane >= LANES, lane - LANES, jnp.where(lane >= low, lane - low + split, -1))


def weight_picks(part, pad, wide, channels, pick_e_ref, pick_p_ref):
    split = 4 * pad // LANES * LANES
    lane = iota((channels, wide), 1)
    row = iota((channels, wide), 0)
    pick_e_ref[...] = (channel_of(expand_slot(lane, pad), part, pad) == row).astype(BF)
    slot = jnp.where(lane >= split, project_slot(lane - split, pad, split), -1)
    pick_p_ref[...] = (channel_of(slot, part, pad) == row).astype(BF)


def output_picks(part, pad, pick_e_ref, pick_p_ref):
    channels, depth = pick_e_ref.shape
    split = 4 * pad // LANES * LANES
    lane, row = iota((channels, depth), 1), iota((channels, depth), 0)
    pick_e_ref[...] = (channel_of(expand_slot(lane, pad), part, pad) == row).astype(BF)
    pick_p_ref[...] = (channel_of(project_slot(lane, pad, split), part, pad) == row).astype(BF)


def pack_weights(
    part, pad, expand_ref, bias_ref, project_ref, kernel_ref, pick_e_ref, pick_p_ref, out_ref, taps_ref, turn_scr
):
    hidden, channels = expand_ref.shape
    turn_scr[...] = jnp.zeros(turn_scr.shape, F32)
    for a in range(3):
        turn_scr[3 * a : 3 * a + 3, 0:part] = kernel_ref[a]
    taps_ref[...] = jnp.transpose(turn_scr[...])[0:pad, :]
    wide = out_ref.shape[1]
    bias = bias_ref[...]
    parts = jnp.zeros((16, hidden), F32)
    at = iota((16, hidden), 0)
    for k in range(3):
        piece = bias.astype(BF).astype(F32)
        bias = bias - piece
        parts = jnp.where(at == k, piece, parts)
    lane, row = iota((16, wide), 1), iota((16, wide), 0)
    pick_b = ((lane == row * pad + part) & (row < 3)).astype(BF)
    turned = (((0,), (0,)), ((), ()))
    packed = (
        jnp.dot(expand_ref[...], pick_e_ref[...], preferred_element_type=F32)
        + lax.dot_general(parts.astype(BF), pick_b, turned, preferred_element_type=F32)
        + jnp.dot(project_ref[...], pick_p_ref[...], preferred_element_type=F32)
    )
    rows = out_ref.shape[0]
    out_ref[0:hidden, :] = packed.astype(BF)
    out_ref[hidden:rows, :] = jnp.zeros((rows - hidden, wide), BF)


GELU_C = math.sqrt(2.0 / math.pi)


def activation_gradient(part, *refs):
    parts, (mask_ref, offset_ref, value_ref) = refs[0:4], refs[4:7]
    act_ref, y_scr, w_scr, t_scr, pick_e_ref, pick_p_ref = refs[7:]
    me = lax.axis_index("ch")
    tiles = w_scr.shape[1] // LANES
    hid = w_scr.shape[0] // 4
    depth, cells = y_scr.shape
    part_rows = cells // LANES
    pad = (parts[0].shape[0] - tiles * hid) // part_rows
    split = 4 * pad // LANES * LANES
    output_picks(part, pad, pick_e_ref, pick_p_ref)
    y_scr[0 : depth - 4 * pad, :] = jnp.zeros((depth - 4 * pad, cells), BF)
    for k, ref in enumerate(parts):
        for t in range(tiles):
            w_scr[k * hid : (k + 1) * hid, t * LANES : (t + 1) * LANES] = ref[
                t * hid : (t + 1) * hid, :
            ]
        block = me ^ k
        start = tiles * hid + (part_rows * pad if k == 3 else 0)
        for r in range(part_rows):
            cols = slice(r * LANES, (r + 1) * LANES)
            for u in range(pad // 16):
                slot = block * pad + 16 * u
                to = jnp.where(slot < split, slot + LANES, slot - split + depth - 4 * pad)
                at = start + r * pad + 16 * u
                y_scr[pl.ds(aligned(to), 16), cols] = ref[at : at + 16, :]
    rows = pl.ds(pl.multiple_of(me * part_rows, part_rows), part_rows)
    swath = swath_rows(part_rows, me * part_rows, offset_ref, value_ref, LANES)
    swath = swath * mask_ref[rows, :].astype(F32)
    for r in range(part_rows):
        at = (slice(LANES, LANES + 16), slice(r * LANES, (r + 1) * LANES))
        y_scr[at] = with_first(y_scr[at], swath[r : r + 1, :]).astype(BF)
    t_scr[...] = jnp.transpose(w_scr[:, 0:depth])
    step = 256
    for start in range(0, cells, step):
        cols = slice(start, start + step)
        act_ref[:, cols] = jnp.dot(
            w_scr[:, split : split + depth], y_scr[:, cols], preferred_element_type=F32
        )


def hidden_gradient(half, *refs):
    xs, (act_ref, y_ref, w_ref), refs = refs[0:4], refs[4:7], refs[7:]
    sums = ()
    if half:
        sums, refs = refs[0:2], refs[2:]
    pre_ref, keep_ref, send_ref, x_scr, value_scr = refs
    part_rows, pad = xs[0].shape[:2]
    hid = w_ref.shape[0] // 4
    split = 4 * pad // LANES * LANES
    depth, cells = x_scr.shape
    offset = half * cells
    me = lax.axis_index("ch")
    x_scr[4 * pad : depth, :] = jnp.zeros((depth - 4 * pad, cells), BF)
    for k in range(4):
        for r in range(part_rows):
            cols = slice(r * LANES, (r + 1) * LANES)
            x_scr[pl.ds(aligned((me ^ k) * pad), pad), cols] = xs[k][r]
    step = 256
    for start in range(0, cells, step):
        cols = slice(start, start + step)
        hidden = jnp.dot(w_ref[:, 0:depth], x_scr[:, cols], preferred_element_type=F32)
        square = hidden * hidden
        tanh = jnp.tanh(hidden * (GELU_C + (0.044715 * GELU_C) * square))
        each = 0.5 + 0.5 * tanh
        slope = each + hidden * (0.5 * GELU_C + (1.5 * 0.044715 * GELU_C) * square) * (
            1.0 - tanh * tanh
        )
        value_scr[:, cols] = (hidden * each).astype(BF)
        pre_ref[:, cols] = (act_ref[:, offset + start : offset + start + step] * slope).astype(BF)
    over_cells = (((1,), (1,)), ((), ()))
    expand = lax.dot_general(pre_ref[...], x_scr[...], over_cells, preferred_element_type=F32)
    project = lax.dot_general(
        value_scr[...], y_ref[:, offset : offset + cells], over_cells, preferred_element_type=F32
    )
    shared = split // LANES
    tiles = [expand[:, t * LANES : (t + 1) * LANES] for t in range(shared)]
    tiles.append(expand[:, split : split + LANES] + project[:, 0:LANES])
    tiles += [project[:, t * LANES : (t + 1) * LANES] for t in range(1, shared + 1)]
    used = len(tiles) * hid
    for ref in (keep_ref, send_ref):
        for k in range(2):
            ref[k, used:, :] = jnp.zeros((ref.shape[1] - used, LANES), ref.dtype)
    for k in range(4):
        to = send_ref if k % 2 else keep_ref
        for t, tile in enumerate(tiles):
            at = (k // 2, slice(t * hid, (t + 1) * hid), slice(None))
            value = tile[k * hid : (k + 1) * hid]
            if half:
                value = value + sums[k % 2][at]
            to[at] = value.astype(to.dtype)


def conv_gradient(away, first_ref, second_ref, t_ref, *rest):
    outs, scr = rest[:-1], rest[-1]
    if away:
        outs = (rest[0].at[0], rest[0].at[1])
    part_rows, pad = outs[0].shape[:2]
    me = lax.axis_index("ch")
    first = ((me // 2 + away) % 2) * 2 * pad
    weights = t_ref[pl.ds(aligned(first), 2 * pad), :]
    step = 256
    half = first_ref.shape[1]
    for start in range(0, 2 * half, step):
        pre = (first_ref if start < half else second_ref)[:, start % half : start % half + step]
        scr[:, start : start + step] = jnp.dot(weights, pre, preferred_element_type=F32).astype(BF)
    for k, to in enumerate(outs):
        at = pl.ds(aligned(((me + k) % 2) * pad), pad)
        for r in range(part_rows):
            to[r] = scr[at, r * LANES : (r + 1) * LANES]


def add_cores(keep_ref, got_ref, own_ref, *sends):
    piece = own_ref.shape[1]
    place = 2 * lax.axis_index("lat") + lax.axis_index("lon") % 2
    for k in range(4):
        at = pl.ds(aligned((place ^ k) * piece), piece)
        for group in range(2):
            total = keep_ref[group, at, :] + got_ref[group, at, :].astype(F32)
            to = sends[k - 1] if k else own_ref
            to[group] = total.astype(to.dtype)


def add_pieces(own_ref, a_ref, b_ref, c_ref, mine_ref, other_ref):
    for group, to in enumerate((mine_ref, other_ref)):
        total = own_ref[group] + (
            a_ref[group].astype(F32) + b_ref[group].astype(F32) + c_ref[group].astype(F32)
        )
        piece = total.shape[0]
        to[0:piece, :] = total.astype(to.dtype)
        if to.shape[0] > piece:
            to[piece:, :] = jnp.zeros((to.shape[0] - piece, LANES), to.dtype)


def add_across(mine_ref, got_ref, out_ref):
    piece = mine_ref.shape[0]
    out_ref[...] = (mine_ref[...] + got_ref[0:piece, :].astype(F32)).astype(BF)


def finish_pieces(mine_ref, line_ref, kernel_ref, third_ref, out_ref, turn_scr):
    piece, pad = mine_ref.shape[0], kernel_ref.shape[0]
    out_ref[0:piece, :] = (mine_ref[...].astype(F32) + line_ref[...].astype(F32)).astype(BF)
    other = pltpu.roll(third_ref[DIL].astype(F32), LANES - RIDE, 1)
    turn_scr[...] = jnp.zeros(turn_scr.shape, F32)
    turn_scr[0:pad, :] = kernel_ref[...].astype(F32) + other
    out_ref[piece:, :] = jnp.transpose(turn_scr[...])[0:TAP_ROWS, :].astype(BF)


def write_parameters(part, pad, scale, hid, p0, p1, p2, p3, pick_e, pick_p, *rest):
    expand_ref, project_ref, bias_ref, taps_ref, all_scr, taps_scr = rest
    piece = p0.shape[0] - TAP_ROWS
    place = 2 * lax.axis_index("lat") + lax.axis_index("lon") % 2
    for k, ref in enumerate((p0, p1, p2, p3)):
        to = place ^ k
        all_scr[pl.ds(aligned(to * piece), piece), :] = ref[0:piece, :]
        taps_scr[pl.ds(aligned(to * TAP_ROWS), TAP_ROWS), :] = ref[piece:, :].astype(F32)
    unpack(part, pad, scale, hid, all_scr, pick_e, pick_p, expand_ref, project_ref, bias_ref)
    total = taps_scr[0:TAP_ROWS, :]
    for k in range(1, 4):
        total = total + taps_scr[k * TAP_ROWS : (k + 1) * TAP_ROWS, :]
    write_taps(total, scale, taps_ref)


def write_taps(total, scale, taps_ref):
    for a in range(3):
        taps_ref[a] = total[3 * a : 3 * a + 3, 0 : taps_ref.shape[2]] * scale


def unpack(part, pad, scale, hid, all_ref, pick_e, pick_p, expand_ref, project_ref, bias_ref):
    hidden = expand_ref.shape[0]
    split = 4 * pad // LANES * LANES
    shared = split // LANES
    tiles = [all_ref[t * hid : (t + 1) * hid, :] for t in range(2 * shared + 1)]
    depth = (shared + 1) * LANES
    expand = jnp.concatenate(tiles[: shared + 1], axis=1)
    project = jnp.concatenate(tiles[shared:], axis=1)
    pick_b = (iota((16, depth), 1) == part).astype(BF)
    last = (((1,), (1,)), ((), ()))
    dot = functools.partial(lax.dot_general, dimension_numbers=last, preferred_element_type=F32)
    expand_ref[...] = dot(expand, pick_e[...])[0:hidden, :] * scale
    bias_ref[...] = dot(pick_b, expand)[0:1, 0:hidden] * scale
    project_ref[...] = dot(project, pick_p[...])[0:hidden, :] * scale


def unpack_whole(part, pad, scale, hid, all_ref, taps_in, pick_e, pick_p, *rest):
    expand_ref, project_ref, bias_ref, taps_ref, turn_scr = rest
    unpack(part, pad, scale, hid, all_ref, pick_e, pick_p, expand_ref, project_ref, bias_ref)
    turn_scr[...] = jnp.zeros(turn_scr.shape, F32)
    turn_scr[0:pad, :] = taps_in[...]
    write_taps(jnp.transpose(turn_scr[...])[0:TAP_ROWS, :], scale, taps_ref)


def on_device(
    ocean_state,
    land_mask,
    out_grad,
    swath_offset,
    swath_value,
    depth_kernel,
    expand_weight,
    expand_bias,
    project_weight,
):
    part, rows, cols = ocean_state.shape
    n_lon, n_lat, n_ch = lax.axis_size("lon"), lax.axis_size("lat"), lax.axis_size("ch")
    channels, hidden = expand_weight.shape
    assert n_ch == 4 and cols == LANES and rows % n_ch == 0
    pad = (part + 16) // 16 * 16
    hid = (hidden + 15) // 16 * 16
    split = n_ch * pad // LANES * LANES
    tail = n_ch * pad - split
    assert tail == LANES // 2
    wide = 2 * n_ch * pad
    depth = split + LANES
    part_rows = rows // n_ch
    cells = part_rows * cols
    swap = n_lat == 2
    scale = 1.0 / math.sqrt(rows * n_lat * cols * n_lon)
    core = [(i, i ^ 1) for i in range(n_ch)]
    across = [(i, i ^ 2) for i in range(n_ch)]
    block = shape((rows, pad, cols), BF)
    quarter = shape((part_rows, pad, cols), BF)
    flat = pltpu.VMEM(((rows + 1) * pad, cols), F32)

    turn = pltpu.VMEM((LANES, LANES), F32)

    tile_rows = wide // LANES * hid
    sum_rows = (tile_rows + 63) // 64 * 64
    near_rows, far_rows = tile_rows + part_rows * pad, tile_rows + 2 * part_rows * pad
    fetched = [
        ocean_state,
        land_mask,
        out_grad,
        swath_offset.reshape(1, -1),
        swath_value.reshape(1, -1),
        expand_weight.T,
        expand_bias.reshape(1, hidden),
        project_weight,
        depth_kernel,
    ]
    count = len(fetched)
    outs = call(
        functools.partial(prepare_outer, part, swap, count),
        outer_shapes(pad, swap)
        + [shape((channels, wide), BF)] * 2
        + [shape(a.shape, a.dtype) for a in fetched],
        fetched,
        [pltpu.VMEM(((2 * DIL + 1) * pad, cols), F32), pltpu.SemaphoreType.DMA((count,))],
        "outer_rows",
        far=True,
    )
    (*outer, pick_e, pick_p), (ocean_state, land_mask, *held) = outs[:-count], outs[-count:]
    to_far, tiles, taps = call(
        functools.partial(prepare_far, part),
        [shape((far_rows, LANES), BF), shape((tile_rows, LANES), BF), shape((pad, LANES), F32)],
        [land_mask, held[0], *held[3:], pick_e, pick_p],
        [
            pltpu.VMEM(((rows // 2 + 1) * pad, cols), F32),
            pltpu.VMEM((hid, wide), BF),
            turn,
        ],
        "far_rows",
    )
    masked, *strips = call(
        prepare_state,
        [block] + strip_shapes(pad),
        [ocean_state, land_mask],
        [flat],
        "state_rows",
        after=[taps],
    )
    cotan, own, to_core = call(
        prepare_near,
        [block, shape((near_rows, LANES), BF), shape((near_rows, LANES), BF)],
        [land_mask, *held[0:3], tiles],
        [flat],
        "cotan_rows",
    )
    around, _ = exchange_halo(rows, strips, outer, swap, "state", after=[to_core])
    from_far = lax.ppermute(to_far, "ch", across)
    ones = functools.partial(conv_forward, part)
    conv_operands = [masked, *around, taps]
    conv_scratch = [
        pltpu.VMEM((rows // 2 + 2 * DIL, pad, cols), BF),
        pltpu.VMEM((pad, LANES), F32),
        pltpu.VMEM((pad, LANES), F32),
        pltpu.VMEM((rows // 2, pad, cols), BF),
    ]
    eighth = shape((part_rows // 2, pad, cols), BF)
    conv_far = call(
        functools.partial(ones, 1), [eighth] * 4, conv_operands, conv_scratch, "conv_away"
    )
    from_far = call(
        relay, [from_far], [from_far], (), "cotan_relay", aliases={0: 0}, after=around[1:2]
    )[0]
    passed = lax.ppermute(from_far, "ch", core)
    conv_near = call(
        functools.partial(ones, 0),
        [eighth] * 4,
        conv_operands,
        conv_scratch,
        "conv_here",
        after=[conv_far[0], passed],
    )
    both = [(i, i ^ 3) for i in range(n_ch)]
    halves = [
        [
            conv_near[2 * h],
            lax.ppermute(conv_near[2 * h + 1], "ch", core),
            lax.ppermute(conv_far[2 * h], "ch", across),
            lax.ppermute(conv_far[2 * h + 1], "ch", both),
        ]
        for h in range(2)
    ]
    act_grad, cotan_all, weights_all, weights_turned, *picks = call(
        functools.partial(activation_gradient, part),
        [
            shape((n_ch * hid, cells), F32),
            shape((depth, cells), BF),
            shape((n_ch * hid, wide), BF),
            shape((depth, n_ch * hid), BF),
            shape((channels, depth), BF),
            shape((channels, depth), BF),
        ],
        [own, lax.ppermute(to_core, "ch", core), from_far, passed, land_mask, *held[1:3]],
        (),
        "activation_gradient",
    )
    pre_grad, sums = [], ()
    for h in range(2):
        pre, *sums = call(
            functools.partial(hidden_gradient, h),
            [
                shape((n_ch * hid, cells // 2), BF),
                shape((2, sum_rows, LANES), F32),
                shape((2, sum_rows, LANES), BF if h else F32),
            ],
            [*halves[h], act_grad, cotan_all, weights_all, *sums],
            [pltpu.VMEM((depth, cells // 2), BF), pltpu.VMEM((n_ch * hid, cells // 2), BF)],
            "hidden_first" if h == 0 else "hidden_second",
        )
        pre_grad.append(pre)
    keep, send = sums
    got = lax.ppermute(send, "ch", core)
    grad_scratch = [pltpu.VMEM((2 * pad, cells), BF)]
    grad_far = call(
        functools.partial(conv_gradient, 1),
        [shape((2, part_rows, pad, cols), BF)],
        [*pre_grad, weights_turned],
        grad_scratch,
        "gradient_away",
    )[0]
    grad_own, grad_core = call(
        functools.partial(conv_gradient, 0),
        [quarter] * 2,
        [*pre_grad, weights_turned],
        grad_scratch,
        "gradient_here",
        after=[grad_far],
    )
    grad_near = lax.ppermute(grad_core, "ch", core)
    grad_far = lax.ppermute(grad_far, "ch", across)
    staged = two_by_four()
    padded = shape((rows + 2 * DIL, pad, cols), BF)
    if not staged:
        shifted = call(shift_columns, [padded, padded], [masked, *around], (), "shift_columns")
    if staged:
        piece = sum_rows // 4
        mine, *sends = call(
            add_cores,
            [shape((2, piece, LANES), F32)] + [shape((2, piece, LANES), BF)] * 3,
            [keep, got],
            (),
            "add_cores",
        )

        shifted = call(
            shift_columns, [padded, padded], [masked, *around], (), "shift_columns", after=sends[:1]
        )

        def turn_plane(k):
            pairs = []
            for lon in range(n_lon):
                for lat in range(n_lat):
                    pairs.append((lon * n_lat + lat, (lon ^ (k & 1)) * n_lat + (lat ^ (k >> 1))))
            return pairs

        def over_plane(values):
            return [lax.ppermute(values[k - 1], ("lon", "lat"), turn_plane(k)) for k in (1, 2, 3)]

        mine, other = call(
            add_pieces,
            [shape((piece, LANES), F32), shape((piece + 112, LANES), BF)],
            [mine, *over_plane(sends)],
            (),
            "add_pieces",
            after=[grad_near, shifted[0]],
        )
    passed = call(
        second_half, [quarter], [grad_far], (), "grad_half", after=[other] if staged else []
    )[0]
    conv_grad, *grad_strips = call(
        functools.partial(collect_grad, swap),
        [block] + strip_shapes(pad) + outer_shapes(pad, swap),
        [grad_own, grad_near, grad_far, lax.ppermute(passed, "ch", core)],
        (),
        "grad_rows",
    )
    kernel_part = call(
        kernel_gradient,
        [shape((pad, LANES), BF)],
        [conv_grad, masked, around[0], *shifted],
        (),
        "kernel_gradient",
    )[0]
    grad_around, marks = exchange_halo(rows, grad_strips[:3], grad_strips[3:], swap, "grad", planes=4, riding=[kernel_part])
    if staged:
        mine = call(
            add_across,
            [shape((piece, LANES), BF)],
            [mine, lax.ppermute(other, "ch", across)],
            (),
            "add_across",
        )[0]
    state_grad, mark = call(
        conv_adjoint,
        [shape((part, rows, cols), BF), shape((8, LANES), F32)],
        [conv_grad, *grad_around, taps, cotan, land_mask],
        [
            pltpu.VMEM((17 * (rows + 8), cols), F32),
            pltpu.VMEM((part, rows, cols), BF),
            pltpu.SemaphoreType.DMA((-(-part // 16),)),
        ],
        "conv_adjoint",
        writes=1,
    )
    outs = [
        shape((hidden, channels), F32),
        shape((hidden, channels), F32),
        shape((1, hidden), F32),
        shape((3, 3, part), F32),
    ]
    if staged:
        far_lon = [(lon, lon ^ 2) for lon in range(n_lon)]
        summed = call(
            finish_pieces,
            [shape((piece + TAP_ROWS, LANES), BF)],
            [
                mine,
                lax.ppermute(mine, "lon", far_lon),
                kernel_part,
                marks[1],
            ],
            [turn],
            "finish_pieces",
            after=marks[2:],
        )[0]
        expand_grad, project_grad, bias_grad, kernel_grad = call(
            functools.partial(write_parameters, part, pad, scale, hid),
            outs,
            [summed, *over_plane([summed] * 3), *picks],
            [pltpu.VMEM((sum_rows, LANES), BF), pltpu.VMEM((4 * TAP_ROWS, LANES), F32)],
            "write_parameters",
            after=[mark],
        )
    else:
        total = keep + got.astype(F32)
        total = total[0] + lax.ppermute(total[1].astype(BF), "ch", across).astype(F32)
        total, kernel_sum = lax.psum((total, kernel_part.astype(F32)), ("lon", "lat"))
        expand_grad, project_grad, bias_grad, kernel_grad = call(
            functools.partial(unpack_whole, part, pad, scale, hid),
            outs,
            [total.astype(BF), kernel_sum, *picks],
            [turn],
            "write_parameters",
        )
    return (
        state_grad,
        expand_grad.T,
        project_grad,
        bias_grad.reshape(hidden),
        kernel_grad,
    )


def solution(mesh):
    return jax.shard_map(
        on_device,
        mesh=mesh,
        in_specs=(
            P("ch", "lat", "lon"),
            P("lat", "lon"),
            P("ch", "lat", "lon"),
            P("lat", "lon", None),
            P("lat", "lon", None),
            P(None, None, "ch"),
            P(None, "ch"),
            P("ch"),
            P("ch", None),
        ),
        out_specs=(
            P("ch", "lat", "lon"),
            P(None, "ch"),
            P("ch", None),
            P("ch"),
            P(None, None, "ch"),
        ),
        check_vma=False,
    )
```
